512 devices in a mesh: ctx: 64 (over y, z_lo, core), grp: 8 (over z_hi, x).
Axes of the slice: x: 4, y: 8, z: 8 (z_hi: 2, z_lo: 4; z = z_hi * 4 + z_lo), core: 2. Of those that a mesh axis runs over, the one named last changes fastest.
Arguments:
- queries: bfloat16 [128, 8192], P('ctx', 'grp'), may hold values from -100 to 100
- fresh_keys: bfloat16 [128, 1024], P('ctx', 'grp'), may hold values from -5 to 5
- fresh_values: bfloat16 [128, 1024], P('ctx', 'grp'), may hold values from -5 to 5
- key_cache: bfloat16 [1536, 128, 1024], P('ctx', None, 'grp'), may hold values from -5 to 5
- value_cache: bfloat16 [1536, 128, 1024], P('ctx', None, 'grp'), may hold values from -5 to 5
- lengths: int32 [128], replicated, may hold values from 1 to 16384, as said below
- block_table: int32 [128, 128], replicated, may hold values from 0 to 1535, as said below
- resid: bfloat16 [128, 8192], P(None, 'ctx'), may hold values from -0.1796875 to 0.1796875
- out_weight: bfloat16 [8192, 8192], P('grp', 'ctx'), may hold values from -0.0625 to 0.0625
- norm_gain: bfloat16 [8192], P('ctx'), may hold values from 0.099609375 to 1.8984375
- gate_weight: bfloat16 [8192, 28672], P('ctx', 'grp'), may hold values from -0.0625 to 0.0625
- up_weight: bfloat16 [8192, 28672], P('ctx', 'grp'), may hold values from -0.0625 to 0.0625
- down_weight: bfloat16 [28672, 8192], P('grp', 'ctx'), may hold values from -0.03125 to 0.03125
- row_order: int32 [128], replicated, may hold values from 0 to 127, each once
Outputs:
- mixed: bfloat16 [128, 8192], P('grp', 'ctx')
The draws below stay inside these ranges and needn't reach their ends.
Inputs may be any that keep to these rules, and one draw needn't show every extreme that they name: Page j of request r lies in slot block_table[r, j], which is row block_table[r, j] % 24 of the cache on ctx index block_table[r, j] // 24. The live pages j < ceil(lengths[r] / 128) of all requests together name every slot exactly once; entries at or beyond a request's last live page repeat that page's slot. At most 16384 tokens a request, reached by one request in every draw; the live pages of all requests, ceil(lengths[r] / 128) each, add up to 1536.
All inputs are finite; a program needn't handle non-finite values.
Results may differ from the reference program's by a relative error of at most 0.025.
Values may be sent and summed in bfloat16 or wider, within the bound.
No kernel may reach another device: no remote copies, remote signals or barrier semaphores. Data moves between devices by JAX's collectives and lax.ppermute only.
A program may use at most 128 MiB of HBM per device.

```python
import jax
import jax.numpy as jnp
from jax import lax

D = 8192
FF = 28672
H = 64
KVH = 8
HD = 128
PAGE = 128
MAXP = 128
REQUESTS = 128
SLOTS = 1536


def page_plan(key):
    plan_key = jax.random.fold_in(key, 700)
    longest = jax.random.randint(jax.random.fold_in(plan_key, 1), (), 0, REQUESTS)
    is_long = jnp.arange(REQUESTS, dtype=jnp.int32) == longest
    weights = jax.random.randint(jax.random.fold_in(plan_key, 2), (REQUESTS,), 1, 5)
    weights = jnp.where(is_long, 0, weights).astype(jnp.int32)
    extra_total = SLOTS - MAXP - (REQUESTS - 1)
    running = jnp.cumsum(weights)
    weight_sum = running[REQUESTS - 1]
    upper = extra_total * running // weight_sum
    lower = extra_total * (running - weights) // weight_sum
    pages = jnp.where(is_long, MAXP, 1 + upper - lower)
    return (pages.astype(jnp.int32), is_long)


def shared_table(key):
    pages, is_long = page_plan(key)
    order = jax.random.permutation(jax.random.fold_in(key, 701), SLOTS).astype(jnp.int32)
    offsets = jnp.cumsum(pages) - pages
    page_ids = jnp.arange(MAXP, dtype=jnp.int32)
    index = offsets[:, None] + jnp.minimum(page_ids[None, :], pages[:, None] - 1)
    return order[index].astype(jnp.int32)


def shared_keys(key):
    base = jax.random.normal(jax.random.fold_in(key, 702), (SLOTS, PAGE, KVH * HD), jnp.float32)
    return jnp.clip(base, -5.0, 5.0)


def draw_block_table(key, part):
    table = shared_table(key)
    return table


def draw_key_cache(key, part):
    cache = shared_keys(key)
    return cache.astype(jnp.bfloat16)


def draw_queries(key, part):
    key = jax.random.fold_in(key, 13)
    result = jnp.clip(jax.random.normal(jax.random.fold_in(key, 1), (REQUESTS, H * HD), jnp.float32), -5.0, 5.0)
    return result.astype(jnp.bfloat16)


def draw_lengths(key, part):
    pages, is_long = page_plan(key)
    key = jax.random.fold_in(key, 14)
    tail_tokens = jax.random.randint(jax.random.fold_in(key, 2), (REQUESTS,), 1, PAGE + 1)
    counts = (pages - 1) * PAGE + tail_tokens
    return jnp.where(is_long, MAXP * PAGE, counts).astype(jnp.int32)


def level_of(rng, shape, cuts, least, largest):
    def one(position, shards_of):
        steps = jax.random.uniform(jax.random.fold_in(jax.random.fold_in(rng, 6), position), (shards_of,), jnp.float32, least / len(cuts), largest / len(cuts))
        return jnp.repeat(jnp.exp(steps), shape[position] // shards_of).reshape((-1,) + (1,) * (len(shape) - position - 1))

    factor_of = one(*cuts[0])
    for cut in cuts[1:]:
        factor_of = factor_of * one(*cut)
    return factor_of


def normal_values(key, extent, deviation, most, pieces=(), kind=jnp.bfloat16):
    values = deviation * jax.random.normal(key, extent, jnp.float32)
    if pieces:
        values = values * level_of(key, extent, pieces, -0.22, 0.18)
    return jnp.clip(values, -most, most).astype(kind)


def setup_inputs(seed: int = 0) -> dict:
    splits = jax.random.split(jax.random.key(seed), 15)
    queries = draw_queries(jax.random.fold_in(splits[14], 71), 0)
    fresh_keys = normal_values(splits[1], (REQUESTS, KVH * HD), 1.0, 5.0, ((0, 64), (1, 8)))
    fresh_values = normal_values(splits[2], (REQUESTS, KVH * HD), 1.0, 5.0, ((0, 64), (1, 8)))
    key_cache = draw_key_cache(jax.random.fold_in(splits[14], 71), 0)
    value_cache = normal_values(splits[4], (SLOTS, PAGE, KVH * HD), 1.0, 5.0, ((0, 64), (2, 8)))
    lengths = draw_lengths(jax.random.fold_in(splits[14], 71), 0)
    block_table = draw_block_table(jax.random.fold_in(splits[14], 71), 0)
    resid = normal_values(splits[7], (REQUESTS, D), 0.03, 0.1796875, ((1, 64),))
    out_weight = normal_values(splits[8], (H * HD, D), (H * HD) ** -0.5, 0.0625, ((0, 8), (1, 64)))
    norm_gain = jnp.clip(1.0 + 0.18 * jax.random.normal(splits[9], (D,), jnp.float32), 0.099609375, 1.8984375).astype(jnp.bfloat16)
    gate_weight = normal_values(splits[10], (D, FF), D ** -0.5, 0.0625, ((0, 64), (1, 8)))
    up_weight = normal_values(splits[11], (D, FF), D ** -0.5, 0.0625, ((0, 64), (1, 8)))
    down_weight = normal_values(splits[12], (FF, D), FF ** -0.5, 0.03125, ((0, 8), (1, 64)))
    row_order = jax.random.permutation(splits[13], REQUESTS).astype(jnp.int32)
    return dict(queries=queries, fresh_keys=fresh_keys, fresh_values=fresh_values, key_cache=key_cache, value_cache=value_cache, lengths=lengths, block_table=block_table, resid=resid, out_weight=out_weight, norm_gain=norm_gain, gate_weight=gate_weight, up_weight=up_weight, down_weight=down_weight, row_order=row_order)


def attend_one(query_row, fresh_key, fresh_value, length, pages, key_cache, value_cache):
    group_size = H // KVH
    inv_root = HD ** (-0.5)
    key_rows = key_cache[pages].reshape(MAXP * PAGE, KVH, HD).astype(jnp.float32)
    value_rows = value_cache[pages].reshape(MAXP * PAGE, KVH, HD).astype(jnp.float32)
    query_heads = query_row.reshape(KVH, group_size, HD).astype(jnp.float32)
    scores = jnp.einsum('kgd,tkd->kgt', query_heads, key_rows) * inv_root
    own_score = jnp.einsum('kgd,kd->kg', query_heads, fresh_key.reshape(KVH, HD).astype(jnp.float32)) * inv_root
    positions = jnp.arange(MAXP * PAGE, dtype=jnp.int32)
    scores = jnp.where(positions[None, None, :] < length, scores, -jnp.inf)
    best = jnp.maximum(lax.optimization_barrier(jnp.max(scores, axis=2)), own_score)
    weights = jnp.exp(scores - best[:, :, None])
    own_weight = jnp.exp(own_score - best)
    weight_total = lax.optimization_barrier(jnp.sum(weights, axis=2)) + own_weight
    rounded = lax.optimization_barrier(weights.astype(jnp.bfloat16)).astype(jnp.float32)
    own_rounded = lax.optimization_barrier(own_weight.astype(jnp.bfloat16)).astype(jnp.float32)
    weighted = jnp.einsum('kgt,tkd->kgd', rounded, value_rows)
    weighted = weighted + own_rounded[:, :, None] * fresh_value.reshape(KVH, 1, HD).astype(jnp.float32)
    return (weighted / weight_total[:, :, None]).reshape(H * HD).astype(jnp.bfloat16)

def reference(queries, fresh_keys, fresh_values, key_cache, value_cache, lengths, block_table, resid, out_weight, norm_gain, gate_weight, up_weight, down_weight, row_order):

    def one_request(items):
        return attend_one(items[0], items[1], items[2], items[3], items[4], key_cache, value_cache)
    attended = lax.map(one_request, (queries, fresh_keys, fresh_values, lengths, block_table))
    projected = jnp.dot(attended, out_weight, preferred_element_type=jnp.float32)
    hidden = (resid.astype(jnp.float32) + projected).astype(jnp.bfloat16)
    hidden_wide = hidden.astype(jnp.float32)
    inv_rms = lax.rsqrt(lax.optimization_barrier(jnp.mean(hidden_wide * hidden_wide, axis=1)) + 1e-05)[:, None]
    gained = (hidden_wide * norm_gain.astype(jnp.float32)[None, :]).astype(jnp.bfloat16)
    gate_sum = jnp.dot(gained, gate_weight, preferred_element_type=jnp.float32) * inv_rms
    up_sum = jnp.dot(gained, up_weight, preferred_element_type=jnp.float32) * inv_rms
    activated = (jax.nn.silu(gate_sum) * up_sum).astype(jnp.bfloat16)
    down_sum = jnp.dot(activated, down_weight, preferred_element_type=jnp.float32)
    result = hidden_wide + down_sum
    return result[row_order].astype(jnp.bfloat16)
```

```python
import jax
import jax.numpy as jnp
from jax import lax
from jax.experimental import pallas as pl
from jax.experimental.pallas import tpu as pltpu
from jax.sharding import Mesh
from jax.sharding import PartitionSpec as P

HD = 128
GROUP = 8
LANES = 128
EPS = 1e-05
NEG = -1e30
CTX = ("y", "zl", "core")
RING = ("y", "zl")
GRP = ("zh", "x")
F32 = jnp.float32
BF16 = jnp.bfloat16
VMEM = pl.BlockSpec(memory_space=pltpu.VMEM)
SMEM = pl.BlockSpec(memory_space=pltpu.SMEM)


def exchange(x, axes):
    return lax.all_to_all(x, axes, 0, 0, tiled=True)


def lane_ids(shape):
    return lax.broadcasted_iota(jnp.int32, shape, len(shape) - 1)


def call(body, out_shape, in_specs, scratch=()):
    return pl.pallas_call(
        body,
        out_shape=out_shape,
        in_specs=in_specs,
        out_specs=jax.tree.map(lambda _: VMEM, out_shape),
        scratch_shapes=list(scratch),
    )


def attend_body(len_ref, table_ref, q_ref, k_ref, v_ref, out_ref, top_ref, sum_ref, acc_ref):
    slots, page = k_ref.shape[0], k_ref.shape[1]
    first = lax.axis_index(CTX) * slots
    table = table_ref[...] - first
    rows, cols = table.shape
    code = lax.broadcasted_iota(jnp.int32, (rows, cols), 0) * cols + lane_ids((rows, cols))
    top_ref[...] = jnp.full(top_ref.shape, NEG, F32)
    sum_ref[...] = jnp.zeros(sum_ref.shape, F32)
    acc_ref[...] = jnp.zeros(acc_ref.shape, F32)
    lane = lane_ids((GROUP, page))
    owners, scores = [], []
    for s in range(slots):
        found = jnp.min(jnp.where(table == s, code, rows * cols - 1))
        owner, page_no = found // cols, found % cols
        live = len_ref[owner] - page_no * page
        pair = q_ref[owner // 2].astype(F32)
        q = jnp.where(owner % 2 == 1, pair[GROUP:], pair[:GROUP]).astype(BF16)
        score = lax.dot_general(q, k_ref[s], (((1,), (1,)), ((), ())), preferred_element_type=F32)
        score = jnp.where(lane < live, score * HD ** (-0.5), NEG)
        best = jnp.max(score, axis=1, keepdims=True)
        top_ref[owner] = jnp.maximum(top_ref[owner], jnp.broadcast_to(best, (GROUP, LANES)))
        owners.append(owner)
        scores.append(score)
    for s in range(slots):
        owner = owners[s]
        shift = top_ref[owner].astype(BF16).astype(F32)
        weight = jnp.exp(scores[s] - shift)
        total = jnp.sum(weight, axis=1, keepdims=True)
        sum_ref[owner] = sum_ref[owner] + jnp.broadcast_to(total, (GROUP, LANES))
        acc_ref[owner] = acc_ref[owner] + jnp.dot(
            weight.astype(BF16), v_ref[s], preferred_element_type=F32
        )
    lane = lane_ids((GROUP, LANES))
    for d in range(out_ref.shape[0]):
        stats = jnp.zeros((GROUP, LANES), F32)
        for par in range(2):
            total = sum_ref[2 * d + par]
            high = total.astype(BF16).astype(F32)
            base = par * 64
            stats = jnp.where(lane == base, top_ref[2 * d + par], stats)
            stats = jnp.where(lane == base + 1, high, stats)
            stats = jnp.where(lane == base + 2, total - high, stats)
        block = jnp.concatenate([acc_ref[2 * d], acc_ref[2 * d + 1], stats], axis=0)
        out_ref[d] = block.astype(BF16)


def combine_body(part_ref, q_ref, fk_ref, fv_ref, out_ref):
    count = part_ref.shape[0]
    fk, fv = fk_ref[...].astype(F32), fv_ref[...].astype(F32)
    q = q_ref[...].astype(F32)
    done = []
    for par in range(2):
        base = par * 64
        mine = slice(par * GROUP, (par + 1) * GROUP)
        own = jnp.sum(q[mine] * fk[par : par + 1], axis=1, keepdims=True) * HD ** (-0.5)
        best = own
        for d in range(count):
            stats = part_ref[d].astype(F32)[2 * GROUP :]
            best = jnp.maximum(best, stats[:, base : base + 1])
        own_weight = jnp.exp(own - best)
        total = own_weight
        acc = own_weight.astype(BF16).astype(F32) * fv[par : par + 1]
        for d in range(count):
            block = part_ref[d].astype(F32)
            stats = block[2 * GROUP :]
            factor = jnp.exp(stats[:, base : base + 1] - best)
            total = total + factor * (stats[:, base + 1 : base + 2] + stats[:, base + 2 : base + 3])
            acc = acc + factor * block[mine]
        done.append(acc / total)
    rows = jnp.concatenate(done, axis=0).astype(BF16)
    for d in range(count):
        out_ref[d] = rows


def project_body(att_ref, w_ref, out_ref, rows_ref):
    count, per, _ = att_ref.shape
    rows_ref[...] = att_ref[...].astype(F32).reshape(count * per, HD)
    reqs = count * per // GROUP
    total = jnp.zeros((reqs, w_ref.shape[1]), F32)
    for h in range(GROUP):
        head = rows_ref[pl.ds(h, reqs, stride=GROUP), :].astype(BF16)
        total = total + jnp.dot(head, w_ref[h * HD : (h + 1) * HD, :], preferred_element_type=F32)
    total = total.astype(BF16)
    for g in range(out_ref.shape[0]):
        out_ref[g] = total


def hidden_body(part_ref, resid_ref, gain_ref, hidden_ref, pay_ref):
    total = resid_ref[...].astype(F32)
    projected = part_ref[0].astype(F32)
    for g in range(1, part_ref.shape[0]):
        projected = projected + part_ref[g].astype(F32)
    hidden = (total + projected).astype(BF16)
    hidden_ref[...] = hidden
    wide = hidden.astype(F32)
    pay_ref[0] = (wide * gain_ref[...].astype(F32)).astype(BF16)
    square = jnp.sum(wide * wide, axis=1, keepdims=True)
    high = square.astype(BF16).astype(F32)
    lane = lane_ids(wide.shape)
    pay_ref[1] = jnp.where(lane == 0, high, jnp.where(lane == 1, square - high, 0.0)).astype(BF16)


def low_half(shape):
    return lax.broadcasted_iota(jnp.int32, shape, 0) % 8 < 4


def split_fours(first, second, low):
    rows = first.shape[0]
    even = jnp.where(low, first, pltpu.roll(second, 4, 0))
    odd = jnp.where(low, pltpu.roll(first, rows - 4, 0), second)
    return even.reshape(rows // 8, 8, LANES), odd.reshape(rows // 8, 8, LANES)


def join_fours(even, odd, low):
    rows = even.shape[0] * 8
    even, odd = even.reshape(rows, LANES), odd.reshape(rows, LANES)
    first = jnp.where(low, even, pltpu.roll(odd, 4, 0))
    second = jnp.where(low, pltpu.roll(even, rows - 4, 0), odd)
    return first, second


def widen_body(pay_ref, gate_ref, up_ref, met_ref, out_ref):
    core = lax.axis_index("core")
    mine, other = pay_ref[core, 0], pay_ref[1 - core, 0]
    square = pay_ref[0, 1].astype(F32) + pay_ref[1, 1].astype(F32)
    high = square.astype(BF16).astype(F32)
    rows = mine.shape[0]
    low = low_half((rows, LANES))
    half = met_ref.shape[2]
    pairs = half // (2 * LANES)

    def pair_tiles(p):
        ref, which, at = (gate_ref, 0, p) if p < pairs else (up_ref, 1, p - pairs)
        start = pl.multiple_of(core * half + at * 2 * LANES, LANES)
        x = jnp.dot(mine, ref[:, pl.ds(start, 2 * LANES)], preferred_element_type=F32)
        x = x + jnp.dot(
            other, met_ref[which, :, at * 2 * LANES : (at + 1) * 2 * LANES], preferred_element_type=F32
        )
        return split_fours(x[:, :LANES], x[:, LANES:], low)

    for g in range(pairs):
        even0, odd0 = pair_tiles(2 * g)
        even1, odd1 = pair_tiles(2 * g + 1)
        out_ref[:, 0, g * 16 : (g + 1) * 16, :] = jnp.concatenate([even0, even1], axis=1).astype(BF16)
        out_ref[:, 1, g * 16 : (g + 1) * 16, :] = jnp.concatenate([odd0, odd1], axis=1).astype(BF16)
    lane = lane_ids((rows, LANES))
    total = square + pltpu.roll(square, LANES - 1, 1)
    high = total.astype(BF16).astype(F32)
    rest = pltpu.roll(total - high, 1, 1)
    square = jnp.where(lane == 0, high, jnp.where(lane == 1, rest, 0.0))
    zero = jnp.zeros((rows, LANES), F32)
    even, odd = split_fours(square, zero, low)
    blank = zero.reshape(rows // 8, 8, LANES)
    g = pairs
    out_ref[:, 0, g * 16 : (g + 1) * 16, :] = jnp.concatenate([even, blank], axis=1).astype(BF16)
    out_ref[:, 1, g * 16 : (g + 1) * 16, :] = jnp.concatenate([odd, blank], axis=1).astype(BF16)


def activate_body(width, part_ref, out_ref):
    total = part_ref[0].astype(F32)
    for d in range(1, part_ref.shape[0]):
        total = total + part_ref[d].astype(F32)
    units = (total.shape[0] - 16) // 2
    square = total[2 * units : 2 * units + 8]
    square = square[:, 0:1] + square[:, 1:2]
    square = jnp.broadcast_to(square, (8, LANES))
    square = square + pltpu.roll(square, 4, 0)
    inv_rms = lax.rsqrt(square / width + EPS)[None]
    gate = total[:units].reshape(units // 8, 8, LANES) * inv_rms
    up = total[units : 2 * units].reshape(units // 8, 8, LANES) * inv_rms
    active = (gate / (1.0 + jnp.exp(-gate)) * up).reshape(units, LANES)
    pad = jnp.zeros((out_ref.shape[1] - units, LANES), F32)
    active = jnp.concatenate([active, pad], axis=0).astype(BF16)
    for d in range(out_ref.shape[0]):
        out_ref[d] = active


def down_body(act_ref, w_ref, order_ref, hidden_ref, out_ref, kept_ref):
    halves, dests = act_ref.shape[0], act_ref.shape[1]
    rows = dests * 8
    low = low_half((rows, LANES))
    half = w_ref.shape[0] // halves
    pairs = half // (2 * LANES)
    total = jnp.zeros((rows, LANES), F32)
    for c in range(halves):
        for g in range((pairs + 1) // 2):
            even = act_ref[c, :, 0, g * 16 : (g + 1) * 16, :].astype(F32)
            odd = act_ref[c, :, 1, g * 16 : (g + 1) * 16, :].astype(F32)
            for k in range(2):
                p = 2 * g + k
                if p >= pairs:
                    continue
                first, second = join_fours(even[:, k * 8 : k * 8 + 8], odd[:, k * 8 : k * 8 + 8], low)
                block = jnp.concatenate([first, second], axis=1).astype(BF16)
                start = c * half + p * 2 * LANES
                total = total + jnp.dot(
                    block, w_ref[start : start + 2 * LANES, :], preferred_element_type=F32
                )
    reqs = order_ref.shape[1]
    pick = lax.broadcasted_iota(jnp.int32, (reqs, reqs), 0) == order_ref[...]
    pick = pick.astype(F32).astype(BF16)
    first_dim = (((0,), (0,)), ((), ()))
    out = lax.dot_general(pick, total.astype(BF16), first_dim, preferred_element_type=F32)
    out_ref[...] = out.astype(BF16)
    kept = lax.dot_general(pick, hidden_ref[...], first_dim, preferred_element_type=F32)
    kept_ref[...] = kept.astype(BF16)


def shards(
    queries,
    fresh_keys,
    fresh_values,
    key_cache,
    value_cache,
    lengths,
    block_table,
    resid,
    out_weight,
    norm_gain,
    gate_weight,
    up_weight,
    down_weight,
    row_order,
):
    ctx, ring, grp = lax.axis_size(CTX), lax.axis_size(RING), lax.axis_size(GRP)
    core = lax.axis_index("core")
    reqs, width = resid.shape
    shape = jax.ShapeDtypeStruct

    half = gate_weight.shape[1] // 2
    given = jnp.stack(
        [lax.dynamic_slice_in_dim(w, (1 - core) * half, half, 1) for w in (gate_weight, up_weight)]
    )
    met = lax.ppermute(given, "core", [(0, 1), (1, 0)])

    my_queries = queries.reshape(2 * GROUP, HD)
    all_queries = exchange(jnp.broadcast_to(my_queries[None], (ctx, 2 * GROUP, HD)), CTX)
    scratch = [pltpu.VMEM((reqs, GROUP, LANES), F32)] * 3
    parts = call(attend_body, shape((ctx, 3 * GROUP, HD), BF16), [SMEM] + [VMEM] * 4, scratch)(
        lengths, block_table, all_queries, key_cache, value_cache
    )
    parts = exchange(parts, CTX)
    local = call(combine_body, shape((ctx, 2 * GROUP, HD), BF16), [VMEM] * 4)(
        parts, my_queries, fresh_keys, fresh_values
    )
    attended = exchange(local, CTX)
    projected = call(
        project_body,
        shape((grp, reqs, width), BF16),
        [VMEM] * 2,
        [pltpu.VMEM((reqs * GROUP, HD), F32)],
    )(attended, out_weight)
    projected = exchange(projected, GRP)
    hidden, pay = call(
        hidden_body,
        (shape((reqs, width), BF16), shape((2, reqs, width), BF16)),
        [VMEM] * 3,
    )(projected, resid, norm_gain.reshape(1, width))
    pay = lax.all_gather(pay, "core", axis=0, tiled=False)
    blocks = 2 * half // LANES
    wide = call(widen_body, shape((ring // 2, 2, blocks * 4 + 16, LANES), BF16), [VMEM] * 4)(
        pay, gate_weight, up_weight, met
    )
    wide = exchange(wide.reshape(ring, blocks * 4 + 16, LANES), RING)
    units = blocks * 2
    padded = -(-units // 16) * 16
    model_width = width * ctx

    def activate(part_ref, out_ref):
        activate_body(model_width, part_ref, out_ref)

    active = call(activate, shape((ring, padded, LANES), BF16), [VMEM])(wide)
    active = exchange(active, RING)
    active = lax.all_gather(active, "core", axis=0, tiled=False)
    rows, kept = call(
        down_body,
        (shape((reqs, width), BF16), shape((reqs, width), BF16)),
        [VMEM] * 4,
    )(
        active.reshape(2, ring // 2, 2, padded, LANES),
        down_weight,
        row_order.reshape(1, reqs),
        hidden,
    )
    share = reqs // grp
    rows = exchange(rows.reshape(grp, share, width), GRP)
    kept = lax.dynamic_index_in_dim(kept.reshape(grp, share, width), lax.axis_index(GRP), 0, False)
    return (kept.astype(F32) + jnp.sum(rows.astype(F32), axis=0)).astype(BF16)


def solution(mesh, sizes=(8, 4, 2, 2, 4)):
    inner = Mesh(mesh.devices.reshape(sizes), ("y", "zl", "core", "zh", "x"))
    in_specs = (
        P(CTX, GRP),
        P(CTX, GRP),
        P(CTX, GRP),
        P(CTX, None, GRP),
        P(CTX, None, GRP),
        P(),
        P(),
        P(None, CTX),
        P(GRP, CTX),
        P(CTX),
        P(CTX, GRP),
        P(CTX, GRP),
        P(GRP, CTX),
        P(),
    )
    out_specs = P(GRP, CTX)
    return jax.shard_map(shards, mesh=inner, in_specs=in_specs, out_specs=out_specs, check_vma=False)
```

```python
import jax
import jax.numpy as jnp
from jax import lax
from jax.experimental import pallas as pl
from jax.experimental.pallas import tpu as pltpu
from jax.sharding import Mesh
from jax.sharding import PartitionSpec as P

HD = 128
GROUP = 8
LANES = 128
EPS = 1e-05
NEG = -1e30
CTX = ("y", "zl", "core")
RING = ("y", "zl")
GRP = ("zh", "x")
F32 = jnp.float32
BF16 = jnp.bfloat16
VMEM = pl.BlockSpec(memory_space=pltpu.VMEM)
SMEM = pl.BlockSpec(memory_space=pltpu.SMEM)


def exchange(x, axes):
    return lax.all_to_all(x, axes, 0, 0, tiled=True)


def lane_ids(shape):
    return lax.broadcasted_iota(jnp.int32, shape, len(shape) - 1)


def call(body, out_shape, in_specs, scratch=()):
    return pl.pallas_call(
        body,
        out_shape=out_shape,
        in_specs=in_specs,
        out_specs=jax.tree.map(lambda _: VMEM, out_shape),
        scratch_shapes=list(scratch),
    )


def attend_body(len_ref, table_ref, q_ref, k_ref, v_ref, out_ref, top_ref, sum_ref, acc_ref):
    slots, page = k_ref.shape[0], k_ref.shape[1]
    first = lax.axis_index(CTX) * slots
    table = table_ref[...] - first
    rows, cols = table.shape
    code = lax.broadcasted_iota(jnp.int32, (rows, cols), 0) * cols + lane_ids((rows, cols))
    top_ref[...] = jnp.full(top_ref.shape, NEG, F32)
    sum_ref[...] = jnp.zeros(sum_ref.shape, F32)
    acc_ref[...] = jnp.zeros(acc_ref.shape, F32)
    lane = lane_ids((GROUP, page))
    owners, scores = [], []
    for s in range(slots):
        found = jnp.min(jnp.where(table == s, code, rows * cols - 1))
        owner, page_no = found // cols, found % cols
        live = len_ref[owner] - page_no * page
        pair = q_ref[owner // 2].astype(F32)
        q = jnp.where(owner % 2 == 1, pair[GROUP:], pair[:GROUP]).astype(BF16)
        score = lax.dot_general(q, k_ref[s], (((1,), (1,)), ((), ())), preferred_element_type=F32)
        score = jnp.where(lane < live, score * HD ** (-0.5), NEG)
        best = jnp.max(score, axis=1, keepdims=True)
        top_ref[owner] = jnp.maximum(top_ref[owner], jnp.broadcast_to(best, (GROUP, LANES)))
        owners.append(owner)
        scores.append(score)
    for s in range(slots):
        owner = owners[s]
        shift = top_ref[owner].astype(BF16).astype(F32)
        weight = jnp.exp(scores[s] - shift)
        total = jnp.sum(weight, axis=1, keepdims=True)
        sum_ref[owner] = sum_ref[owner] + jnp.broadcast_to(total, (GROUP, LANES))
        acc_ref[owner] = acc_ref[owner] + jnp.dot(
            weight.astype(BF16), v_ref[s], preferred_element_type=F32
        )
    lane = lane_ids((GROUP, LANES))
    for d in range(out_ref.shape[0]):
        stats = jnp.zeros((GROUP, LANES), F32)
        for par in range(2):
            total = sum_ref[2 * d + par]
            high = total.astype(BF16).astype(F32)
            base = par * 64
            stats = jnp.where(lane == base, top_ref[2 * d + par], stats)
            stats = jnp.where(lane == base + 1, high, stats)
            stats = jnp.where(lane == base + 2, total - high, stats)
        block = jnp.concatenate([acc_ref[2 * d], acc_ref[2 * d + 1], stats], axis=0)
        out_ref[d] = block.astype(BF16)


def combine_body(part_ref, q_ref, fk_ref, fv_ref, out_ref):
    count = part_ref.shape[0]
    fk, fv = fk_ref[...].astype(F32), fv_ref[...].astype(F32)
    q = q_ref[...].astype(F32)
    done = []
    for par in range(2):
        base = par * 64
        mine = slice(par * GROUP, (par + 1) * GROUP)
        own = jnp.sum(q[mine] * fk[par : par + 1], axis=1, keepdims=True) * HD ** (-0.5)
        best = own
        for d in range(count):
            stats = part_ref[d].astype(F32)[2 * GROUP :]
            best = jnp.maximum(best, stats[:, base : base + 1])
        own_weight = jnp.exp(own - best)
        total = own_weight
        acc = own_weight.astype(BF16).astype(F32) * fv[par : par + 1]
        for d in range(count):
            block = part_ref[d].astype(F32)
            stats = block[2 * GROUP :]
            factor = jnp.exp(stats[:, base : base + 1] - best)
            total = total + factor * (stats[:, base + 1 : base + 2] + stats[:, base + 2 : base + 3])
            acc = acc + factor * block[mine]
        done.append(acc / total)
    rows = jnp.concatenate(done, axis=0).astype(BF16)
    for d in range(count):
        out_ref[d] = rows


def project_body(att_ref, w_ref, out_ref, rows_ref):
    count, per, _ = att_ref.shape
    rows_ref[...] = att_ref[...].astype(F32).reshape(count * per, HD)
    reqs = count * per // GROUP
    total = jnp.zeros((reqs, w_ref.shape[1]), F32)
    for h in range(GROUP):
        head = rows_ref[pl.ds(h, reqs, stride=GROUP), :].astype(BF16)
        total = total + jnp.dot(head, w_ref[h * HD : (h + 1) * HD, :], preferred_element_type=F32)
    total = total.astype(BF16)
    for g in range(out_ref.shape[0]):
        out_ref[g] = total


def hidden_body(part_ref, resid_ref, gain_ref, hidden_ref, pay_ref):
    total = resid_ref[...].astype(F32)
    projected = part_ref[0].astype(F32)
    for g in range(1, part_ref.shape[0]):
        projected = projected + part_ref[g].astype(F32)
    hidden = (total + projected).astype(BF16)
    hidden_ref[...] = hidden
    wide = hidden.astype(F32)
    pay_ref[0] = (wide * gain_ref[...].astype(F32)).astype(BF16)
    square = jnp.sum(wide * wide, axis=1, keepdims=True)
    high = square.astype(BF16).astype(F32)
    lane = lane_ids(wide.shape)
    pay_ref[1] = jnp.where(lane == 0, high, jnp.where(lane == 1, square - high, 0.0)).astype(BF16)


def low_half(shape):
    return lax.broadcasted_iota(jnp.int32, shape, 0) % 8 < 4


def split_fours(first, second, low):
    rows = first.shape[0]
    even = jnp.where(low, first, pltpu.roll(second, 4, 0))
    odd = jnp.where(low, pltpu.roll(first, rows - 4, 0), second)
    return even.reshape(rows // 8, 8, LANES), odd.reshape(rows // 8, 8, LANES)


def join_fours(even, odd, low):
    rows = even.shape[0] * 8
    even, odd = even.reshape(rows, LANES), odd.reshape(rows, LANES)
    first = jnp.where(low, even, pltpu.roll(odd, 4, 0))
    second = jnp.where(low, pltpu.roll(even, rows - 4, 0), odd)
    return first, second


def widen_body(pay_ref, gate_ref, up_ref, met_ref, out_ref):
    core = lax.axis_index("core")
    mine, other = pay_ref[core, 0], pay_ref[1 - core, 0]
    square = pay_ref[0, 1].astype(F32) + pay_ref[1, 1].astype(F32)
    high = square.astype(BF16).astype(F32)
    rows = mine.shape[0]
    low = low_half((rows, LANES))
    half = met_ref.shape[2]
    pairs = half // (2 * LANES)

    def pair_tiles(p):
        ref, which, at = (gate_ref, 0, p) if p < pairs else (up_ref, 1, p - pairs)
        start = pl.multiple_of(core * half + at * 2 * LANES, LANES)
        x = jnp.dot(mine, ref[:, pl.ds(start, 2 * LANES)], preferred_element_type=F32)
        x = x + jnp.dot(
            other, met_ref[which, :, at * 2 * LANES : (at + 1) * 2 * LANES], preferred_element_type=F32
        )
        return split_fours(x[:, :LANES], x[:, LANES:], low)

    for g in range(pairs):
        even0, odd0 = pair_tiles(2 * g)
        even1, odd1 = pair_tiles(2 * g + 1)
        out_ref[:, 0, g * 16 : (g + 1) * 16, :] = jnp.concatenate([even0, even1], axis=1).astype(BF16)
        out_ref[:, 1, g * 16 : (g + 1) * 16, :] = jnp.concatenate([odd0, odd1], axis=1).astype(BF16)
    lane = lane_ids((rows, LANES))
    total = square + pltpu.roll(square, LANES - 1, 1)
    high = total.astype(BF16).astype(F32)
    rest = pltpu.roll(total - high, 1, 1)
    square = jnp.where(lane == 0, high, jnp.where(lane == 1, rest, 0.0))
    zero = jnp.zeros((rows, LANES), F32)
    even, odd = split_fours(square, zero, low)
    out_ref[:, 0, pairs * 16 :, :] = even.astype(BF16)
    out_ref[:, 1, pairs * 16 :, :] = odd.astype(BF16)


def activate_body(width, part_ref, out_ref):
    total = part_ref[0].astype(F32)
    for d in range(1, part_ref.shape[0]):
        total = total + part_ref[d].astype(F32)
    units = (total.shape[0] - 8) // 2
    square = total[2 * units : 2 * units + 8]
    square = square[:, 0:1] + square[:, 1:2]
    square = jnp.broadcast_to(square, (8, LANES))
    square = square + pltpu.roll(square, 4, 0)
    inv_rms = lax.rsqrt(square / width + EPS)[None]
    gate = total[:units].reshape(units // 8, 8, LANES) * inv_rms
    up = total[units : 2 * units].reshape(units // 8, 8, LANES) * inv_rms
    active = (gate / (1.0 + jnp.exp(-gate)) * up).reshape(units, LANES)
    pad = jnp.zeros((out_ref.shape[1] - units, LANES), F32)
    active = jnp.concatenate([active, pad], axis=0).astype(BF16)
    for d in range(out_ref.shape[0]):
        out_ref[d] = active


def down_body(mine_ref, met_ref, w_ref, order_ref, hidden_ref, out_ref, kept_ref):
    core = lax.axis_index("core")
    rows = mine_ref.shape[0] * 8
    low = low_half((rows, LANES))
    half = w_ref.shape[0] // 2
    pairs = half // (2 * LANES)
    total = jnp.zeros((rows, LANES), F32)
    for act_ref, c in ((mine_ref, core), (met_ref, 1 - core)):
        for g in range((pairs + 1) // 2):
            even = act_ref[:, 0, g * 16 : (g + 1) * 16, :].astype(F32)
            odd = act_ref[:, 1, g * 16 : (g + 1) * 16, :].astype(F32)
            for k in range(2):
                p = 2 * g + k
                if p >= pairs:
                    continue
                first, second = join_fours(even[:, k * 8 : k * 8 + 8], odd[:, k * 8 : k * 8 + 8], low)
                block = jnp.concatenate([first, second], axis=1).astype(BF16)
                start = pl.multiple_of(c * half + p * 2 * LANES, LANES)
                total = total + jnp.dot(
                    block, w_ref[pl.ds(start, 2 * LANES), :], preferred_element_type=F32
                )
    reqs = order_ref.shape[1]
    pick = lax.broadcasted_iota(jnp.int32, (reqs, reqs), 0) == order_ref[...]
    pick = pick.astype(F32).astype(BF16)
    first_dim = (((0,), (0,)), ((), ()))
    out = lax.dot_general(pick, total.astype(BF16), first_dim, preferred_element_type=F32)
    out_ref[...] = out.astype(BF16)
    kept = lax.dot_general(pick, hidden_ref[...], first_dim, preferred_element_type=F32)
    kept_ref[...] = kept.astype(BF16)


def shards(
    queries,
    fresh_keys,
    fresh_values,
    key_cache,
    value_cache,
    lengths,
    block_table,
    resid,
    out_weight,
    norm_gain,
    gate_weight,
    up_weight,
    down_weight,
    row_order,
):
    ctx, ring, grp = lax.axis_size(CTX), lax.axis_size(RING), lax.axis_size(GRP)
    core = lax.axis_index("core")
    reqs, width = resid.shape
    shape = jax.ShapeDtypeStruct

    half = gate_weight.shape[1] // 2
    given = jnp.stack(
        [lax.dynamic_slice_in_dim(w, (1 - core) * half, half, 1) for w in (gate_weight, up_weight)]
    )
    met = lax.ppermute(given, "core", [(0, 1), (1, 0)])

    my_queries = queries.reshape(2 * GROUP, HD)
    all_queries = exchange(jnp.broadcast_to(my_queries[None], (ctx, 2 * GROUP, HD)), CTX)
    scratch = [pltpu.VMEM((reqs, GROUP, LANES), F32)] * 3
    parts = call(attend_body, shape((ctx, 3 * GROUP, HD), BF16), [SMEM] + [VMEM] * 4, scratch)(
        lengths, block_table, all_queries, key_cache, value_cache
    )
    parts = exchange(parts, CTX)
    local = call(combine_body, shape((ctx, 2 * GROUP, HD), BF16), [VMEM] * 4)(
        parts, my_queries, fresh_keys, fresh_values
    )
    attended = exchange(local, CTX)
    projected = call(
        project_body,
        shape((grp, reqs, width), BF16),
        [VMEM] * 2,
        [pltpu.VMEM((reqs * GROUP, HD), F32)],
    )(attended, out_weight)
    projected = exchange(projected, GRP)
    hidden, pay = call(
        hidden_body,
        (shape((reqs, width), BF16), shape((2, reqs, width), BF16)),
        [VMEM] * 3,
    )(projected, resid, norm_gain.reshape(1, width))
    pay = lax.all_gather(pay, "core", axis=0, tiled=False)
    blocks = 2 * half // LANES
    wide = call(widen_body, shape((ring // 2, 2, blocks * 4 + 8, LANES), BF16), [VMEM] * 4)(
        pay, gate_weight, up_weight, met
    )
    wide = exchange(wide.reshape(ring, blocks * 4 + 8, LANES), RING)
    units = blocks * 2
    padded = -(-units // 16) * 16
    model_width = width * ctx

    def activate(part_ref, out_ref):
        activate_body(model_width, part_ref, out_ref)

    active = call(activate, shape((ring, padded, LANES), BF16), [VMEM])(wide)
    active = exchange(active, RING)
    met_active = lax.ppermute(active, "core", [(0, 1), (1, 0)])
    rows, kept = call(
        down_body,
        (shape((reqs, width), BF16), shape((reqs, width), BF16)),
        [VMEM] * 5,
    )(
        active.reshape(ring // 2, 2, padded, LANES),
        met_active.reshape(ring // 2, 2, padded, LANES),
        down_weight,
        row_order.reshape(1, reqs),
        hidden,
    )
    share = reqs // grp
    rows = exchange(rows.reshape(grp, share, width), GRP)
    kept = lax.dynamic_index_in_dim(kept.reshape(grp, share, width), lax.axis_index(GRP), 0, False)
    return (kept.astype(F32) + jnp.sum(rows.astype(F32), axis=0)).astype(BF16)


def solution(mesh, sizes=(8, 4, 2, 2, 4)):
    inner = Mesh(mesh.devices.reshape(sizes), ("y", "zl", "core", "zh", "x"))
    in_specs = (
        P(CTX, GRP),
        P(CTX, GRP),
        P(CTX, GRP),
        P(CTX, None, GRP),
        P(CTX, None, GRP),
        P(),
        P(),
        P(None, CTX),
        P(GRP, CTX),
        P(CTX),
        P(CTX, GRP),
        P(CTX, GRP),
        P(GRP, CTX),
        P(),
    )
    out_specs = P(GRP, CTX)
    return jax.shard_map(shards, mesh=inner, in_specs=in_specs, out_specs=out_specs, check_vma=False)
```

```python
import jax
import jax.numpy as jnp
from jax import lax
from jax.experimental import pallas as pl
from jax.experimental.pallas import tpu as pltpu
from jax.sharding import Mesh
from jax.sharding import PartitionSpec as P

HD = 128
GROUP = 8
LANES = 128
EPS = 1e-05
NEG = -1e30
VMEM_LIMIT = 16 * 2**20
CTX = ("y", "zl", "core")
RING = ("y", "zl")
GRP = ("zh", "x")
F32 = jnp.float32
BF16 = jnp.bfloat16
VMEM = pl.BlockSpec(memory_space=pltpu.VMEM)
SMEM = pl.BlockSpec(memory_space=pltpu.SMEM)


def exchange(x, axes):
    return lax.all_to_all(x, axes, 0, 0, tiled=True)


def lane_ids(shape):
    return lax.broadcasted_iota(jnp.int32, shape, len(shape) - 1)


def call(body, out_shape, in_specs, scratch=()):
    return pl.pallas_call(
        body,
        out_shape=out_shape,
        in_specs=in_specs,
        out_specs=jax.tree.map(lambda _: VMEM, out_shape),
        scratch_shapes=list(scratch),
        compiler_params=pltpu.CompilerParams(vmem_limit_bytes=VMEM_LIMIT),
    )


def attend_body(len_ref, table_ref, q_ref, k_ref, v_ref, out_ref, top_ref, sum_ref, acc_ref):
    slots, page = k_ref.shape[0], k_ref.shape[1]
    first = lax.axis_index(CTX) * slots
    table = table_ref[...] - first
    rows, cols = table.shape
    code = lax.broadcasted_iota(jnp.int32, (rows, cols), 0) * cols + lane_ids((rows, cols))
    top_ref[...] = jnp.full(top_ref.shape, NEG, F32)
    sum_ref[...] = jnp.zeros(sum_ref.shape, F32)
    acc_ref[...] = jnp.zeros(acc_ref.shape, F32)
    lane = lane_ids((GROUP, page))
    owners, scores = [], []
    for s in range(slots):
        found = jnp.min(jnp.where(table == s, code, rows * cols - 1))
        owner, page_no = found // cols, found % cols
        live = len_ref[owner] - page_no * page
        pair = q_ref[owner // 2].astype(F32)
        q = jnp.where(owner % 2 == 1, pair[GROUP:], pair[:GROUP]).astype(BF16)
        score = lax.dot_general(q, k_ref[s], (((1,), (1,)), ((), ())), preferred_element_type=F32)
        score = jnp.where(lane < live, score * HD ** (-0.5), NEG)
        best = jnp.max(score, axis=1, keepdims=True)
        top_ref[owner] = jnp.maximum(top_ref[owner], jnp.broadcast_to(best, (GROUP, LANES)))
        owners.append(owner)
        scores.append(score)
    for s in range(slots):
        owner = owners[s]
        shift = top_ref[owner].astype(BF16).astype(F32)
        weight = jnp.exp(scores[s] - shift)
        total = jnp.sum(weight, axis=1, keepdims=True)
        sum_ref[owner] = sum_ref[owner] + jnp.broadcast_to(total, (GROUP, LANES))
        acc_ref[owner] = acc_ref[owner] + jnp.dot(
            weight.astype(BF16), v_ref[s], preferred_element_type=F32
        )
    lane = lane_ids((GROUP, LANES))
    for d in range(out_ref.shape[0]):
        stats = jnp.zeros((GROUP, LANES), F32)
        for par in range(2):
            total = sum_ref[2 * d + par]
            high = total.astype(BF16).astype(F32)
            base = par * 64
            stats = jnp.where(lane == base, top_ref[2 * d + par], stats)
            stats = jnp.where(lane == base + 1, high, stats)
            stats = jnp.where(lane == base + 2, total - high, stats)
        block = jnp.concatenate([acc_ref[2 * d], acc_ref[2 * d + 1], stats], axis=0)
        out_ref[d] = block.astype(BF16)


def combine_body(part_ref, q_ref, fk_ref, fv_ref, out_ref):
    count = part_ref.shape[0]
    fk, fv = fk_ref[...].astype(F32), fv_ref[...].astype(F32)
    q = q_ref[...].astype(F32)
    done = []
    for par in range(2):
        base = par * 64
        mine = slice(par * GROUP, (par + 1) * GROUP)
        own = jnp.sum(q[mine] * fk[par : par + 1], axis=1, keepdims=True) * HD ** (-0.5)
        best = own
        for d in range(count):
            stats = part_ref[d].astype(F32)[2 * GROUP :]
            best = jnp.maximum(best, stats[:, base : base + 1])
        own_weight = jnp.exp(own - best)
        total = own_weight
        acc = own_weight.astype(BF16).astype(F32) * fv[par : par + 1]
        for d in range(count):
            block = part_ref[d].astype(F32)
            stats = block[2 * GROUP :]
            factor = jnp.exp(stats[:, base : base + 1] - best)
            total = total + factor * (stats[:, base + 1 : base + 2] + stats[:, base + 2 : base + 3])
            acc = acc + factor * block[mine]
        done.append(acc / total)
    rows = jnp.concatenate(done, axis=0).astype(BF16)
    for d in range(count):
        out_ref[d] = rows


def project_body(att_ref, w_ref, out_ref, rows_ref):
    count, per, _ = att_ref.shape
    rows_ref[...] = att_ref[...].astype(F32).reshape(count * per, HD)
    reqs = count * per // GROUP
    total = jnp.zeros((reqs, w_ref.shape[1]), F32)
    for h in range(GROUP):
        head = rows_ref[pl.ds(h, reqs, stride=GROUP), :].astype(BF16)
        total = total + jnp.dot(head, w_ref[h * HD : (h + 1) * HD, :], preferred_element_type=F32)
    total = total.astype(BF16)
    for g in range(out_ref.shape[0]):
        out_ref[g] = total


def hidden_body(part_ref, resid_ref, gain_ref, hidden_ref, pay_ref):
    total = resid_ref[...].astype(F32)
    projected = part_ref[0].astype(F32)
    for g in range(1, part_ref.shape[0]):
        projected = projected + part_ref[g].astype(F32)
    hidden = (total + projected).astype(BF16)
    hidden_ref[...] = hidden
    wide = hidden.astype(F32)
    pay_ref[0] = (wide * gain_ref[...].astype(F32)).astype(BF16)
    square = jnp.sum(wide * wide, axis=1, keepdims=True)
    high = square.astype(BF16).astype(F32)
    lane = lane_ids(wide.shape)
    pay_ref[1] = jnp.where(lane == 0, high, jnp.where(lane == 1, square - high, 0.0)).astype(BF16)


def low_half(shape):
    return lax.broadcasted_iota(jnp.int32, shape, 0) % 8 < 4


def split_fours(first, second, low):
    rows = first.shape[0]
    even = jnp.where(low, first, pltpu.roll(second, 4, 0))
    odd = jnp.where(low, pltpu.roll(first, rows - 4, 0), second)
    return even.reshape(rows // 8, 8, LANES), odd.reshape(rows // 8, 8, LANES)


def join_fours(even, odd, low):
    rows = even.shape[0] * 8
    even, odd = even.reshape(rows, LANES), odd.reshape(rows, LANES)
    first = jnp.where(low, even, pltpu.roll(odd, 4, 0))
    second = jnp.where(low, pltpu.roll(even, rows - 4, 0), odd)
    return first, second


def widen_body(pay_ref, gate_ref, up_ref, met_ref, out_ref):
    core = lax.axis_index("core")
    mine, other = pay_ref[core, 0], pay_ref[1 - core, 0]
    square = pay_ref[0, 1].astype(F32) + pay_ref[1, 1].astype(F32)
    high = square.astype(BF16).astype(F32)
    rows = mine.shape[0]
    low = low_half((rows, LANES))
    half = met_ref.shape[2]
    pairs = half // (2 * LANES)

    def pair_tiles(p):
        ref, which, at = (gate_ref, 0, p) if p < pairs else (up_ref, 1, p - pairs)
        start = pl.multiple_of(core * half + at * 2 * LANES, LANES)
        x = jnp.dot(mine, ref[:, pl.ds(start, 2 * LANES)], preferred_element_type=F32)
        x = x + jnp.dot(
            other, met_ref[which, :, at * 2 * LANES : (at + 1) * 2 * LANES], preferred_element_type=F32
        )
        return split_fours(x[:, :LANES], x[:, LANES:], low)

    for g in range(pairs):
        even0, odd0 = pair_tiles(2 * g)
        even1, odd1 = pair_tiles(2 * g + 1)
        out_ref[:, 0, g * 16 : (g + 1) * 16, :] = jnp.concatenate([even0, even1], axis=1).astype(BF16)
        out_ref[:, 1, g * 16 : (g + 1) * 16, :] = jnp.concatenate([odd0, odd1], axis=1).astype(BF16)
    lane = lane_ids((rows, LANES))
    total = square + pltpu.roll(square, LANES - 1, 1)
    high = total.astype(BF16).astype(F32)
    rest = pltpu.roll(total - high, 1, 1)
    square = jnp.where(lane == 0, high, jnp.where(lane == 1, rest, 0.0))
    zero = jnp.zeros((rows, LANES), F32)
    even, odd = split_fours(square, zero, low)
    out_ref[:, 0, pairs * 16 :, :] = even.astype(BF16)
    out_ref[:, 1, pairs * 16 :, :] = odd.astype(BF16)


def activate_body(width, part_ref, out_ref):
    total = part_ref[0].astype(F32)
    for d in range(1, part_ref.shape[0]):
        total = total + part_ref[d].astype(F32)
    units = (total.shape[0] - 8) // 2
    square = total[2 * units : 2 * units + 8]
    square = square[:, 0:1] + square[:, 1:2]
    square = jnp.broadcast_to(square, (8, LANES))
    square = square + pltpu.roll(square, 4, 0)
    inv_rms = lax.rsqrt(square / width + EPS)[None]
    gate = total[:units].reshape(units // 8, 8, LANES) * inv_rms
    up = total[units : 2 * units].reshape(units // 8, 8, LANES) * inv_rms
    active = (gate / (1.0 + jnp.exp(-gate)) * up).reshape(units, LANES)
    pad = jnp.zeros((out_ref.shape[1] - units, LANES), F32)
    active = jnp.concatenate([active, pad], axis=0).astype(BF16)
    for d in range(out_ref.shape[0]):
        out_ref[d] = active


def down_body(mine_ref, met_ref, w_ref, order_ref, hidden_ref, out_ref, kept_ref):
    core = lax.axis_index("core")
    rows = mine_ref.shape[0] * 8
    low = low_half((rows, LANES))
    half = w_ref.shape[0] // 2
    pairs = half // (2 * LANES)
    total = jnp.zeros((rows, LANES), F32)
    for act_ref, c in ((mine_ref, core), (met_ref, 1 - core)):
        for g in range((pairs + 1) // 2):
            even = act_ref[:, 0, g * 16 : (g + 1) * 16, :].astype(F32)
            odd = act_ref[:, 1, g * 16 : (g + 1) * 16, :].astype(F32)
            for k in range(2):
                p = 2 * g + k
                if p >= pairs:
                    continue
                first, second = join_fours(even[:, k * 8 : k * 8 + 8], odd[:, k * 8 : k * 8 + 8], low)
                block = jnp.concatenate([first, second], axis=1).astype(BF16)
                start = pl.multiple_of(c * half + p * 2 * LANES, LANES)
                total = total + jnp.dot(
                    block, w_ref[pl.ds(start, 2 * LANES), :], preferred_element_type=F32
                )
    reqs = order_ref.shape[1]
    pick = lax.broadcasted_iota(jnp.int32, (reqs, reqs), 0) == order_ref[...]
    pick = pick.astype(F32).astype(BF16)
    first_dim = (((0,), (0,)), ((), ()))
    out = lax.dot_general(pick, total.astype(BF16), first_dim, preferred_element_type=F32)
    out_ref[...] = out.astype(BF16)
    kept = lax.dot_general(pick, hidden_ref[...], first_dim, preferred_element_type=F32)
    kept_ref[...] = kept.astype(BF16)


def shards(
    queries,
    fresh_keys,
    fresh_values,
    key_cache,
    value_cache,
    lengths,
    block_table,
    resid,
    out_weight,
    norm_gain,
    gate_weight,
    up_weight,
    down_weight,
    row_order,
):
    ctx, ring, grp = lax.axis_size(CTX), lax.axis_size(RING), lax.axis_size(GRP)
    core = lax.axis_index("core")
    reqs, width = resid.shape
    shape = jax.ShapeDtypeStruct

    half = gate_weight.shape[1] // 2
    given = jnp.stack(
        [lax.dynamic_slice_in_dim(w, (1 - core) * half, half, 1) for w in (gate_weight, up_weight)]
    )
    met = lax.ppermute(given, "core", [(0, 1), (1, 0)])

    my_queries = queries.reshape(2 * GROUP, HD)
    all_queries = exchange(jnp.broadcast_to(my_queries[None], (ctx, 2 * GROUP, HD)), CTX)
    scratch = [pltpu.VMEM((reqs, GROUP, LANES), F32)] * 3
    parts = call(attend_body, shape((ctx, 3 * GROUP, HD), BF16), [SMEM] + [VMEM] * 4, scratch)(
        lengths, block_table, all_queries, key_cache, value_cache
    )
    parts = exchange(parts, CTX)
    local = call(combine_body, shape((ctx, 2 * GROUP, HD), BF16), [VMEM] * 4)(
        parts, my_queries, fresh_keys, fresh_values
    )
    attended = exchange(local, CTX)
    projected = call(
        project_body,
        shape((grp, reqs, width), BF16),
        [VMEM] * 2,
        [pltpu.VMEM((reqs * GROUP, HD), F32)],
    )(attended, out_weight)
    projected = exchange(projected, GRP)
    hidden, pay = call(
        hidden_body,
        (shape((reqs, width), BF16), shape((2, reqs, width), BF16)),
        [VMEM] * 3,
    )(projected, resid, norm_gain.reshape(1, width))
    pay = lax.all_gather(pay, "core", axis=0, tiled=False)
    blocks = 2 * half // LANES
    wide = call(widen_body, shape((ring // 2, 2, blocks * 4 + 8, LANES), BF16), [VMEM] * 4)(
        pay, gate_weight, up_weight, met
    )
    wide = exchange(wide.reshape(ring, blocks * 4 + 8, LANES), RING)
    units = blocks * 2
    padded = -(-units // 16) * 16
    model_width = width * ctx

    def activate(part_ref, out_ref):
        activate_body(model_width, part_ref, out_ref)

    active = call(activate, shape((ring, padded, LANES), BF16), [VMEM])(wide)
    active = exchange(active, RING)
    met_active = lax.ppermute(active, "core", [(0, 1), (1, 0)])
    rows, kept = call(
        down_body,
        (shape((reqs, width), BF16), shape((reqs, width), BF16)),
        [VMEM] * 5,
    )(
        active.reshape(ring // 2, 2, padded, LANES),
        met_active.reshape(ring // 2, 2, padded, LANES),
        down_weight,
        row_order.reshape(1, reqs),
        hidden,
    )
    share = reqs // grp
    rows = exchange(rows.reshape(grp, share, width), GRP)
    kept = lax.dynamic_index_in_dim(kept.reshape(grp, share, width), lax.axis_index(GRP), 0, False)
    return (kept.astype(F32) + jnp.sum(rows.astype(F32), axis=0)).astype(BF16)


def solution(mesh, sizes=(8, 4, 2, 2, 4)):
    inner = Mesh(mesh.devices.reshape(sizes), ("y", "zl", "core", "zh", "x"))
    in_specs = (
        P(CTX, GRP),
        P(CTX, GRP),
        P(CTX, GRP),
        P(CTX, None, GRP),
        P(CTX, None, GRP),
        P(),
        P(),
        P(None, CTX),
        P(GRP, CTX),
        P(CTX),
        P(CTX, GRP),
        P(CTX, GRP),
        P(GRP, CTX),
        P(),
    )
    out_specs = P(GRP, CTX)
    return jax.shard_map(shards, mesh=inner, in_specs=in_specs, out_specs=out_specs, check_vma=False)
```

```python
import jax
import jax.numpy as jnp
from jax import lax
from jax.experimental import pallas as pl
from jax.experimental.pallas import tpu as pltpu
from jax.sharding import Mesh
from jax.sharding import PartitionSpec as P

HD = 128
GROUP = 8
LANES = 128
EPS = 1e-05
NEG = -1e30
VMEM_LIMIT = 16 * 2**20
CTX = ("y", "zlh", "zll", "core")
RING = ("y", "zlh", "zll")
REST = ("y", "zlh")
TEAM = ("zll", "core")
GRP = ("zh", "x")
LAST = ("core", "zh", "x")
F32 = jnp.float32
BF16 = jnp.bfloat16
VMEM = pl.BlockSpec(memory_space=pltpu.VMEM)
SMEM = pl.BlockSpec(memory_space=pltpu.SMEM)


def exchange(x, axes):
    return lax.all_to_all(x, axes, 0, 0, tiled=True)


def lane_ids(shape):
    return lax.broadcasted_iota(jnp.int32, shape, len(shape) - 1)


def call(body, out_shape, in_specs, scratch=(), out_specs=None):
    return pl.pallas_call(
        body,
        out_shape=out_shape,
        in_specs=in_specs,
        out_specs=jax.tree.map(lambda _: VMEM, out_shape) if out_specs is None else out_specs,
        scratch_shapes=list(scratch),
        compiler_params=pltpu.CompilerParams(vmem_limit_bytes=VMEM_LIMIT),
    )


def prepare_body(len_ref, table_ref, gain_ref, order_ref, meta_ref, wide_gain_ref, pick_ref):
    slots = meta_ref.shape[0] // 2
    first = lax.axis_index(CTX) * slots
    table = table_ref[...] - first
    rows, cols = table.shape
    code = lax.broadcasted_iota(jnp.int32, (rows, cols), 0) * cols + lane_ids((rows, cols))
    for s in range(slots):
        found = jnp.min(jnp.where(table == s, code, rows * cols - 1))
        owner = found // cols
        meta_ref[s] = owner
        meta_ref[slots + s] = len_ref[owner] - (found % cols) * LANES
    wide_gain_ref[...] = jnp.broadcast_to(gain_ref[...].astype(F32), wide_gain_ref.shape)
    pick = lax.broadcasted_iota(jnp.int32, pick_ref.shape, 0) == order_ref[...]
    pick_ref[...] = pick.astype(F32).astype(BF16)


def cut_body(gate_ref, up_ref, *out_refs):
    me = lax.axis_index(TEAM)
    width = out_refs[0].shape[2]
    for flip, out_ref in enumerate(out_refs, 1):
        start = pl.multiple_of((me ^ flip) * width, LANES)
        out_ref[0] = gate_ref[:, pl.ds(start, width)]
        out_ref[1] = up_ref[:, pl.ds(start, width)]


def cut_down_body(w_ref, out_ref):
    other = 1 - lax.axis_index("core")
    height = out_ref.shape[1]
    for z in range(2):
        start = pl.multiple_of((2 * z + other) * height, LANES)
        out_ref[z] = w_ref[pl.ds(start, height), :]


def attend_body(meta_ref, q_ref, k_ref, v_ref, out_ref, top_ref, sum_ref, acc_ref):
    slots, page = k_ref.shape[0], k_ref.shape[1]
    top_ref[...] = jnp.full(top_ref.shape, NEG, F32)
    sum_ref[...] = jnp.zeros(sum_ref.shape, F32)
    acc_ref[...] = jnp.zeros(acc_ref.shape, F32)
    lane = lane_ids((GROUP, page))
    owners, scores = [], []
    for s in range(slots):
        owner, live = meta_ref[s], meta_ref[slots + s]
        home = owner // 2
        pair = q_ref[home % 2, home // 2].astype(F32)
        q = jnp.where(owner % 2 == 1, pair[GROUP:], pair[:GROUP]).astype(BF16)
        score = lax.dot_general(q, k_ref[s], (((1,), (1,)), ((), ())), preferred_element_type=F32)
        score = jnp.where(lane < live, score * HD ** (-0.5), NEG)
        best = jnp.max(score, axis=1, keepdims=True)
        top_ref[owner] = jnp.maximum(top_ref[owner], jnp.broadcast_to(best, (GROUP, LANES)))
        owners.append(owner)
        scores.append(score)
    for s in range(slots):
        owner = owners[s]
        shift = top_ref[owner].astype(BF16).astype(F32)
        weight = jnp.exp(scores[s] - shift)
        total = jnp.sum(weight, axis=1, keepdims=True)
        sum_ref[owner] = sum_ref[owner] + jnp.broadcast_to(total, (GROUP, LANES))
        acc_ref[owner] = acc_ref[owner] + jnp.dot(
            weight.astype(BF16), v_ref[s], preferred_element_type=F32
        )
    lane = lane_ids((GROUP, LANES))
    for d in range(out_ref.shape[0]):
        stats = jnp.zeros((GROUP, LANES), F32)
        for par in range(2):
            total = sum_ref[2 * d + par]
            high = total.astype(BF16).astype(F32)
            base = par * 64
            stats = jnp.where(lane == base, top_ref[2 * d + par], stats)
            stats = jnp.where(lane == base + 1, high, stats)
            stats = jnp.where(lane == base + 2, total - high, stats)
        block = jnp.concatenate([acc_ref[2 * d], acc_ref[2 * d + 1], stats], axis=0)
        out_ref[d] = block.astype(BF16)


def combine_body(part_ref, q_ref, fk_ref, fv_ref, out_ref):
    count = part_ref.shape[0]
    fk, fv = fk_ref[...].astype(F32), fv_ref[...].astype(F32)
    q = q_ref[...].astype(F32)
    done = []
    for par in range(2):
        base = par * 64
        mine = slice(par * GROUP, (par + 1) * GROUP)
        own = jnp.sum(q[mine] * fk[par : par + 1], axis=1, keepdims=True) * HD ** (-0.5)
        best = own
        for d in range(count):
            stats = part_ref[d].astype(F32)[2 * GROUP :]
            best = jnp.maximum(best, stats[:, base : base + 1])
        own_weight = jnp.exp(own - best)
        total = own_weight
        acc = own_weight.astype(BF16).astype(F32) * fv[par : par + 1]
        for d in range(count):
            block = part_ref[d].astype(F32)
            stats = block[2 * GROUP :]
            factor = jnp.exp(stats[:, base : base + 1] - best)
            total = total + factor * (stats[:, base + 1 : base + 2] + stats[:, base + 2 : base + 3])
            acc = acc + factor * block[mine]
        done.append(acc / total)
    rows = jnp.concatenate(done, axis=0).astype(BF16)
    for d in range(out_ref.shape[0]):
        out_ref[d] = rows


def project_body(att_ref, w_ref, out_ref, rows_ref):
    cores, count, per, _ = att_ref.shape
    for d in range(count):
        for c in range(cores):
            start = (d * cores + c) * per
            rows_ref[start : start + per, :] = att_ref[c, d].astype(F32)
    reqs = rows_ref.shape[0] // GROUP
    total = jnp.zeros((reqs, w_ref.shape[1]), F32)
    for h in range(GROUP):
        head = rows_ref[pl.ds(h, reqs, stride=GROUP), :].astype(BF16)
        total = total + jnp.dot(head, w_ref[h * HD : (h + 1) * HD, :], preferred_element_type=F32)
    total = total.astype(BF16)
    for g in range(out_ref.shape[0]):
        out_ref[g] = total


def turned(column):
    return jnp.transpose(jnp.broadcast_to(column, (LANES, LANES)))


def hidden_body(part_ref, resid_ref, gain_ref, hidden_ref, pay_ref):
    projected = part_ref[0].astype(F32)
    for g in range(1, part_ref.shape[0]):
        projected = projected + part_ref[g].astype(F32)
    hidden = (resid_ref[...].astype(F32) + projected).astype(BF16)
    hidden_ref[...] = hidden
    wide = hidden.astype(F32)
    reqs = wide.shape[0]
    pay_ref[:reqs] = (wide * gain_ref[0:1, :]).astype(BF16)
    square = jnp.sum(wide * wide, axis=1, keepdims=True)
    square = jnp.concatenate([square, jnp.zeros((LANES - reqs, 1), F32)], axis=0) if reqs < LANES else square
    square = turned(square)[:8]
    high = square.astype(BF16).astype(F32)
    row = lax.broadcasted_iota(jnp.int32, (8, LANES), 0)
    pay_ref[reqs:] = jnp.where(row == 0, high, jnp.where(row == 1, square - high, 0.0)).astype(BF16)


def widen_body(pay_ref, gate_ref, up_ref, met1_ref, met2_ref, met3_ref, out_ref):
    me = lax.axis_index(TEAM)
    team, reqs = pay_ref.shape[0], pay_ref.shape[1] - 8
    mets = (met1_ref, met2_ref, met3_ref)
    width = met1_ref.shape[2]
    start = pl.multiple_of(me * width, LANES)
    tiles = []
    for which, ref in enumerate((gate_ref, up_ref)):
        x = jnp.dot(pay_ref[me, :reqs], ref[:, pl.ds(start, width)], preferred_element_type=F32)
        for flip, met_ref in enumerate(mets, 1):
            x = x + jnp.dot(pay_ref[me ^ flip, :reqs], met_ref[which], preferred_element_type=F32)
        for b in range(width // LANES):
            tiles.append(x[:, b * LANES : (b + 1) * LANES].reshape(reqs // 8, 8, LANES))
    for i in range(len(tiles) // 2):
        out_ref[:, i * 16 : (i + 1) * 16, :] = jnp.concatenate(
            [tiles[2 * i], tiles[2 * i + 1]], axis=1
        ).astype(BF16)
    square = pay_ref[0, reqs:].astype(F32)
    for d in range(1, team):
        square = square + pay_ref[d, reqs:].astype(F32)
    square = turned(square[0:1] + square[1:2])[:reqs]
    high = square.astype(BF16).astype(F32)
    lane = lane_ids(square.shape)
    square = jnp.where(lane == 0, high, jnp.where(lane == 1, square - high, 0.0))
    out_ref[:, len(tiles) * 8 :, :] = square.reshape(reqs // 8, 8, LANES).astype(BF16)


def activate_body(width, part_ref, out_ref):
    total = part_ref[0].astype(F32)
    for d in range(1, part_ref.shape[0]):
        total = total + part_ref[d].astype(F32)
    units = (total.shape[0] - 8) // 2
    square = total[2 * units :]
    square = square[:, 0:1] + square[:, 1:2]
    inv_rms = lax.rsqrt(jnp.broadcast_to(square, (8, LANES)) / width + EPS)[None]
    gate = total[:units].reshape(units // 8, 8, LANES) * inv_rms
    up = total[units : 2 * units].reshape(units // 8, 8, LANES) * inv_rms
    active = (gate / (1.0 + jnp.exp(-gate)) * up).reshape(units, LANES).astype(BF16)
    for d in range(out_ref.shape[0]):
        out_ref[d] = active


def down_body(act_ref, w_ref, met_ref, pick_ref, hidden_ref, out_ref, kept_ref):
    core = lax.axis_index("core")
    dests = act_ref.shape[0]
    reqs = dests * 8
    height = met_ref.shape[1]
    mine = jnp.zeros((reqs, LANES), F32)
    other = jnp.zeros((reqs, LANES), F32)
    for z in range(2):
        act = act_ref[:, z].astype(F32)
        blocks = [
            act[:, b * 8 : b * 8 + 8].reshape(reqs, LANES).astype(BF16) for b in range(height // LANES)
        ]
        act = jnp.concatenate(blocks, axis=1)
        start = pl.multiple_of((2 * z + core) * height, LANES)
        mine = mine + jnp.dot(act, w_ref[pl.ds(start, height), :], preferred_element_type=F32)
        other = other + jnp.dot(act, met_ref[z], preferred_element_type=F32)
    pick = pick_ref[...]
    dims = (((0,), (0,)), ((), ()))
    out_ref[core] = lax.dot_general(
        pick, mine.astype(BF16), dims, preferred_element_type=F32
    ).astype(BF16)
    out_ref[1 - core] = lax.dot_general(
        pick, other.astype(BF16), dims, preferred_element_type=F32
    ).astype(BF16)
    kept = lax.dot_general(pick, hidden_ref[...], dims, preferred_element_type=F32)
    kept_ref[...] = kept.astype(BF16)


def shards(
    queries,
    fresh_keys,
    fresh_values,
    key_cache,
    value_cache,
    lengths,
    block_table,
    resid,
    out_weight,
    norm_gain,
    gate_weight,
    up_weight,
    down_weight,
    row_order,
):
    ctx, ring, rest, grp = (lax.axis_size(axes) for axes in (CTX, RING, REST, GRP))
    team = lax.axis_size(TEAM)
    reqs, width = resid.shape
    slots = key_cache.shape[0]
    shape = jax.ShapeDtypeStruct

    quarter = gate_weight.shape[1] // team
    given = call(cut_body, (shape((2, width, quarter), BF16),) * 3, [VMEM] * 2)(gate_weight, up_weight)
    met = [
        lax.ppermute(block, TEAM, [(i, i ^ flip) for i in range(team)])
        for flip, block in enumerate(given, 1)
    ]
    given_down = call(cut_down_body, shape((2, quarter, width), BF16), [VMEM])(down_weight)
    met_down = lax.ppermute(given_down, "core", [(0, 1), (1, 0)])
    meta, wide_gain, pick = call(
        prepare_body,
        (shape((2 * slots,), jnp.int32), shape((8, width), F32), shape((reqs, reqs), BF16)),
        [SMEM] + [VMEM] * 3,
        out_specs=(SMEM, VMEM, VMEM),
    )(lengths, block_table, norm_gain.reshape(1, width), row_order.reshape(1, reqs))

    my_queries = queries.reshape(2 * GROUP, HD)
    all_queries = exchange(jnp.broadcast_to(my_queries[None], (ring, 2 * GROUP, HD)), RING)
    all_queries = lax.all_gather(all_queries, "core", axis=0, tiled=False)
    scratch = [pltpu.VMEM((reqs, GROUP, LANES), F32)] * 3
    parts = call(attend_body, shape((ctx, 3 * GROUP, HD), BF16), [SMEM] + [VMEM] * 3, scratch)(
        meta, all_queries, key_cache, value_cache
    )
    parts = exchange(parts, CTX)
    local = call(combine_body, shape((ring, 2 * GROUP, HD), BF16), [VMEM] * 4)(
        parts, my_queries, fresh_keys, fresh_values
    )
    attended = lax.all_gather(exchange(local, RING), "core", axis=0, tiled=False)
    attended, *met = lax.optimization_barrier((attended, *met))
    projected = call(
        project_body,
        shape((grp, reqs, width), BF16),
        [VMEM] * 2,
        [pltpu.VMEM((reqs * GROUP, HD), F32)],
    )(attended, out_weight)
    projected = exchange(projected, GRP)
    hidden, pay = call(
        hidden_body,
        (shape((reqs, width), BF16), shape((reqs + 8, width), BF16)),
        [VMEM] * 3,
    )(projected, resid, wide_gain)
    pay = lax.all_gather(pay, TEAM, axis=0, tiled=False)
    units = quarter // LANES * 8
    wide = call(widen_body, shape((rest, 2 * units + 8, LANES), BF16), [VMEM] * 6)(
        pay, gate_weight, up_weight, *met
    )
    wide = exchange(wide, REST)
    model_width = width * ctx

    def activate(part_ref, out_ref):
        activate_body(model_width, part_ref, out_ref)

    active = call(activate, shape((ring, units, LANES), BF16), [VMEM])(wide)
    active = exchange(active, RING)
    rows, kept = call(
        down_body,
        (shape((2, reqs, width), BF16), shape((reqs, width), BF16)),
        [VMEM] * 5,
    )(active.reshape(rest, 2, units, LANES), down_weight, met_down, pick, hidden)
    share = reqs // grp
    rows = exchange(rows.reshape(2 * grp, share, width), LAST)
    kept = lax.dynamic_index_in_dim(kept.reshape(grp, share, width), lax.axis_index(GRP), 0, False)
    return (kept.astype(F32) + jnp.sum(rows.astype(F32), axis=0)).astype(BF16)


def solution(mesh, sizes=(8, 2, 2, 2, 2, 4)):
    inner = Mesh(mesh.devices.reshape(sizes), ("y", "zlh", "zll", "core", "zh", "x"))
    in_specs = (
        P(CTX, GRP),
        P(CTX, GRP),
        P(CTX, GRP),
        P(CTX, None, GRP),
        P(CTX, None, GRP),
        P(),
        P(),
        P(None, CTX),
        P(GRP, CTX),
        P(CTX),
        P(CTX, GRP),
        P(CTX, GRP),
        P(GRP, CTX),
        P(),
    )
    out_specs = P(GRP, CTX)
    return jax.shard_map(shards, mesh=inner, in_specs=in_specs, out_specs=out_specs, check_vma=False)
```

```python
import functools

import jax
import jax.numpy as jnp
from jax import lax
from jax.experimental import pallas as pl
from jax.experimental.pallas import tpu as pltpu
from jax.sharding import Mesh
from jax.sharding import PartitionSpec as P

HD = 128
GROUP = 8
LANES = 128
EPS = 1e-05
NEG = -1e30
VMEM_LIMIT = 16 * 2**20
CTX = ("yh", "yl", "zl", "core")
RING = ("yh", "yl", "zl")
REST = ("yh", "zl")
TEAM = ("yl", "core")
GRP = ("zh", "x")
LAST = TEAM + GRP
F32 = jnp.float32
BF16 = jnp.bfloat16
VMEM = pl.BlockSpec(memory_space=pltpu.VMEM)
SMEM = pl.BlockSpec(memory_space=pltpu.SMEM)


def exchange(x, axes):
    return lax.all_to_all(x, axes, 0, 0, tiled=True)


def lane_ids(shape):
    return lax.broadcasted_iota(jnp.int32, shape, len(shape) - 1)


def call(body, out_shape, in_specs, scratch=(), out_specs=None):
    return pl.pallas_call(
        body,
        out_shape=out_shape,
        in_specs=in_specs,
        out_specs=jax.tree.map(lambda _: VMEM, out_shape) if out_specs is None else out_specs,
        scratch_shapes=list(scratch),
        compiler_params=pltpu.CompilerParams(vmem_limit_bytes=VMEM_LIMIT),
    )


def request_of(place, ring):
    core, at = place >> ring.bit_length(), place & (2 * ring - 1)
    return (at >> 1) * 4 + core * 2 + (at & 1)


def prepare_body(ring, len_ref, table_ref, order_ref, meta_ref, pick_ref):
    slots = meta_ref.shape[0] // 2
    first = lax.axis_index(CTX) * slots
    table = table_ref[...] - first
    rows, cols = table.shape
    code = lax.broadcasted_iota(jnp.int32, (rows, cols), 0) * cols + lane_ids((rows, cols))
    for s in range(slots):
        found = jnp.min(jnp.where(table == s, code, rows * cols - 1))
        owner = found // cols
        meta_ref[s] = owner
        meta_ref[slots + s] = len_ref[owner] - (found % cols) * LANES
    place = lax.broadcasted_iota(jnp.int32, pick_ref.shape, 0)
    pick = request_of(place, ring) == order_ref[...]
    pick_ref[...] = pick.astype(F32).astype(BF16)


def cut_body(ring, gate_ref, up_ref, down_ref, resid_ref, gain_ref, *out_refs):
    me = lax.axis_index(TEAM)
    mine, out_refs = out_refs[0], out_refs[1:]
    reqs = resid_ref.shape[0]
    place = lax.broadcasted_iota(jnp.int32, (reqs, reqs), 0)
    turn = (request_of(place, ring) == lane_ids((reqs, reqs))).astype(F32).astype(BF16)
    resid = jnp.dot(turn, resid_ref[...], preferred_element_type=F32).astype(BF16)
    gain = jnp.broadcast_to(gain_ref[...].astype(F32), (LANES, LANES)).astype(BF16)
    mine[0, :reqs] = resid
    mine[1] = gain
    blocks = (out_refs[0].shape[0] - 2) // 3
    for flip, out_ref in enumerate(out_refs, 1):
        start = (me ^ flip) * blocks * LANES
        for b in range(blocks):
            cols = pl.ds(pl.multiple_of(start + b * LANES, LANES), LANES)
            out_ref[b] = gate_ref[:, cols]
            out_ref[blocks + b] = up_ref[:, cols]
            out_ref[2 * blocks + b] = down_ref[cols, :]
        out_ref[3 * blocks, :reqs] = resid
        out_ref[3 * blocks + 1] = gain


def attend_body(meta_ref, q_ref, k_ref, v_ref, out_ref, top_ref, sum_ref, acc_ref):
    slots, page = k_ref.shape[0], k_ref.shape[1]
    top_ref[...] = jnp.full(top_ref.shape, NEG, F32)
    sum_ref[...] = jnp.zeros(sum_ref.shape, F32)
    acc_ref[...] = jnp.zeros(acc_ref.shape, F32)
    lane = lane_ids((GROUP, page))
    owners, scores = [], []
    for s in range(slots):
        owner, live = meta_ref[s], meta_ref[slots + s]
        home = owner // 2
        pair = q_ref[home % 2, home // 2].astype(F32)
        q = jnp.where(owner % 2 == 1, pair[GROUP:], pair[:GROUP]).astype(BF16)
        score = lax.dot_general(q, k_ref[s], (((1,), (1,)), ((), ())), preferred_element_type=F32)
        score = jnp.where(lane < live, score * HD ** (-0.5), NEG)
        best = jnp.max(score, axis=1, keepdims=True)
        top_ref[owner] = jnp.maximum(top_ref[owner], jnp.broadcast_to(best, (GROUP, LANES)))
        owners.append(owner)
        scores.append(score)
    for s in range(slots):
        owner = owners[s]
        shift = top_ref[owner].astype(BF16).astype(F32)
        weight = jnp.exp(scores[s] - shift)
        total = jnp.sum(weight, axis=1, keepdims=True)
        sum_ref[owner] = sum_ref[owner] + jnp.broadcast_to(total, (GROUP, LANES))
        acc_ref[owner] = acc_ref[owner] + jnp.dot(
            weight.astype(BF16), v_ref[s], preferred_element_type=F32
        )
    lane = lane_ids((GROUP, LANES))
    for d in range(out_ref.shape[0]):
        stats = jnp.zeros((GROUP, LANES), F32)
        for par in range(2):
            total = sum_ref[2 * d + par]
            high = total.astype(BF16).astype(F32)
            base = par * 64
            stats = jnp.where(lane == base, top_ref[2 * d + par], stats)
            stats = jnp.where(lane == base + 1, high, stats)
            stats = jnp.where(lane == base + 2, total - high, stats)
        block = jnp.concatenate([acc_ref[2 * d], acc_ref[2 * d + 1], stats], axis=0)
        out_ref[d] = block.astype(BF16)


def combine_body(part_ref, q_ref, fk_ref, fv_ref, out_ref):
    count = part_ref.shape[0]
    fk, fv = fk_ref[...].astype(F32), fv_ref[...].astype(F32)
    q = q_ref[...].astype(F32)
    done = []
    for par in range(2):
        base = par * 64
        mine = slice(par * GROUP, (par + 1) * GROUP)
        own = jnp.sum(q[mine] * fk[par : par + 1], axis=1, keepdims=True) * HD ** (-0.5)
        best = own
        for d in range(count):
            stats = part_ref[d].astype(F32)[2 * GROUP :]
            best = jnp.maximum(best, stats[:, base : base + 1])
        own_weight = jnp.exp(own - best)
        total = own_weight
        acc = own_weight.astype(BF16).astype(F32) * fv[par : par + 1]
        for d in range(count):
            block = part_ref[d].astype(F32)
            stats = block[2 * GROUP :]
            factor = jnp.exp(stats[:, base : base + 1] - best)
            total = total + factor * (stats[:, base + 1 : base + 2] + stats[:, base + 2 : base + 3])
            acc = acc + factor * block[mine]
        done.append(acc / total)
    rows = jnp.concatenate(done, axis=0).astype(BF16)
    for d in range(out_ref.shape[0]):
        out_ref[d] = rows


def project_body(att_ref, w_ref, met_ref, out_ref, rows_ref):
    core = lax.axis_index("core")
    count, per, _ = att_ref.shape
    rows_ref[...] = att_ref[...].astype(F32).reshape(count * per, HD)
    reqs = count * per // GROUP
    heads = [rows_ref[pl.ds(h, reqs, stride=GROUP), :].astype(BF16) for h in range(GROUP)]
    heads = jnp.concatenate(heads, axis=1)
    for at, ref in ((core, w_ref), (1 - core, met_ref)):
        total = jnp.dot(heads, ref[...], preferred_element_type=F32).astype(BF16)
        for g in range(out_ref.shape[0]):
            out_ref[g, at] = total


def gather_body(part_ref, out_ref):
    total = part_ref[0].astype(F32)
    for g in range(1, part_ref.shape[0]):
        total = total + part_ref[g].astype(F32)
    out_ref[...] = total.astype(BF16)


def widen_body(
    pay_ref, mine_ref, gate_ref, up_ref, met1_ref, met2_ref, met3_ref, out_ref, hidden_ref
):
    me = lax.axis_index(TEAM)
    team = 2 * pay_ref.shape[0]
    reqs = 2 * pay_ref.shape[3]
    mets = (met1_ref, met2_ref, met3_ref)
    blocks = (met1_ref.shape[0] - 2) // 3
    square = jnp.zeros((reqs, 1), F32)
    gained = []
    for flip in range(team):
        ref, at = (mine_ref, 0) if flip == 0 else (mets[flip - 1], 3 * blocks)
        owner = me ^ flip
        chip, core = owner // 2, owner % 2
        projected = jnp.concatenate([pay_ref[chip, c, core].astype(F32) for c in range(2)], axis=0)
        hidden = (ref[at, :reqs].astype(F32) + projected).astype(BF16)
        if flip == 0:
            hidden_ref[...] = hidden
        wide = hidden.astype(F32)
        square = square + jnp.sum(wide * wide, axis=1, keepdims=True)
        gained.append((wide * ref[at + 1, :reqs].astype(F32)).astype(BF16))
    gained = jnp.concatenate(gained, axis=1)
    tiles = []
    for b in range(2 * blocks):
        ref, at = (gate_ref, b) if b < blocks else (up_ref, b - blocks)
        cols = pl.ds(pl.multiple_of((me * blocks + at) * LANES, LANES), LANES)
        w = jnp.concatenate([ref[:, cols]] + [met_ref[b] for met_ref in mets], axis=0)
        x = jnp.dot(gained, w, preferred_element_type=F32)
        tiles.append(x.reshape(reqs // 8, 8, LANES))
    for i in range(blocks):
        out_ref[:, i * 16 : (i + 1) * 16, :] = jnp.concatenate(
            [tiles[2 * i], tiles[2 * i + 1]], axis=1
        ).astype(BF16)
    square = jnp.broadcast_to(square, (reqs, LANES))
    high = square.astype(BF16).astype(F32)
    lane = lane_ids(square.shape)
    square = jnp.where(lane == 0, high, jnp.where(lane == 1, square - high, 0.0))
    out_ref[:, blocks * 16 :, :] = square.reshape(reqs // 8, 8, LANES).astype(BF16)


def activate_body(width, part_ref, out_ref):
    total = part_ref[0].astype(F32)
    for d in range(1, part_ref.shape[0]):
        total = total + part_ref[d].astype(F32)
    units = (total.shape[0] - 8) // 2
    square = total[2 * units :]
    square = square[:, 0:1] + square[:, 1:2]
    inv_rms = lax.rsqrt(jnp.broadcast_to(square, (8, LANES)) / width + EPS)[None]
    gate = total[:units].reshape(units // 8, 8, LANES) * inv_rms
    up = total[units : 2 * units].reshape(units // 8, 8, LANES) * inv_rms
    active = (gate / (1.0 + jnp.exp(-gate)) * up).reshape(units, LANES).astype(BF16)
    for d in range(out_ref.shape[0]):
        out_ref[d] = active


def down_body(
    act_ref, w_ref, met1_ref, met2_ref, met3_ref, pick_ref, hidden_ref, out_ref, kept_ref
):
    me = lax.axis_index(TEAM)
    reqs = act_ref.shape[0] * 8
    blocks = act_ref.shape[1] // 8
    act = act_ref[...].astype(F32)
    act = jnp.concatenate(
        [act[:, b * 8 : b * 8 + 8].reshape(reqs, LANES).astype(BF16) for b in range(blocks)], axis=1
    )
    height = blocks * LANES
    pick = pick_ref[...]
    dims = (((0,), (0,)), ((), ()))
    for flip, ref in enumerate((w_ref, met1_ref, met2_ref, met3_ref)):
        if flip == 0:
            w = ref[pl.ds(pl.multiple_of(me * height, LANES), height), :]
        else:
            w = ref[2 * blocks : 3 * blocks].reshape(height, LANES)
        total = jnp.dot(act, w, preferred_element_type=F32).astype(BF16)
        total = lax.dot_general(pick, total, dims, preferred_element_type=F32)
        out_ref[me ^ flip] = total.astype(BF16)
    kept = lax.dot_general(pick, hidden_ref[...], dims, preferred_element_type=F32)
    kept_ref[...] = kept.astype(BF16)


def shards(
    queries,
    fresh_keys,
    fresh_values,
    key_cache,
    value_cache,
    lengths,
    block_table,
    resid,
    out_weight,
    norm_gain,
    gate_weight,
    up_weight,
    down_weight,
    row_order,
):
    ctx, ring, rest, grp = (lax.axis_size(axes) for axes in (CTX, RING, REST, GRP))
    team = lax.axis_size(TEAM)
    reqs, width = resid.shape
    slots = key_cache.shape[0]
    share = reqs // grp
    shape = jax.ShapeDtypeStruct
    blocks = gate_weight.shape[1] // (team * LANES)

    def passed(blocks_out):
        return [
            lax.ppermute(block, TEAM, [(i, i ^ flip) for i in range(team)])
            for flip, block in enumerate(blocks_out, 1)
        ]

    bundle = shape((3 * blocks + 2, LANES, LANES), BF16)
    mine, *given = call(
        functools.partial(cut_body, ring),
        (shape((2, LANES, LANES), BF16),) + (bundle,) * 3,
        [VMEM] * 5,
    )(gate_weight, up_weight, down_weight, resid, norm_gain.reshape(1, width))
    met = passed(given)
    met_out = lax.ppermute(out_weight, "core", [(0, 1), (1, 0)])
    meta, pick = call(
        functools.partial(prepare_body, ring),
        (shape((2 * slots,), jnp.int32), shape((reqs, reqs), BF16)),
        [SMEM] + [VMEM] * 2,
        out_specs=(SMEM, VMEM),
    )(lengths, block_table, row_order.reshape(1, reqs))

    my_queries = queries.reshape(2 * GROUP, HD)
    all_queries = exchange(jnp.broadcast_to(my_queries[None], (ring, 2 * GROUP, HD)), RING)
    all_queries = lax.all_gather(all_queries, "core", axis=0, tiled=False)
    scratch = [pltpu.VMEM((reqs, GROUP, LANES), F32)] * 3
    parts = call(attend_body, shape((ctx, 3 * GROUP, HD), BF16), [SMEM] + [VMEM] * 3, scratch)(
        meta, all_queries, key_cache, value_cache
    )
    parts = exchange(parts, CTX)
    parts, mine = lax.optimization_barrier((parts, mine))
    local = call(combine_body, shape((ring, 2 * GROUP, HD), BF16), [VMEM] * 4)(
        parts, my_queries, fresh_keys, fresh_values
    )
    attended = exchange(local, RING)
    projected = call(
        project_body,
        shape((grp, 2, reqs // 2, width), BF16),
        [VMEM] * 3,
        [pltpu.VMEM((ring * 2 * GROUP, HD), F32)],
    )(attended, out_weight, met_out)
    projected = exchange(projected.reshape(grp, reqs, width), GRP)
    pay = call(gather_body, shape((reqs, width), BF16), [VMEM])(projected)
    pay = lax.all_gather(pay, TEAM, axis=0, tiled=False)
    units = blocks * 8
    wide, hidden = call(
        widen_body,
        (shape((rest, 2 * units + 8, LANES), BF16), shape((reqs, width), BF16)),
        [VMEM] * 7,
    )(pay.reshape(team // 2, 2, 2, reqs // 2, width), mine, gate_weight, up_weight, *met)
    wide = exchange(wide, REST)
    active = call(
        functools.partial(activate_body, width * ctx), shape((rest, units, LANES), BF16), [VMEM]
    )(wide)
    active = exchange(active, REST)
    rows, kept = call(
        down_body,
        (shape((team, reqs, width), BF16), shape((reqs, width), BF16)),
        [VMEM] * 7,
    )(active, down_weight, *met, pick, hidden)
    rows = exchange(rows.reshape(team * grp, share, width), LAST)
    kept = lax.dynamic_index_in_dim(kept.reshape(grp, share, width), lax.axis_index(GRP), 0, False)
    return (kept.astype(F32) + jnp.sum(rows.astype(F32), axis=0)).astype(BF16)


def solution(mesh, sizes=(4, 2, 4, 2, 2, 4)):
    inner = Mesh(mesh.devices.reshape(sizes), ("yh", "yl", "zl", "core", "zh", "x"))
    in_specs = (
        P(CTX, GRP),
        P(CTX, GRP),
        P(CTX, GRP),
        P(CTX, None, GRP),
        P(CTX, None, GRP),
        P(),
        P(),
        P(None, CTX),
        P(GRP, CTX),
        P(CTX),
        P(CTX, GRP),
        P(CTX, GRP),
        P(GRP, CTX),
        P(),
    )
    out_specs = P(GRP, CTX)
    return jax.shard_map(shards, mesh=inner, in_specs=in_specs, out_specs=out_specs, check_vma=False)
```

```python
import functools

import jax
import jax.numpy as jnp
from jax import lax
from jax.experimental import pallas as pl
from jax.experimental.pallas import tpu as pltpu
from jax.sharding import Mesh
from jax.sharding import PartitionSpec as P

HD = 128
GROUP = 8
LANES = 128
EPS = 1e-05
NEG = -1e30
VMEM_LIMIT = 16 * 2**20
CTX = ("yh", "yl", "zl", "core")
RING = ("yh", "yl", "zl")
REST = ("yh", "zl")
TEAM = ("yl", "core")
GRP = ("zh", "x")
LAST = ("core",) + GRP
F32 = jnp.float32
BF16 = jnp.bfloat16
VMEM = pl.BlockSpec(memory_space=pltpu.VMEM)
SMEM = pl.BlockSpec(memory_space=pltpu.SMEM)
HBM = pl.BlockSpec(memory_space=pltpu.HBM)


def exchange(x, axes):
    return lax.all_to_all(x, axes, 0, 0, tiled=True)


def lane_ids(shape):
    return lax.broadcasted_iota(jnp.int32, shape, len(shape) - 1)


def call(body, out_shape, in_specs, scratch=(), out_specs=None):
    kernel = pl.pallas_call(
        body,
        out_shape=out_shape,
        in_specs=in_specs,
        out_specs=jax.tree.map(lambda _: VMEM, out_shape) if out_specs is None else out_specs,
        scratch_shapes=list(scratch),
        compiler_params=pltpu.CompilerParams(vmem_limit_bytes=VMEM_LIMIT),
    )

    def run(*operands):
        placed = [
            pltpu.with_memory_space_constraint(x, pltpu.HBM) if spec is HBM else x
            for x, spec in zip(operands, in_specs, strict=True)
        ]
        return kernel(*placed)

    return run


def request_of(place, ring):
    core, at = place >> ring.bit_length(), place & (2 * ring - 1)
    return (at >> 1) * 4 + core * 2 + (at & 1)


def pack_body(q_ref, out_ref, mine_ref):
    wide = q_ref[...].astype(F32)
    rows = [
        wide[r : r + 1, h * HD : (h + 1) * HD] for r in range(wide.shape[0]) for h in range(GROUP)
    ]
    rows = jnp.concatenate(rows, axis=0).astype(BF16)
    mine_ref[...] = rows
    for d in range(out_ref.shape[0]):
        out_ref[d] = rows


def prepare_body(
    ring, len_hbm, table_hbm, order_hbm, meta_ref, pick_ref, len_ref, table_ref, order_ref, sems
):
    pairs = ((table_hbm, table_ref), (len_hbm, len_ref), (order_hbm, order_ref))
    copies = [pltpu.make_async_copy(a, b, sems.at[i]) for i, (a, b) in enumerate(pairs)]
    for copy in copies:
        copy.start()
    for copy in copies:
        copy.wait()
    slots = meta_ref.shape[0] // 2
    first = lax.axis_index(CTX) * slots
    table = table_ref[...] - first
    rows, cols = table.shape
    code = lax.broadcasted_iota(jnp.int32, (rows, cols), 0) * cols + lane_ids((rows, cols))
    for s in range(slots):
        found = jnp.min(jnp.where(table == s, code, rows * cols - 1))
        owner = found // cols
        meta_ref[s] = owner
        meta_ref[slots + s] = len_ref[owner] - (found % cols) * LANES
    place = lax.broadcasted_iota(jnp.int32, pick_ref.shape, 0)
    pick = request_of(place, ring) == order_ref[...]
    pick_ref[...] = pick.astype(F32).astype(BF16)


def cut_body(ring, gate_ref, up_ref, down_ref, w_ref, resid_ref, gain_ref, mine, core_ref, *out_refs):
    me = lax.axis_index(TEAM)
    reqs = resid_ref.shape[0]
    place = lax.broadcasted_iota(jnp.int32, (reqs, reqs), 0)
    turn = (request_of(place, ring) == lane_ids((reqs, reqs))).astype(F32).astype(BF16)
    resid = jnp.dot(turn, resid_ref[...], preferred_element_type=F32).astype(BF16)
    gain = jnp.broadcast_to(gain_ref[...].astype(F32), (LANES, LANES)).astype(BF16)
    mine[0, :reqs] = resid
    mine[1] = gain
    blocks = (out_refs[0].shape[0] - 2) // 2
    heads = w_ref.shape[0] // LANES
    core_ref[:heads] = w_ref[...].reshape(heads, LANES, LANES)
    other = 1 - lax.axis_index("core")
    for z in range(2):
        start = pl.multiple_of((2 * z + other) * blocks * LANES, LANES)
        rows = down_ref[pl.ds(start, blocks * LANES), :]
        core_ref[heads + z * blocks : heads + (z + 1) * blocks] = rows.reshape(blocks, LANES, LANES)
    for flip, out_ref in enumerate(out_refs, 1):
        start = (me ^ flip) * blocks * LANES
        for b in range(blocks):
            cols = pl.ds(pl.multiple_of(start + b * LANES, LANES), LANES)
            out_ref[b] = gate_ref[:, cols]
            out_ref[blocks + b] = up_ref[:, cols]
        out_ref[2 * blocks, :reqs] = resid
        out_ref[2 * blocks + 1] = gain


def attend_body(meta_ref, q_ref, k_ref, v_hbm, out_ref, top_ref, sum_ref, acc_ref, v_ref, sem):
    slots, page = k_ref.shape[0], k_ref.shape[1]
    fetch = pltpu.make_async_copy(v_hbm, v_ref, sem)
    fetch.start()
    top_ref[...] = jnp.full(top_ref.shape, NEG, F32)
    sum_ref[...] = jnp.zeros(sum_ref.shape, F32)
    acc_ref[...] = jnp.zeros(acc_ref.shape, F32)
    lane = lane_ids((GROUP, page))
    owners, scores = [], []
    for s in range(slots):
        owner, live = meta_ref[s], meta_ref[slots + s]
        home = owner // 2
        pair = q_ref[home % 2, home // 2].astype(F32)
        q = jnp.where(owner % 2 == 1, pair[GROUP:], pair[:GROUP]).astype(BF16)
        score = lax.dot_general(q, k_ref[s], (((1,), (1,)), ((), ())), preferred_element_type=F32)
        score = jnp.where(lane < live, score * HD ** (-0.5), NEG)
        best = jnp.max(score, axis=1, keepdims=True)
        top_ref[owner] = jnp.maximum(top_ref[owner], jnp.broadcast_to(best, (GROUP, LANES)))
        owners.append(owner)
        scores.append(score)
    fetch.wait()
    for s in range(slots):
        owner = owners[s]
        shift = top_ref[owner].astype(BF16).astype(F32)
        weight = jnp.exp(scores[s] - shift)
        total = jnp.sum(weight, axis=1, keepdims=True)
        sum_ref[owner] = sum_ref[owner] + jnp.broadcast_to(total, (GROUP, LANES))
        acc_ref[owner] = acc_ref[owner] + jnp.dot(
            weight.astype(BF16), v_ref[s], preferred_element_type=F32
        )
    lane = lane_ids((GROUP, LANES))
    for d in range(out_ref.shape[0]):
        stats = jnp.zeros((GROUP, LANES), F32)
        for par in range(2):
            total = sum_ref[2 * d + par]
            high = total.astype(BF16).astype(F32)
            base = par * 64
            stats = jnp.where(lane == base, top_ref[2 * d + par], stats)
            stats = jnp.where(lane == base + 1, high, stats)
            stats = jnp.where(lane == base + 2, total - high, stats)
        block = jnp.concatenate([acc_ref[2 * d], acc_ref[2 * d + 1], stats], axis=0)
        out_ref[d] = block.astype(BF16)


def combine_body(part_ref, q_ref, fk_ref, fv_ref, out_ref):
    count = part_ref.shape[0]
    fk, fv = fk_ref[...].astype(F32), fv_ref[...].astype(F32)
    q = q_ref[...].astype(F32)
    done = []
    for par in range(2):
        base = par * 64
        mine = slice(par * GROUP, (par + 1) * GROUP)
        own = jnp.sum(q[mine] * fk[par : par + 1], axis=1, keepdims=True) * HD ** (-0.5)
        best = own
        for d in range(count):
            stats = part_ref[d].astype(F32)[2 * GROUP :]
            best = jnp.maximum(best, stats[:, base : base + 1])
        own_weight = jnp.exp(own - best)
        total = own_weight
        acc = own_weight.astype(BF16).astype(F32) * fv[par : par + 1]
        for d in range(count):
            block = part_ref[d].astype(F32)
            stats = block[2 * GROUP :]
            factor = jnp.exp(stats[:, base : base + 1] - best)
            total = total + factor * (stats[:, base + 1 : base + 2] + stats[:, base + 2 : base + 3])
            acc = acc + factor * block[mine]
        done.append(acc / total)
    rows = jnp.concatenate(done, axis=0).astype(BF16)
    for d in range(out_ref.shape[0]):
        out_ref[d] = rows


def project_body(att_ref, w_ref, met_ref, out_ref, rows_ref):
    core = lax.axis_index("core")
    count, per, _ = att_ref.shape
    rows_ref[...] = att_ref[...].astype(F32).reshape(count * per, HD)
    reqs = count * per // GROUP
    heads = [rows_ref[pl.ds(h, reqs, stride=GROUP), :].astype(BF16) for h in range(GROUP)]
    heads = jnp.concatenate(heads, axis=1)
    for at, ref in ((core, w_ref), (1 - core, met_ref)):
        w = ref[...] if ref is w_ref else ref[:GROUP].reshape(GROUP * HD, LANES)
        total = jnp.dot(heads, w, preferred_element_type=F32).astype(BF16)
        for g in range(out_ref.shape[0]):
            out_ref[g, at] = total


def gather_body(part_ref, out_ref):
    total = part_ref[0].astype(F32)
    for g in range(1, part_ref.shape[0]):
        total = total + part_ref[g].astype(F32)
    out_ref[...] = total.astype(BF16)


def widen_body(
    pay_ref, mine_ref, gate_ref, up_ref, met1_ref, met2_ref, met3_ref, out_ref, hidden_ref
):
    me = lax.axis_index(TEAM)
    team = 2 * pay_ref.shape[0]
    reqs = 2 * pay_ref.shape[3]
    mets = (met1_ref, met2_ref, met3_ref)
    blocks = (met1_ref.shape[0] - 2) // 2
    square = jnp.zeros((reqs, 1), F32)
    gained = []
    for flip in range(team):
        ref, at = (mine_ref, 0) if flip == 0 else (mets[flip - 1], 2 * blocks)
        owner = me ^ flip
        chip, core = owner // 2, owner % 2
        projected = jnp.concatenate([pay_ref[chip, c, core].astype(F32) for c in range(2)], axis=0)
        hidden = (ref[at, :reqs].astype(F32) + projected).astype(BF16)
        if flip == 0:
            hidden_ref[...] = hidden
        wide = hidden.astype(F32)
        square = square + jnp.sum(wide * wide, axis=1, keepdims=True)
        gained.append((wide * ref[at + 1, :reqs].astype(F32)).astype(BF16))
    gained = jnp.concatenate(gained, axis=1)
    tiles = []
    for b in range(2 * blocks):
        ref, at = (gate_ref, b) if b < blocks else (up_ref, b - blocks)
        cols = pl.ds(pl.multiple_of((me * blocks + at) * LANES, LANES), LANES)
        w = jnp.concatenate([ref[:, cols]] + [met_ref[b] for met_ref in mets], axis=0)
        x = jnp.dot(gained, w, preferred_element_type=F32)
        tiles.append(x.reshape(reqs // 8, 8, LANES))
    for i in range(blocks):
        out_ref[:, i * 16 : (i + 1) * 16, :] = jnp.concatenate(
            [tiles[2 * i], tiles[2 * i + 1]], axis=1
        ).astype(BF16)
    square = jnp.broadcast_to(square, (reqs, LANES))
    high = square.astype(BF16).astype(F32)
    lane = lane_ids(square.shape)
    square = jnp.where(lane == 0, high, jnp.where(lane == 1, square - high, 0.0))
    out_ref[:, blocks * 16 :, :] = square.reshape(reqs // 8, 8, LANES).astype(BF16)


def activate_body(width, part_ref, out_ref):
    total = part_ref[0].astype(F32)
    for d in range(1, part_ref.shape[0]):
        total = total + part_ref[d].astype(F32)
    units = (total.shape[0] - 8) // 2
    square = total[2 * units :]
    square = square[:, 0:1] + square[:, 1:2]
    inv_rms = lax.rsqrt(jnp.broadcast_to(square, (8, LANES)) / width + EPS)[None]
    gate = total[:units].reshape(units // 8, 8, LANES) * inv_rms
    up = total[units : 2 * units].reshape(units // 8, 8, LANES) * inv_rms
    active = (gate / (1.0 + jnp.exp(-gate)) * up).reshape(units, LANES).astype(BF16)
    for d in range(out_ref.shape[0]):
        out_ref[d] = active


def down_body(act_ref, w_ref, met_ref, pick_ref, hidden_ref, out_ref, kept_ref):
    core = lax.axis_index("core")
    reqs = act_ref.shape[0] * act_ref.shape[2] * 8
    blocks = act_ref.shape[3] // 8
    height = blocks * LANES
    acts, own = [], []
    for z in range(2):
        act = act_ref[:, z].astype(F32).reshape(reqs // 8, blocks * 8, LANES)
        for b in range(blocks):
            acts.append(act[:, b * 8 : b * 8 + 8].reshape(reqs, LANES).astype(BF16))
        own.append(w_ref[pl.ds(pl.multiple_of((2 * z + core) * height, LANES), height), :])
    acts = jnp.concatenate(acts, axis=1)
    met = met_ref[GROUP:].reshape(2 * height, LANES)
    pick = pick_ref[...]
    dims = (((0,), (0,)), ((), ()))
    for at, w in ((core, jnp.concatenate(own, axis=0)), (1 - core, met)):
        total = jnp.dot(acts, w, preferred_element_type=F32).astype(BF16)
        total = lax.dot_general(pick, total, dims, preferred_element_type=F32)
        out_ref[at] = total.astype(BF16)
    kept = lax.dot_general(pick, hidden_ref[...], dims, preferred_element_type=F32)
    kept_ref[...] = kept.astype(BF16)


def finish_body(part_ref, kept_ref, out_ref):
    total = kept_ref[lax.axis_index(GRP)].astype(F32)
    for d in range(part_ref.shape[0]):
        total = total + part_ref[d].astype(F32)
    out_ref[...] = total.astype(BF16)


def shards(
    queries,
    fresh_keys,
    fresh_values,
    key_cache,
    value_cache,
    lengths,
    block_table,
    resid,
    out_weight,
    norm_gain,
    gate_weight,
    up_weight,
    down_weight,
    row_order,
):
    ctx, ring, rest, grp = (lax.axis_size(axes) for axes in (CTX, RING, REST, GRP))
    team = lax.axis_size(TEAM)
    reqs, width = resid.shape
    slots = key_cache.shape[0]
    share = reqs // grp
    shape = jax.ShapeDtypeStruct
    blocks = gate_weight.shape[1] // (team * LANES)

    def passed(blocks_out):
        return [
            lax.ppermute(block, TEAM, [(i, i ^ flip) for i in range(team)])
            for flip, block in enumerate(blocks_out, 1)
        ]

    bundle = shape((2 * blocks + 2, LANES, LANES), BF16)
    core_bundle = shape((GROUP + 2 * blocks, LANES, LANES), BF16)
    mine, given_core, *given = call(
        functools.partial(cut_body, ring),
        (shape((2, LANES, LANES), BF16), core_bundle) + (bundle,) * 3,
        [VMEM] * 6,
    )(gate_weight, up_weight, down_weight, out_weight, resid, norm_gain.reshape(1, width))
    met = [
        lax.ppermute(block, TEAM, [(i, i ^ flip) for i in range(team)])
        for flip, block in enumerate(given, 1)
    ]
    met_core = lax.ppermute(given_core, "core", [(0, 1), (1, 0)])
    meta, pick = call(
        functools.partial(prepare_body, ring),
        (shape((2 * slots,), jnp.int32), shape((reqs, reqs), BF16)),
        [HBM] * 3,
        [
            pltpu.SMEM(lengths.shape, jnp.int32),
            pltpu.VMEM(block_table.shape, jnp.int32),
            pltpu.VMEM((1, reqs), jnp.int32),
            pltpu.SemaphoreType.DMA((3,)),
        ],
        out_specs=(SMEM, VMEM),
    )(lengths, block_table, row_order.reshape(1, reqs))

    packed, my_queries = call(
        pack_body, (shape((ring, 2 * GROUP, HD), BF16), shape((2 * GROUP, HD), BF16)), [VMEM]
    )(queries)
    all_queries = exchange(packed, RING)
    all_queries = lax.all_gather(all_queries, "core", axis=0, tiled=False)
    scratch = [pltpu.VMEM((reqs, GROUP, LANES), F32)] * 3
    scratch += [pltpu.VMEM(value_cache.shape, BF16), pltpu.SemaphoreType.DMA(())]
    parts = call(attend_body, shape((ctx, 3 * GROUP, HD), BF16), [SMEM, VMEM, VMEM, HBM], scratch)(
        meta, all_queries, key_cache, value_cache
    )
    parts = exchange(parts, CTX)
    parts, mine = lax.optimization_barrier((parts, mine))
    local = call(combine_body, shape((ring, 2 * GROUP, HD), BF16), [VMEM] * 4)(
        parts, my_queries, fresh_keys, fresh_values
    )
    attended = exchange(local, RING)
    attended, met_core, *met = lax.optimization_barrier((attended, met_core, *met))
    projected = call(
        project_body,
        shape((grp, 2, reqs // 2, width), BF16),
        [VMEM] * 3,
        [pltpu.VMEM((ring * 2 * GROUP, HD), F32)],
    )(attended, out_weight, met_core)
    projected = exchange(projected.reshape(grp, reqs, width), GRP)
    pay = call(gather_body, shape((reqs, width), BF16), [VMEM])(projected)
    pay = lax.all_gather(pay, TEAM, axis=0, tiled=False)
    units = blocks * 8
    wide, hidden = call(
        widen_body,
        (shape((rest, 2 * units + 8, LANES), BF16), shape((reqs, width), BF16)),
        [VMEM] * 7,
    )(pay.reshape(team // 2, 2, 2, reqs // 2, width), mine, gate_weight, up_weight, *met)
    wide = exchange(wide, REST)
    active = call(
        functools.partial(activate_body, width * ctx), shape((ring, units, LANES), BF16), [VMEM]
    )(wide)
    active = exchange(active, RING)
    line = lax.axis_size("zl")
    rows, kept = call(
        down_body,
        (shape((2, reqs, width), BF16), shape((reqs, width), BF16)),
        [VMEM] * 5,
    )(active.reshape(ring // (2 * line), 2, line, units, LANES), down_weight, met_core, pick, hidden)
    rows = exchange(rows.reshape(2 * grp, share, width), LAST)
    return call(finish_body, shape((share, width), BF16), [VMEM] * 2)(
        rows, kept.reshape(grp, share, width)
    )


def solution(mesh, sizes=(4, 2, 4, 2, 2, 4)):
    inner = Mesh(mesh.devices.reshape(sizes), ("yh", "yl", "zl", "core", "zh", "x"))
    in_specs = (
        P(CTX, GRP),
        P(CTX, GRP),
        P(CTX, GRP),
        P(CTX, None, GRP),
        P(CTX, None, GRP),
        P(),
        P(),
        P(None, CTX),
        P(GRP, CTX),
        P(CTX),
        P(CTX, GRP),
        P(CTX, GRP),
        P(GRP, CTX),
        P(),
    )
    out_specs = P(GRP, CTX)
    return jax.shard_map(shards, mesh=inner, in_specs=in_specs, out_specs=out_specs, check_vma=False)
```

```python
import functools

import jax
import jax.numpy as jnp
from jax import lax
from jax.experimental import pallas as pl
from jax.experimental.pallas import tpu as pltpu
from jax.sharding import Mesh
from jax.sharding import PartitionSpec as P

HD = 128
GROUP = 8
LANES = 128
EPS = 1e-05
CHUNKS = 6
NEG = -1e30
VMEM_LIMIT = 16 * 2**20
CTX = ("yh", "yl", "zl", "core")
RING = ("yh", "yl", "zl")
REST = ("yh", "zl")
TEAM = ("yl", "core")
GRP = ("zh", "x")
LAST = ("core",) + GRP
F32 = jnp.float32
BF16 = jnp.bfloat16
VMEM = pl.BlockSpec(memory_space=pltpu.VMEM)
SMEM = pl.BlockSpec(memory_space=pltpu.SMEM)
HBM = pl.BlockSpec(memory_space=pltpu.HBM)


def exchange(x, axes):
    return lax.all_to_all(x, axes, 0, 0, tiled=True)


def lane_ids(shape):
    return lax.broadcasted_iota(jnp.int32, shape, len(shape) - 1)


def call(body, out_shape, in_specs, scratch=(), out_specs=None):
    kernel = pl.pallas_call(
        body,
        out_shape=out_shape,
        in_specs=in_specs,
        out_specs=jax.tree.map(lambda _: VMEM, out_shape) if out_specs is None else out_specs,
        scratch_shapes=list(scratch),
        compiler_params=pltpu.CompilerParams(vmem_limit_bytes=VMEM_LIMIT),
    )

    def run(*operands):
        placed = [
            pltpu.with_memory_space_constraint(x, pltpu.HBM) if spec is HBM else x
            for x, spec in zip(operands, in_specs, strict=True)
        ]
        return kernel(*placed)

    return run


def request_of(place, ring):
    core, at = place >> ring.bit_length(), place & (2 * ring - 1)
    return (at >> 1) * 4 + core * 2 + (at & 1)


def pack_body(q_ref, out_ref, mine_ref):
    wide = q_ref[...].astype(F32)
    rows = [
        wide[r : r + 1, h * HD : (h + 1) * HD] for r in range(wide.shape[0]) for h in range(GROUP)
    ]
    rows = jnp.concatenate(rows, axis=0).astype(BF16)
    mine_ref[...] = rows
    for d in range(out_ref.shape[0]):
        out_ref[d] = rows


def prepare_body(len_hbm, table_hbm, meta_ref, len_ref, table_ref, sems):
    pairs = ((table_hbm, table_ref), (len_hbm, len_ref))
    copies = [pltpu.make_async_copy(a, b, sems.at[i]) for i, (a, b) in enumerate(pairs)]
    for copy in copies:
        copy.start()
    for copy in copies:
        copy.wait()
    slots = meta_ref.shape[0] // 2
    first = lax.axis_index(CTX) * slots
    table = table_ref[...] - first
    rows, cols = table.shape
    code = lax.broadcasted_iota(jnp.int32, (rows, cols), 0) * cols + lane_ids((rows, cols))
    for s in range(slots):
        found = jnp.min(jnp.where(table == s, code, rows * cols - 1))
        owner = found // cols
        meta_ref[s] = owner
        meta_ref[slots + s] = len_ref[owner] - (found % cols) * LANES


def cut_body(ring, gate_ref, up_ref, down_ref, w_ref, resid_ref, gain_ref, mine, core_ref, *out_refs):
    me = lax.axis_index(TEAM)
    reqs = resid_ref.shape[0]
    place = lax.broadcasted_iota(jnp.int32, (reqs, reqs), 0)
    turn = (request_of(place, ring) == lane_ids((reqs, reqs))).astype(F32).astype(BF16)
    resid = jnp.dot(turn, resid_ref[...], preferred_element_type=F32).astype(BF16)
    gain = jnp.broadcast_to(gain_ref[...].astype(F32), (LANES, LANES)).astype(BF16)
    mine[0, :reqs] = resid
    mine[1] = gain
    blocks = (out_refs[0].shape[0] - 2) // 2
    heads = w_ref.shape[0] // LANES
    core_ref[:heads] = w_ref[...].reshape(heads, LANES, LANES)
    other = 1 - lax.axis_index("core")
    for z in range(2):
        start = pl.multiple_of((2 * z + other) * blocks * LANES, LANES)
        rows = down_ref[pl.ds(start, blocks * LANES), :]
        core_ref[heads + z * blocks : heads + (z + 1) * blocks] = rows.reshape(blocks, LANES, LANES)
    for flip, out_ref in enumerate(out_refs, 1):
        start = (me ^ flip) * blocks * LANES
        for b in range(blocks):
            cols = pl.ds(pl.multiple_of(start + b * LANES, LANES), LANES)
            out_ref[b] = gate_ref[:, cols]
            out_ref[blocks + b] = up_ref[:, cols]
        out_ref[2 * blocks, :reqs] = resid
        out_ref[2 * blocks + 1] = gain


def attend_body(
    meta_ref, q_ref, k_hbm, v_hbm, out_ref, top_ref, sum_ref, acc_ref, k_ref, v_ref, sems
):
    slots, page = k_ref.shape[0], k_ref.shape[1]
    part = slots // CHUNKS
    fetches = [
        [
            pltpu.make_async_copy(a.at[pl.ds(i * part, part)], b.at[pl.ds(i * part, part)], sems.at[w, i])
            for i in range(CHUNKS)
        ]
        for w, (a, b) in enumerate(((k_hbm, k_ref), (v_hbm, v_ref)))
    ]
    for fetch in fetches[0] + fetches[1]:
        fetch.start()
    top_ref[...] = jnp.full(top_ref.shape, NEG, F32)
    sum_ref[...] = jnp.zeros(sum_ref.shape, F32)
    acc_ref[...] = jnp.zeros(acc_ref.shape, F32)
    lane = lane_ids((GROUP, page))
    owners, scores = [], []
    for s in range(slots):
        if s % part == 0:
            fetches[0][s // part].wait()
        owner, live = meta_ref[s], meta_ref[slots + s]
        home = owner // 2
        pair = q_ref[home % 2, home // 2].astype(F32)
        q = jnp.where(owner % 2 == 1, pair[GROUP:], pair[:GROUP]).astype(BF16)
        score = lax.dot_general(q, k_ref[s], (((1,), (1,)), ((), ())), preferred_element_type=F32)
        score = jnp.where(lane < live, score * HD ** (-0.5), NEG)
        best = jnp.max(score, axis=1, keepdims=True)
        top_ref[owner] = jnp.maximum(top_ref[owner], jnp.broadcast_to(best, (GROUP, LANES)))
        owners.append(owner)
        scores.append(score)
    for s in range(slots):
        if s % part == 0:
            fetches[1][s // part].wait()
        owner = owners[s]
        shift = top_ref[owner].astype(BF16).astype(F32)
        weight = jnp.exp(scores[s] - shift)
        total = jnp.sum(weight, axis=1, keepdims=True)
        sum_ref[owner] = sum_ref[owner] + jnp.broadcast_to(total, (GROUP, LANES))
        acc_ref[owner] = acc_ref[owner] + jnp.dot(
            weight.astype(BF16), v_ref[s], preferred_element_type=F32
        )
    lane = lane_ids((GROUP, LANES))
    for d in range(out_ref.shape[0]):
        stats = jnp.zeros((GROUP, LANES), F32)
        for par in range(2):
            total = sum_ref[2 * d + par]
            high = total.astype(BF16).astype(F32)
            base = par * 64
            stats = jnp.where(lane == base, top_ref[2 * d + par], stats)
            stats = jnp.where(lane == base + 1, high, stats)
            stats = jnp.where(lane == base + 2, total - high, stats)
        block = jnp.concatenate([acc_ref[2 * d], acc_ref[2 * d + 1], stats], axis=0)
        out_ref[d] = block.astype(BF16)


def combine_body(part_ref, q_ref, fk_hbm, fv_hbm, out_ref, fk_ref, fv_ref, sems):
    fetches = [
        pltpu.make_async_copy(fk_hbm, fk_ref, sems.at[0]),
        pltpu.make_async_copy(fv_hbm, fv_ref, sems.at[1]),
    ]
    for fetch in fetches:
        fetch.start()
    count = part_ref.shape[0]
    best = jnp.full((GROUP, LANES), NEG, F32)
    for d in range(count):
        best = jnp.maximum(best, part_ref[d].astype(F32)[2 * GROUP :])
    for fetch in fetches:
        fetch.wait()
    fk, fv = fk_ref[...].astype(F32), fv_ref[...].astype(F32)
    q = q_ref[...].astype(F32)
    tops, totals, accs = [], [], []
    for par in range(2):
        mine = slice(par * GROUP, (par + 1) * GROUP)
        own = jnp.sum(q[mine] * fk[par : par + 1], axis=1, keepdims=True) * HD ** (-0.5)
        top = jnp.maximum(best[:, par * 64 : par * 64 + 1], own)
        own_weight = jnp.exp(own - top)
        tops.append(top)
        totals.append(own_weight)
        accs.append(own_weight.astype(BF16).astype(F32) * fv[par : par + 1])
    for d in range(count):
        block = part_ref[d].astype(F32)
        stats = block[2 * GROUP :]
        for par in range(2):
            base = par * 64
            factor = jnp.exp(stats[:, base : base + 1] - tops[par])
            total = stats[:, base + 1 : base + 2] + stats[:, base + 2 : base + 3]
            totals[par] = totals[par] + factor * total
            accs[par] = accs[par] + factor * block[par * GROUP : (par + 1) * GROUP]
    rows = jnp.concatenate([accs[par] / totals[par] for par in range(2)], axis=0).astype(BF16)
    for d in range(out_ref.shape[0]):
        out_ref[d] = rows


def project_body(att_ref, w_hbm, met_ref, out_ref, rows_ref, w_ref, sem):
    fetch = pltpu.make_async_copy(w_hbm, w_ref, sem)
    fetch.start()
    core = lax.axis_index("core")
    count, per, _ = att_ref.shape
    rows_ref[...] = att_ref[...].astype(F32).reshape(count * per, HD)
    reqs = count * per // GROUP
    heads = [rows_ref[pl.ds(h, reqs, stride=GROUP), :].astype(BF16) for h in range(GROUP)]
    heads = jnp.concatenate(heads, axis=1)
    for at, ref in ((1 - core, met_ref), (core, w_ref)):
        if ref is w_ref:
            fetch.wait()
        w = ref[...] if ref is w_ref else ref[:GROUP].reshape(GROUP * HD, LANES)
        total = jnp.dot(heads, w, preferred_element_type=F32).astype(BF16)
        for g in range(out_ref.shape[0]):
            out_ref[g, at] = total


def gather_body(part_ref, out_ref):
    total = part_ref[0].astype(F32)
    for g in range(1, part_ref.shape[0]):
        total = total + part_ref[g].astype(F32)
    out_ref[...] = total.astype(BF16)


def widen_body(
    pay_ref, mine_ref, gate_ref, up_ref, met1_ref, met2_ref, met3_ref, out_ref, hidden_ref
):
    me = lax.axis_index(TEAM)
    team = 2 * pay_ref.shape[0]
    reqs = 2 * pay_ref.shape[3]
    mets = (met1_ref, met2_ref, met3_ref)
    blocks = (met1_ref.shape[0] - 2) // 2
    square = jnp.zeros((reqs, 1), F32)
    gained = []
    for flip in range(team):
        ref, at = (mine_ref, 0) if flip == 0 else (mets[flip - 1], 2 * blocks)
        owner = me ^ flip
        chip, core = owner // 2, owner % 2
        projected = jnp.concatenate([pay_ref[chip, c, core].astype(F32) for c in range(2)], axis=0)
        hidden = (ref[at, :reqs].astype(F32) + projected).astype(BF16)
        if flip == 0:
            hidden_ref[...] = hidden
        wide = hidden.astype(F32)
        square = square + jnp.sum(wide * wide, axis=1, keepdims=True)
        gained.append((wide * ref[at + 1, :reqs].astype(F32)).astype(BF16))
    gained = jnp.concatenate(gained, axis=1)
    tiles = []
    for b in range(2 * blocks):
        ref, at = (gate_ref, b) if b < blocks else (up_ref, b - blocks)
        cols = pl.ds(pl.multiple_of((me * blocks + at) * LANES, LANES), LANES)
        w = jnp.concatenate([ref[:, cols]] + [met_ref[b] for met_ref in mets], axis=0)
        x = jnp.dot(gained, w, preferred_element_type=F32)
        tiles.append(x.reshape(reqs // 8, 8, LANES))
    for i in range(blocks):
        out_ref[:, i * 16 : (i + 1) * 16, :] = jnp.concatenate(
            [tiles[2 * i], tiles[2 * i + 1]], axis=1
        ).astype(BF16)
    square = jnp.broadcast_to(square, (reqs, LANES))
    high = square.astype(BF16).astype(F32)
    lane = lane_ids(square.shape)
    square = jnp.where(lane == 0, high, jnp.where(lane == 1, square - high, 0.0))
    out_ref[:, blocks * 16 :, :] = square.reshape(reqs // 8, 8, LANES).astype(BF16)


def activate_body(width, part_ref, out_ref):
    total = part_ref[0].astype(F32)
    for d in range(1, part_ref.shape[0]):
        total = total + part_ref[d].astype(F32)
    units = (total.shape[0] - 8) // 2
    square = total[2 * units :]
    square = square[:, 0:1] + square[:, 1:2]
    inv_rms = lax.rsqrt(jnp.broadcast_to(square, (8, LANES)) / width + EPS)[None]
    gate = total[:units].reshape(units // 8, 8, LANES) * inv_rms
    up = total[units : 2 * units].reshape(units // 8, 8, LANES) * inv_rms
    active = (gate / (1.0 + jnp.exp(-gate)) * up).reshape(units, LANES).astype(BF16)
    for d in range(out_ref.shape[0]):
        out_ref[d] = active


def down_body(
    ring, act_ref, w_ref, met_ref, hidden_ref, order_hbm, out_ref, kept_ref, order_ref, sem
):
    fetch = pltpu.make_async_copy(order_hbm, order_ref, sem)
    fetch.start()
    core = lax.axis_index("core")
    reqs = act_ref.shape[0] * act_ref.shape[2] * 8
    blocks = act_ref.shape[3] // 8
    height = blocks * LANES
    acts, own = [], []
    for z in range(2):
        act = act_ref[:, z].astype(F32).reshape(reqs // 8, blocks * 8, LANES)
        for b in range(blocks):
            acts.append(act[:, b * 8 : b * 8 + 8].reshape(reqs, LANES).astype(BF16))
        own.append(w_ref[pl.ds(pl.multiple_of((2 * z + core) * height, LANES), height), :])
    acts = jnp.concatenate(acts, axis=1)
    met = met_ref[GROUP:].reshape(2 * height, LANES)
    totals = [
        jnp.dot(acts, w, preferred_element_type=F32).astype(BF16)
        for w in (jnp.concatenate(own, axis=0), met)
    ]
    fetch.wait()
    place = lax.broadcasted_iota(jnp.int32, (reqs, reqs), 0)
    pick = (request_of(place, ring) == order_ref[...]).astype(F32).astype(BF16)
    dims = (((0,), (0,)), ((), ()))
    for at, total in ((core, totals[0]), (1 - core, totals[1])):
        total = lax.dot_general(pick, total, dims, preferred_element_type=F32)
        out_ref[at] = total.astype(BF16)
    kept = lax.dot_general(pick, hidden_ref[...], dims, preferred_element_type=F32)
    kept_ref[...] = kept.astype(BF16)


def finish_body(part_ref, kept_ref, out_ref):
    total = kept_ref[lax.axis_index(GRP)].astype(F32)
    for d in range(part_ref.shape[0]):
        total = total + part_ref[d].astype(F32)
    out_ref[...] = total.astype(BF16)


def shards(
    queries,
    fresh_keys,
    fresh_values,
    key_cache,
    value_cache,
    lengths,
    block_table,
    resid,
    out_weight,
    norm_gain,
    gate_weight,
    up_weight,
    down_weight,
    row_order,
):
    ctx, ring, rest, grp = (lax.axis_size(axes) for axes in (CTX, RING, REST, GRP))
    team = lax.axis_size(TEAM)
    reqs, width = resid.shape
    slots = key_cache.shape[0]
    share = reqs // grp
    shape = jax.ShapeDtypeStruct
    blocks = gate_weight.shape[1] // (team * LANES)

    def passed(blocks_out):
        return [
            lax.ppermute(block, TEAM, [(i, i ^ flip) for i in range(team)])
            for flip, block in enumerate(blocks_out, 1)
        ]

    bundle = shape((2 * blocks + 2, LANES, LANES), BF16)
    core_bundle = shape((GROUP + 2 * blocks, LANES, LANES), BF16)
    mine, given_core, *given = call(
        functools.partial(cut_body, ring),
        (shape((2, LANES, LANES), BF16), core_bundle) + (bundle,) * 3,
        [VMEM] * 6,
    )(gate_weight, up_weight, down_weight, out_weight, resid, norm_gain.reshape(1, width))
    met = [
        lax.ppermute(block, TEAM, [(i, i ^ flip) for i in range(team)])
        for flip, block in enumerate(given, 1)
    ]
    met_core = lax.ppermute(given_core, "core", [(0, 1), (1, 0)])
    meta = call(
        prepare_body,
        shape((2 * slots,), jnp.int32),
        [HBM] * 2,
        [
            pltpu.SMEM(lengths.shape, jnp.int32),
            pltpu.VMEM(block_table.shape, jnp.int32),
            pltpu.SemaphoreType.DMA((2,)),
        ],
        out_specs=SMEM,
    )(lengths, block_table)

    packed, my_queries = call(
        pack_body, (shape((ring, 2 * GROUP, HD), BF16), shape((2 * GROUP, HD), BF16)), [VMEM]
    )(queries)
    all_queries = exchange(packed, RING)
    all_queries = lax.all_gather(all_queries, "core", axis=0, tiled=False)
    scratch = [pltpu.VMEM((reqs, GROUP, LANES), F32)] * 3
    scratch += [pltpu.VMEM(value_cache.shape, BF16)] * 2 + [pltpu.SemaphoreType.DMA((2, CHUNKS))]
    parts = call(attend_body, shape((ctx, 3 * GROUP, HD), BF16), [SMEM, VMEM, HBM, HBM], scratch)(
        meta, all_queries, key_cache, value_cache
    )
    parts = exchange(parts, CTX)
    parts, mine = lax.optimization_barrier((parts, mine))
    scratch = [pltpu.VMEM(fresh_keys.shape, BF16)] * 2 + [pltpu.SemaphoreType.DMA((2,))]
    local = call(
        combine_body, shape((ring, 2 * GROUP, HD), BF16), [VMEM, VMEM, HBM, HBM], scratch
    )(
        parts, my_queries, fresh_keys, fresh_values
    )
    local, met_core = lax.optimization_barrier((local, met_core))
    attended = exchange(local, RING)
    projected = call(
        project_body,
        shape((grp, 2, reqs // 2, width), BF16),
        [VMEM, HBM, VMEM],
        [
            pltpu.VMEM((ring * 2 * GROUP, HD), F32),
            pltpu.VMEM(out_weight.shape, BF16),
            pltpu.SemaphoreType.DMA(()),
        ],
    )(attended, out_weight, met_core)
    projected = exchange(projected.reshape(grp, reqs, width), GRP)
    pay = call(gather_body, shape((reqs, width), BF16), [VMEM])(projected)
    pay = lax.all_gather(pay, TEAM, axis=0, tiled=False)
    units = blocks * 8
    wide, hidden = call(
        widen_body,
        (shape((rest, 2 * units + 8, LANES), BF16), shape((reqs, width), BF16)),
        [VMEM] * 7,
    )(pay.reshape(team // 2, 2, 2, reqs // 2, width), mine, gate_weight, up_weight, *met)
    wide = exchange(wide, REST)
    active = call(
        functools.partial(activate_body, width * ctx), shape((ring, units, LANES), BF16), [VMEM]
    )(wide)
    active = exchange(active, RING)
    line = lax.axis_size("zl")
    rows, kept = call(
        functools.partial(down_body, ring),
        (shape((2, reqs, width), BF16), shape((reqs, width), BF16)),
        [VMEM] * 4 + [HBM],
        [pltpu.VMEM((1, reqs), jnp.int32), pltpu.SemaphoreType.DMA(())],
    )(
        active.reshape(ring // (2 * line), 2, line, units, LANES),
        down_weight,
        met_core,
        hidden,
        row_order.reshape(1, reqs),
    )
    rows = exchange(rows.reshape(2 * grp, share, width), LAST)
    return call(finish_body, shape((share, width), BF16), [VMEM] * 2)(
        rows, kept.reshape(grp, share, width)
    )


def solution(mesh, sizes=(4, 2, 4, 2, 2, 4)):
    inner = Mesh(mesh.devices.reshape(sizes), ("yh", "yl", "zl", "core", "zh", "x"))
    in_specs = (
        P(CTX, GRP),
        P(CTX, GRP),
        P(CTX, GRP),
        P(CTX, None, GRP),
        P(CTX, None, GRP),
        P(),
        P(),
        P(None, CTX),
        P(GRP, CTX),
        P(CTX),
        P(CTX, GRP),
        P(CTX, GRP),
        P(GRP, CTX),
        P(),
    )
    out_specs = P(GRP, CTX)
    return jax.shard_map(shards, mesh=inner, in_specs=in_specs, out_specs=out_specs, check_vma=False)
```

```python
import functools

import jax
import jax.numpy as jnp
from jax import lax
from jax.experimental import pallas as pl
from jax.experimental.pallas import tpu as pltpu
from jax.sharding import Mesh
from jax.sharding import PartitionSpec as P

HD = 128
GROUP = 8
LANES = 128
EPS = 1e-05
NEG = -1e30
VMEM_LIMIT = 16 * 2**20
CTX = ("yh", "yl", "zl", "core")
RING = ("yh", "yl", "zl")
REST = ("yh", "zl")
TEAM = ("yl", "core")
GRP = ("zh", "x")
LAST = ("core",) + GRP
F32 = jnp.float32
BF16 = jnp.bfloat16
VMEM = pl.BlockSpec(memory_space=pltpu.VMEM)
SMEM = pl.BlockSpec(memory_space=pltpu.SMEM)
HBM = pl.BlockSpec(memory_space=pltpu.HBM)


def exchange(x, axes):
    return lax.all_to_all(x, axes, 0, 0, tiled=True)


def lane_ids(shape):
    return lax.broadcasted_iota(jnp.int32, shape, len(shape) - 1)


def call(body, out_shape, in_specs, scratch=(), out_specs=None):
    kernel = pl.pallas_call(
        body,
        out_shape=out_shape,
        in_specs=in_specs,
        out_specs=jax.tree.map(lambda _: VMEM, out_shape) if out_specs is None else out_specs,
        scratch_shapes=list(scratch),
        compiler_params=pltpu.CompilerParams(vmem_limit_bytes=VMEM_LIMIT),
    )

    def run(*operands):
        placed = [
            pltpu.with_memory_space_constraint(x, pltpu.HBM) if spec is HBM else x
            for x, spec in zip(operands, in_specs, strict=True)
        ]
        return kernel(*placed)

    return run


def request_of(place, ring):
    core, at = place >> ring.bit_length(), place & (2 * ring - 1)
    return (at >> 1) * 4 + core * 2 + (at & 1)


def pack_body(q_ref, out_ref, mine_ref):
    wide = q_ref[...].astype(F32)
    rows = [
        wide[r : r + 1, h * HD : (h + 1) * HD] for r in range(wide.shape[0]) for h in range(GROUP)
    ]
    rows = jnp.concatenate(rows, axis=0).astype(BF16)
    mine_ref[...] = rows
    for d in range(out_ref.shape[0]):
        out_ref[d] = rows


def prepare_body(len_hbm, table_hbm, meta_ref, len_ref, table_ref, sems):
    pairs = ((table_hbm, table_ref), (len_hbm, len_ref))
    copies = [pltpu.make_async_copy(a, b, sems.at[i]) for i, (a, b) in enumerate(pairs)]
    for copy in copies:
        copy.start()
    for copy in copies:
        copy.wait()
    slots = meta_ref.shape[0] // 2
    first = lax.axis_index(CTX) * slots
    table = table_ref[...] - first
    rows, cols = table.shape
    code = lax.broadcasted_iota(jnp.int32, (rows, cols), 0) * cols + lane_ids((rows, cols))
    for s in range(slots):
        found = jnp.min(jnp.where(table == s, code, rows * cols - 1))
        owner = found // cols
        meta_ref[s] = owner
        meta_ref[slots + s] = len_ref[owner] - (found % cols) * LANES


def cut_body(ring, gate_ref, up_ref, down_ref, resid_ref, gain_ref, mine, core_ref, *out_refs):
    me = lax.axis_index(TEAM)
    reqs = resid_ref.shape[0]
    place = lax.broadcasted_iota(jnp.int32, (reqs, reqs), 0)
    turn = (request_of(place, ring) == lane_ids((reqs, reqs))).astype(F32).astype(BF16)
    resid = jnp.dot(turn, resid_ref[...], preferred_element_type=F32).astype(BF16)
    gain = jnp.broadcast_to(gain_ref[...].astype(F32), (LANES, LANES)).astype(BF16)
    mine[0, :reqs] = resid
    mine[1] = gain
    blocks = (out_refs[0].shape[0] - 2) // 2
    other = 1 - lax.axis_index("core")
    for z in range(2):
        start = pl.multiple_of((2 * z + other) * blocks * LANES, LANES)
        rows = down_ref[pl.ds(start, blocks * LANES), :]
        core_ref[z * blocks : (z + 1) * blocks] = rows.reshape(blocks, LANES, LANES)
    for flip, out_ref in enumerate(out_refs, 1):
        start = (me ^ flip) * blocks * LANES
        for b in range(blocks):
            cols = pl.ds(pl.multiple_of(start + b * LANES, LANES), LANES)
            out_ref[b] = gate_ref[:, cols]
            out_ref[blocks + b] = up_ref[:, cols]
        out_ref[2 * blocks, :reqs] = resid
        out_ref[2 * blocks + 1] = gain


def attend_body(meta_ref, q_ref, k_ref, v_ref, out_ref, top_ref, sum_ref, acc_ref):
    slots, page = k_ref.shape[0], k_ref.shape[1]
    top_ref[...] = jnp.full(top_ref.shape, NEG, F32)
    sum_ref[...] = jnp.zeros(sum_ref.shape, F32)
    acc_ref[...] = jnp.zeros(acc_ref.shape, F32)
    lane = lane_ids((GROUP, page))
    owners, scores = [], []
    for s in range(slots):
        owner, live = meta_ref[s], meta_ref[slots + s]
        home = owner // 2
        pair = q_ref[home % 2, home // 2].astype(F32)
        q = jnp.where(owner % 2 == 1, pair[GROUP:], pair[:GROUP]).astype(BF16)
        score = lax.dot_general(q, k_ref[s], (((1,), (1,)), ((), ())), preferred_element_type=F32)
        score = jnp.where(lane < live, score * HD ** (-0.5), NEG)
        best = jnp.max(score, axis=1, keepdims=True)
        top_ref[owner] = jnp.maximum(top_ref[owner], jnp.broadcast_to(best, (GROUP, LANES)))
        owners.append(owner)
        scores.append(score)
    for s in range(slots):
        owner = owners[s]
        shift = top_ref[owner].astype(BF16).astype(F32)
        weight = jnp.exp(scores[s] - shift)
        total = jnp.sum(weight, axis=1, keepdims=True)
        sum_ref[owner] = sum_ref[owner] + jnp.broadcast_to(total, (GROUP, LANES))
        acc_ref[owner] = acc_ref[owner] + jnp.dot(
            weight.astype(BF16), v_ref[s], preferred_element_type=F32
        )
    lane = lane_ids((GROUP, LANES))
    for d in range(out_ref.shape[0]):
        stats = jnp.zeros((GROUP, LANES), F32)
        for par in range(2):
            total = sum_ref[2 * d + par]
            high = total.astype(BF16).astype(F32)
            base = par * 64
            stats = jnp.where(lane == base, top_ref[2 * d + par], stats)
            stats = jnp.where(lane == base + 1, high, stats)
            stats = jnp.where(lane == base + 2, total - high, stats)
        block = jnp.concatenate([acc_ref[2 * d], acc_ref[2 * d + 1], stats], axis=0)
        out_ref[d] = block.astype(BF16)


def combine_body(part_ref, q_ref, fk_ref, fv_ref, out_ref):
    count = part_ref.shape[0]
    best = jnp.full((GROUP, LANES), NEG, F32)
    for d in range(count):
        best = jnp.maximum(best, part_ref[d].astype(F32)[2 * GROUP :])
    fk, fv = fk_ref[...].astype(F32), fv_ref[...].astype(F32)
    q = q_ref[...].astype(F32)
    tops, totals, accs = [], [], []
    for par in range(2):
        mine = slice(par * GROUP, (par + 1) * GROUP)
        own = jnp.sum(q[mine] * fk[par : par + 1], axis=1, keepdims=True) * HD ** (-0.5)
        top = jnp.maximum(best[:, par * 64 : par * 64 + 1], own)
        own_weight = jnp.exp(own - top)
        tops.append(top)
        totals.append(own_weight)
        accs.append(own_weight.astype(BF16).astype(F32) * fv[par : par + 1])
    for d in range(count):
        block = part_ref[d].astype(F32)
        stats = block[2 * GROUP :]
        for par in range(2):
            base = par * 64
            factor = jnp.exp(stats[:, base : base + 1] - tops[par])
            total = stats[:, base + 1 : base + 2] + stats[:, base + 2 : base + 3]
            totals[par] = totals[par] + factor * total
            accs[par] = accs[par] + factor * block[par * GROUP : (par + 1) * GROUP]
    rows = jnp.concatenate([accs[par] / totals[par] for par in range(2)], axis=0).astype(BF16)
    for d in range(out_ref.shape[0]):
        out_ref[d] = rows


def project_body(att_ref, w_ref, met_ref, out_ref, rows_ref):
    core = lax.axis_index("core")
    count, per, _ = att_ref.shape
    rows_ref[...] = att_ref[...].astype(F32).reshape(count * per, HD)
    reqs = count * per // GROUP
    heads = [rows_ref[pl.ds(h, reqs, stride=GROUP), :].astype(BF16) for h in range(GROUP)]
    heads = jnp.concatenate(heads, axis=1)
    for at, ref in ((core, w_ref), (1 - core, met_ref)):
        total = jnp.dot(heads, ref[...], preferred_element_type=F32).astype(BF16)
        for g in range(out_ref.shape[0]):
            out_ref[g, at] = total


def gather_body(part_ref, out_ref):
    total = part_ref[0].astype(F32)
    for g in range(1, part_ref.shape[0]):
        total = total + part_ref[g].astype(F32)
    out_ref[...] = total.astype(BF16)


def widen_body(
    pay_ref, mine_ref, gate_ref, up_ref, met1_ref, met2_ref, met3_ref, out_ref, hidden_ref
):
    me = lax.axis_index(TEAM)
    team = 2 * pay_ref.shape[0]
    reqs = 2 * pay_ref.shape[3]
    mets = (met1_ref, met2_ref, met3_ref)
    blocks = (met1_ref.shape[0] - 2) // 2
    square = jnp.zeros((reqs, 1), F32)
    gained = []
    for flip in range(team):
        ref, at = (mine_ref, 0) if flip == 0 else (mets[flip - 1], 2 * blocks)
        owner = me ^ flip
        chip, core = owner // 2, owner % 2
        projected = jnp.concatenate([pay_ref[chip, c, core].astype(F32) for c in range(2)], axis=0)
        hidden = (ref[at, :reqs].astype(F32) + projected).astype(BF16)
        if flip == 0:
            hidden_ref[...] = hidden
        wide = hidden.astype(F32)
        square = square + jnp.sum(wide * wide, axis=1, keepdims=True)
        gained.append((wide * ref[at + 1, :reqs].astype(F32)).astype(BF16))
    gained = jnp.concatenate(gained, axis=1)
    tiles = []
    for b in range(2 * blocks):
        ref, at = (gate_ref, b) if b < blocks else (up_ref, b - blocks)
        cols = pl.ds(pl.multiple_of((me * blocks + at) * LANES, LANES), LANES)
        w = jnp.concatenate([ref[:, cols]] + [met_ref[b] for met_ref in mets], axis=0)
        x = jnp.dot(gained, w, preferred_element_type=F32)
        tiles.append(x.reshape(reqs // 8, 8, LANES))
    for i in range(blocks):
        out_ref[:, i * 16 : (i + 1) * 16, :] = jnp.concatenate(
            [tiles[2 * i], tiles[2 * i + 1]], axis=1
        ).astype(BF16)
    square = jnp.broadcast_to(square, (reqs, LANES))
    high = square.astype(BF16).astype(F32)
    lane = lane_ids(square.shape)
    square = jnp.where(lane == 0, high, jnp.where(lane == 1, square - high, 0.0))
    out_ref[:, blocks * 16 :, :] = square.reshape(reqs // 8, 8, LANES).astype(BF16)


def activate_body(width, part_ref, out_ref):
    total = part_ref[0].astype(F32)
    for d in range(1, part_ref.shape[0]):
        total = total + part_ref[d].astype(F32)
    units = (total.shape[0] - 8) // 2
    square = total[2 * units :]
    square = square[:, 0:1] + square[:, 1:2]
    inv_rms = lax.rsqrt(jnp.broadcast_to(square, (8, LANES)) / width + EPS)[None]
    gate = total[:units].reshape(units // 8, 8, LANES) * inv_rms
    up = total[units : 2 * units].reshape(units // 8, 8, LANES) * inv_rms
    active = (gate / (1.0 + jnp.exp(-gate)) * up).reshape(units, LANES).astype(BF16)
    for d in range(out_ref.shape[0]):
        out_ref[d] = active


def down_body(
    ring, act_ref, w_ref, met_ref, hidden_ref, order_hbm, out_ref, kept_ref, order_ref, sem
):
    fetch = pltpu.make_async_copy(order_hbm, order_ref, sem)
    fetch.start()
    core = lax.axis_index("core")
    reqs = act_ref.shape[0] * act_ref.shape[2] * 8
    blocks = act_ref.shape[3] // 8
    height = blocks * LANES
    acts, own = [], []
    for z in range(2):
        act = act_ref[:, z].astype(F32).reshape(reqs // 8, blocks * 8, LANES)
        for b in range(blocks):
            acts.append(act[:, b * 8 : b * 8 + 8].reshape(reqs, LANES).astype(BF16))
        own.append(w_ref[pl.ds(pl.multiple_of((2 * z + core) * height, LANES), height), :])
    acts = jnp.concatenate(acts, axis=1)
    met = met_ref[...].reshape(2 * height, LANES)
    totals = [
        jnp.dot(acts, w, preferred_element_type=F32).astype(BF16)
        for w in (jnp.concatenate(own, axis=0), met)
    ]
    fetch.wait()
    place = lax.broadcasted_iota(jnp.int32, (reqs, reqs), 0)
    pick = (request_of(place, ring) == order_ref[...]).astype(F32).astype(BF16)
    dims = (((0,), (0,)), ((), ()))
    for at, total in ((core, totals[0]), (1 - core, totals[1])):
        total = lax.dot_general(pick, total, dims, preferred_element_type=F32)
        out_ref[at] = total.astype(BF16)
    kept = lax.dot_general(pick, hidden_ref[...], dims, preferred_element_type=F32)
    kept_ref[...] = kept.astype(BF16)


def finish_body(part_ref, kept_ref, out_ref):
    total = kept_ref[lax.axis_index(GRP)].astype(F32)
    for d in range(part_ref.shape[0]):
        total = total + part_ref[d].astype(F32)
    out_ref[...] = total.astype(BF16)


def shards(
    queries,
    fresh_keys,
    fresh_values,
    key_cache,
    value_cache,
    lengths,
    block_table,
    resid,
    out_weight,
    norm_gain,
    gate_weight,
    up_weight,
    down_weight,
    row_order,
):
    ctx, ring, rest, grp = (lax.axis_size(axes) for axes in (CTX, RING, REST, GRP))
    team = lax.axis_size(TEAM)
    reqs, width = resid.shape
    slots = key_cache.shape[0]
    share = reqs // grp
    shape = jax.ShapeDtypeStruct
    blocks = gate_weight.shape[1] // (team * LANES)

    def passed(blocks_out):
        return [
            lax.ppermute(block, TEAM, [(i, i ^ flip) for i in range(team)])
            for flip, block in enumerate(blocks_out, 1)
        ]

    bundle = shape((2 * blocks + 2, LANES, LANES), BF16)
    core_bundle = shape((2 * blocks, LANES, LANES), BF16)
    mine, given_core, *given = call(
        functools.partial(cut_body, ring),
        (shape((2, LANES, LANES), BF16), core_bundle) + (bundle,) * 3,
        [VMEM] * 5,
    )(gate_weight, up_weight, down_weight, resid, norm_gain.reshape(1, width))
    met = [
        lax.ppermute(block, TEAM, [(i, i ^ flip) for i in range(team)])
        for flip, block in enumerate(given, 1)
    ]
    met_core = lax.ppermute(given_core, "core", [(0, 1), (1, 0)])
    met_out = lax.ppermute(out_weight, "core", [(0, 1), (1, 0)])
    meta = call(
        prepare_body,
        shape((2 * slots,), jnp.int32),
        [HBM] * 2,
        [
            pltpu.SMEM(lengths.shape, jnp.int32),
            pltpu.VMEM(block_table.shape, jnp.int32),
            pltpu.SemaphoreType.DMA((2,)),
        ],
        out_specs=SMEM,
    )(lengths, block_table)

    packed, my_queries = call(
        pack_body, (shape((ring, 2 * GROUP, HD), BF16), shape((2 * GROUP, HD), BF16)), [VMEM]
    )(queries)
    all_queries = exchange(packed, RING)
    all_queries = lax.all_gather(all_queries, "core", axis=0, tiled=False)
    scratch = [pltpu.VMEM((reqs, GROUP, LANES), F32)] * 3
    parts = call(attend_body, shape((ctx, 3 * GROUP, HD), BF16), [SMEM] + [VMEM] * 3, scratch)(
        meta, all_queries, key_cache, value_cache
    )
    parts = exchange(parts, CTX)
    parts, mine = lax.optimization_barrier((parts, mine))
    local = call(combine_body, shape((ring, 2 * GROUP, HD), BF16), [VMEM] * 4)(
        parts, my_queries, fresh_keys, fresh_values
    )
    local, met_core = lax.optimization_barrier((local, met_core))
    attended = exchange(local, RING)
    projected = call(
        project_body,
        shape((grp, 2, reqs // 2, width), BF16),
        [VMEM] * 3,
        [pltpu.VMEM((ring * 2 * GROUP, HD), F32)],
    )(attended, out_weight, met_out)
    projected = exchange(projected.reshape(grp, reqs, width), GRP)
    pay = call(gather_body, shape((reqs, width), BF16), [VMEM])(projected)
    pay = lax.all_gather(pay, TEAM, axis=0, tiled=False)
    units = blocks * 8
    wide, hidden = call(
        widen_body,
        (shape((rest, 2 * units + 8, LANES), BF16), shape((reqs, width), BF16)),
        [VMEM] * 7,
    )(pay.reshape(team // 2, 2, 2, reqs // 2, width), mine, gate_weight, up_weight, *met)
    wide = exchange(wide, REST)
    active = call(
        functools.partial(activate_body, width * ctx), shape((ring, units, LANES), BF16), [VMEM]
    )(wide)
    active = exchange(active, RING)
    line = lax.axis_size("zl")
    rows, kept = call(
        functools.partial(down_body, ring),
        (shape((2, reqs, width), BF16), shape((reqs, width), BF16)),
        [VMEM] * 4 + [HBM],
        [pltpu.VMEM((1, reqs), jnp.int32), pltpu.SemaphoreType.DMA(())],
    )(
        active.reshape(ring // (2 * line), 2, line, units, LANES),
        down_weight,
        met_core,
        hidden,
        row_order.reshape(1, reqs),
    )
    rows = exchange(rows.reshape(2 * grp, share, width), LAST)
    return call(finish_body, shape((share, width), BF16), [VMEM] * 2)(
        rows, kept.reshape(grp, share, width)
    )


def solution(mesh, sizes=(4, 2, 4, 2, 2, 4)):
    inner = Mesh(mesh.devices.reshape(sizes), ("yh", "yl", "zl", "core", "zh", "x"))
    in_specs = (
        P(CTX, GRP),
        P(CTX, GRP),
        P(CTX, GRP),
        P(CTX, None, GRP),
        P(CTX, None, GRP),
        P(),
        P(),
        P(None, CTX),
        P(GRP, CTX),
        P(CTX),
        P(CTX, GRP),
        P(CTX, GRP),
        P(GRP, CTX),
        P(),
    )
    out_specs = P(GRP, CTX)
    return jax.shard_map(shards, mesh=inner, in_specs=in_specs, out_specs=out_specs, check_vma=False)
```

```python
import functools

import jax
import jax.numpy as jnp
from jax import lax
from jax.experimental import pallas as pl
from jax.experimental.pallas import tpu as pltpu
from jax.sharding import Mesh
from jax.sharding import PartitionSpec as P

HD = 128
GROUP = 8
LANES = 128
EPS = 1e-05
CHUNKS = 6
NEG = -1e30
VMEM_LIMIT = 16 * 2**20
CTX = ("yh", "yl", "zl", "core")
RING = ("yh", "yl", "zl")
REST = ("yh", "zl")
TEAM = ("yl", "core")
GRP = ("zh", "x")
LAST = ("core",) + GRP
F32 = jnp.float32
BF16 = jnp.bfloat16
VMEM = pl.BlockSpec(memory_space=pltpu.VMEM)
SMEM = pl.BlockSpec(memory_space=pltpu.SMEM)
HBM = pl.BlockSpec(memory_space=pltpu.HBM)


def exchange(x, axes):
    return lax.all_to_all(x, axes, 0, 0, tiled=True)


def lane_ids(shape):
    return lax.broadcasted_iota(jnp.int32, shape, len(shape) - 1)


def call(body, out_shape, in_specs, scratch=(), out_specs=None):
    kernel = pl.pallas_call(
        body,
        out_shape=out_shape,
        in_specs=in_specs,
        out_specs=jax.tree.map(lambda _: VMEM, out_shape) if out_specs is None else out_specs,
        scratch_shapes=list(scratch),
        compiler_params=pltpu.CompilerParams(vmem_limit_bytes=VMEM_LIMIT),
    )

    def run(*operands):
        placed = [
            pltpu.with_memory_space_constraint(x, pltpu.HBM) if spec is HBM else x
            for x, spec in zip(operands, in_specs, strict=True)
        ]
        return kernel(*placed)

    return run


def request_of(place, ring):
    core, at = place >> ring.bit_length(), place & (2 * ring - 1)
    return (at >> 1) * 4 + core * 2 + (at & 1)


def pack_body(q_ref, out_ref, mine_ref):
    wide = q_ref[...].astype(F32)
    rows = [
        wide[r : r + 1, h * HD : (h + 1) * HD] for r in range(wide.shape[0]) for h in range(GROUP)
    ]
    rows = jnp.concatenate(rows, axis=0).astype(BF16)
    mine_ref[...] = rows
    for d in range(out_ref.shape[0]):
        out_ref[d] = rows


def prepare_body(len_hbm, table_hbm, meta_ref, len_ref, table_ref, sems):
    pairs = ((table_hbm, table_ref), (len_hbm, len_ref))
    copies = [pltpu.make_async_copy(a, b, sems.at[i]) for i, (a, b) in enumerate(pairs)]
    for copy in copies:
        copy.start()
    for copy in copies:
        copy.wait()
    slots = meta_ref.shape[0] // 2
    first = lax.axis_index(CTX) * slots
    table = table_ref[...] - first
    rows, cols = table.shape
    code = lax.broadcasted_iota(jnp.int32, (rows, cols), 0) * cols + lane_ids((rows, cols))
    for s in range(slots):
        found = jnp.min(jnp.where(table == s, code, rows * cols - 1))
        owner = found // cols
        meta_ref[s] = owner
        meta_ref[slots + s] = len_ref[owner] - (found % cols) * LANES


def cut_body(
    ring, gate_ref, up_ref, down_ref, resid_ref, gain_ref, mine, core_ref, met2_ref, met3_ref
):
    me = lax.axis_index(TEAM)
    reqs = resid_ref.shape[0]
    place = lax.broadcasted_iota(jnp.int32, (reqs, reqs), 0)
    turn = (request_of(place, ring) == lane_ids((reqs, reqs))).astype(F32).astype(BF16)
    resid = jnp.dot(turn, resid_ref[...], preferred_element_type=F32).astype(BF16)
    gain = jnp.broadcast_to(gain_ref[...].astype(F32), (LANES, LANES)).astype(BF16)
    mine[0, :reqs] = resid
    mine[1] = gain
    blocks = (met2_ref.shape[0] - 2) // 2
    other = 1 - lax.axis_index("core")
    for z in range(2):
        start = pl.multiple_of((2 * z + other) * blocks * LANES, LANES)
        rows = down_ref[pl.ds(start, blocks * LANES), :]
        core_ref[z * blocks : (z + 1) * blocks] = rows.reshape(blocks, LANES, LANES)
    for flip, out_ref, base in ((1, core_ref, 2 * blocks), (2, met2_ref, 0), (3, met3_ref, 0)):
        start = (me ^ flip) * blocks * LANES
        for b in range(blocks):
            cols = pl.ds(pl.multiple_of(start + b * LANES, LANES), LANES)
            out_ref[base + b] = gate_ref[:, cols]
            out_ref[base + blocks + b] = up_ref[:, cols]
        out_ref[base + 2 * blocks, :reqs] = resid
        out_ref[base + 2 * blocks + 1] = gain


def attend_body(
    meta_ref, q_ref, k_hbm, v_hbm, out_ref, top_ref, sum_ref, acc_ref, k_ref, v_ref, sems
):
    slots, page = k_ref.shape[0], k_ref.shape[1]
    part = slots // CHUNKS
    fetches = []
    for w, (a, b) in enumerate(((k_hbm, k_ref), (v_hbm, v_ref))):
        for i in range(CHUNKS):
            span = pl.ds(i * part, part)
            fetches.append(pltpu.make_async_copy(a.at[span], b.at[span], sems.at[w, i]))
    for fetch in fetches:
        fetch.start()
    top_ref[...] = jnp.full(top_ref.shape, NEG, F32)
    sum_ref[...] = jnp.zeros(sum_ref.shape, F32)
    acc_ref[...] = jnp.zeros(acc_ref.shape, F32)
    for fetch in fetches:
        fetch.wait()
    lane = lane_ids((GROUP, page))
    owners, scores = [], []
    for s in range(slots):
        owner, live = meta_ref[s], meta_ref[slots + s]
        home = owner // 2
        pair = q_ref[home % 2, home // 2].astype(F32)
        q = jnp.where(owner % 2 == 1, pair[GROUP:], pair[:GROUP]).astype(BF16)
        score = lax.dot_general(q, k_ref[s], (((1,), (1,)), ((), ())), preferred_element_type=F32)
        score = jnp.where(lane < live, score * HD ** (-0.5), NEG)
        best = jnp.max(score, axis=1, keepdims=True)
        top_ref[owner] = jnp.maximum(top_ref[owner], jnp.broadcast_to(best, (GROUP, LANES)))
        owners.append(owner)
        scores.append(score)
    for s in range(slots):
        owner = owners[s]
        shift = top_ref[owner].astype(BF16).astype(F32)
        weight = jnp.exp(scores[s] - shift)
        total = jnp.sum(weight, axis=1, keepdims=True)
        sum_ref[owner] = sum_ref[owner] + jnp.broadcast_to(total, (GROUP, LANES))
        acc_ref[owner] = acc_ref[owner] + jnp.dot(
            weight.astype(BF16), v_ref[s], preferred_element_type=F32
        )
    lane = lane_ids((GROUP, LANES))
    for d in range(out_ref.shape[0]):
        stats = jnp.zeros((GROUP, LANES), F32)
        for par in range(2):
            total = sum_ref[2 * d + par]
            high = total.astype(BF16).astype(F32)
            base = par * 64
            stats = jnp.where(lane == base, top_ref[2 * d + par], stats)
            stats = jnp.where(lane == base + 1, high, stats)
            stats = jnp.where(lane == base + 2, total - high, stats)
        block = jnp.concatenate([acc_ref[2 * d], acc_ref[2 * d + 1], stats], axis=0)
        out_ref[d] = block.astype(BF16)


def combine_body(part_ref, q_ref, fk_ref, fv_ref, out_ref):
    count = part_ref.shape[0]
    best = jnp.full((GROUP, LANES), NEG, F32)
    for d in range(count):
        best = jnp.maximum(best, part_ref[d].astype(F32)[2 * GROUP :])
    fk, fv = fk_ref[...].astype(F32), fv_ref[...].astype(F32)
    q = q_ref[...].astype(F32)
    tops, totals, accs = [], [], []
    for par in range(2):
        mine = slice(par * GROUP, (par + 1) * GROUP)
        own = jnp.sum(q[mine] * fk[par : par + 1], axis=1, keepdims=True) * HD ** (-0.5)
        top = jnp.maximum(best[:, par * 64 : par * 64 + 1], own)
        own_weight = jnp.exp(own - top)
        tops.append(top)
        totals.append(own_weight)
        accs.append(own_weight.astype(BF16).astype(F32) * fv[par : par + 1])
    for d in range(count):
        block = part_ref[d].astype(F32)
        stats = block[2 * GROUP :]
        for par in range(2):
            base = par * 64
            factor = jnp.exp(stats[:, base : base + 1] - tops[par])
            total = stats[:, base + 1 : base + 2] + stats[:, base + 2 : base + 3]
            totals[par] = totals[par] + factor * total
            accs[par] = accs[par] + factor * block[par * GROUP : (par + 1) * GROUP]
    rows = jnp.concatenate([accs[par] / totals[par] for par in range(2)], axis=0).astype(BF16)
    for d in range(out_ref.shape[0]):
        out_ref[d] = rows


def project_body(att_ref, w_ref, met_ref, out_ref, rows_ref):
    core = lax.axis_index("core")
    count, per, _ = att_ref.shape
    rows_ref[...] = att_ref[...].astype(F32).reshape(count * per, HD)
    reqs = count * per // GROUP
    heads = [rows_ref[pl.ds(h, reqs, stride=GROUP), :].astype(BF16) for h in range(GROUP)]
    heads = jnp.concatenate(heads, axis=1)
    for at, ref in ((core, w_ref), (1 - core, met_ref)):
        total = jnp.dot(heads, ref[...], preferred_element_type=F32).astype(BF16)
        for g in range(out_ref.shape[0]):
            out_ref[g, at] = total


def gather_body(part_ref, out_ref):
    total = part_ref[0].astype(F32)
    for g in range(1, part_ref.shape[0]):
        total = total + part_ref[g].astype(F32)
    out_ref[...] = total.astype(BF16)


def widen_body(
    pay_ref, mine_ref, gate_ref, up_ref, met1_ref, met2_ref, met3_ref, out_ref, hidden_ref
):
    me = lax.axis_index(TEAM)
    team = 2 * pay_ref.shape[0]
    reqs = 2 * pay_ref.shape[3]
    mets = (met1_ref, met2_ref, met3_ref)
    blocks = (met2_ref.shape[0] - 2) // 2
    bases = (met1_ref.shape[0] - met2_ref.shape[0], 0, 0)
    square = jnp.zeros((reqs, 1), F32)
    gained = []
    for flip in range(team):
        ref, at = (mine_ref, 0) if flip == 0 else (mets[flip - 1], bases[flip - 1] + 2 * blocks)
        owner = me ^ flip
        chip, core = owner // 2, owner % 2
        projected = jnp.concatenate([pay_ref[chip, c, core].astype(F32) for c in range(2)], axis=0)
        hidden = (ref[at, :reqs].astype(F32) + projected).astype(BF16)
        if flip == 0:
            hidden_ref[...] = hidden
        wide = hidden.astype(F32)
        square = square + jnp.sum(wide * wide, axis=1, keepdims=True)
        gained.append((wide * ref[at + 1, :reqs].astype(F32)).astype(BF16))
    gained = jnp.concatenate(gained, axis=1)
    tiles = []
    for b in range(2 * blocks):
        ref, at = (gate_ref, b) if b < blocks else (up_ref, b - blocks)
        cols = pl.ds(pl.multiple_of((me * blocks + at) * LANES, LANES), LANES)
        w = jnp.concatenate([ref[:, cols]] + [met_ref[base + b] for met_ref, base in zip(mets, bases)], axis=0)
        x = jnp.dot(gained, w, preferred_element_type=F32)
        tiles.append(x.reshape(reqs // 8, 8, LANES))
    for i in range(blocks):
        out_ref[:, i * 16 : (i + 1) * 16, :] = jnp.concatenate(
            [tiles[2 * i], tiles[2 * i + 1]], axis=1
        ).astype(BF16)
    square = jnp.broadcast_to(square, (reqs, LANES))
    high = square.astype(BF16).astype(F32)
    lane = lane_ids(square.shape)
    square = jnp.where(lane == 0, high, jnp.where(lane == 1, square - high, 0.0))
    out_ref[:, blocks * 16 :, :] = square.reshape(reqs // 8, 8, LANES).astype(BF16)


def activate_body(width, part_ref, out_ref):
    total = part_ref[0].astype(F32)
    for d in range(1, part_ref.shape[0]):
        total = total + part_ref[d].astype(F32)
    units = (total.shape[0] - 8) // 2
    square = total[2 * units :]
    square = square[:, 0:1] + square[:, 1:2]
    inv_rms = lax.rsqrt(jnp.broadcast_to(square, (8, LANES)) / width + EPS)[None]
    gate = total[:units].reshape(units // 8, 8, LANES) * inv_rms
    up = total[units : 2 * units].reshape(units // 8, 8, LANES) * inv_rms
    active = (gate / (1.0 + jnp.exp(-gate)) * up).reshape(units, LANES).astype(BF16)
    for d in range(out_ref.shape[0]):
        out_ref[d] = active


def down_body(
    ring, act_ref, w_ref, met_ref, hidden_ref, order_hbm, out_ref, kept_ref, order_ref, sem
):
    fetch = pltpu.make_async_copy(order_hbm, order_ref, sem)
    fetch.start()
    core = lax.axis_index("core")
    reqs = act_ref.shape[0] * act_ref.shape[2] * 8
    blocks = act_ref.shape[3] // 8
    height = blocks * LANES
    acts, own = [], []
    for z in range(2):
        act = act_ref[:, z].astype(F32).reshape(reqs // 8, blocks * 8, LANES)
        for b in range(blocks):
            acts.append(act[:, b * 8 : b * 8 + 8].reshape(reqs, LANES).astype(BF16))
        own.append(w_ref[pl.ds(pl.multiple_of((2 * z + core) * height, LANES), height), :])
    acts = jnp.concatenate(acts, axis=1)
    met = met_ref[: 2 * blocks].reshape(2 * height, LANES)
    totals = [
        jnp.dot(acts, w, preferred_element_type=F32).astype(BF16)
        for w in (jnp.concatenate(own, axis=0), met)
    ]
    fetch.wait()
    place = lax.broadcasted_iota(jnp.int32, (reqs, reqs), 0)
    pick = (request_of(place, ring) == order_ref[...]).astype(F32).astype(BF16)
    dims = (((0,), (0,)), ((), ()))
    for at, total in ((core, totals[0]), (1 - core, totals[1])):
        total = lax.dot_general(pick, total, dims, preferred_element_type=F32)
        out_ref[at] = total.astype(BF16)
    kept = lax.dot_general(pick, hidden_ref[...], dims, preferred_element_type=F32)
    kept_ref[...] = kept.astype(BF16)


def finish_body(part_ref, kept_ref, out_ref):
    total = kept_ref[lax.axis_index(GRP)].astype(F32)
    for d in range(part_ref.shape[0]):
        total = total + part_ref[d].astype(F32)
    out_ref[...] = total.astype(BF16)


def shards(
    queries,
    fresh_keys,
    fresh_values,
    key_cache,
    value_cache,
    lengths,
    block_table,
    resid,
    out_weight,
    norm_gain,
    gate_weight,
    up_weight,
    down_weight,
    row_order,
):
    ctx, ring, rest, grp = (lax.axis_size(axes) for axes in (CTX, RING, REST, GRP))
    team = lax.axis_size(TEAM)
    reqs, width = resid.shape
    slots = key_cache.shape[0]
    share = reqs // grp
    shape = jax.ShapeDtypeStruct
    blocks = gate_weight.shape[1] // (team * LANES)

    def passed(blocks_out):
        return [
            lax.ppermute(block, TEAM, [(i, i ^ flip) for i in range(team)])
            for flip, block in enumerate(blocks_out, 1)
        ]

    bundle = shape((2 * blocks + 2, LANES, LANES), BF16)
    core_bundle = shape((4 * blocks + 2, LANES, LANES), BF16)
    mine, given_core, *given = call(
        functools.partial(cut_body, ring),
        (shape((2, LANES, LANES), BF16), core_bundle, bundle, bundle),
        [VMEM] * 5,
    )(gate_weight, up_weight, down_weight, resid, norm_gain.reshape(1, width))
    met = [
        lax.ppermute(block, TEAM, [(i, i ^ flip) for i in range(team)])
        for flip, block in enumerate(given, 2)
    ]
    met_core = lax.ppermute(given_core, "core", [(0, 1), (1, 0)])
    met_out = lax.ppermute(out_weight, "core", [(0, 1), (1, 0)])
    meta = call(
        prepare_body,
        shape((2 * slots,), jnp.int32),
        [HBM] * 2,
        [
            pltpu.SMEM(lengths.shape, jnp.int32),
            pltpu.VMEM(block_table.shape, jnp.int32),
            pltpu.SemaphoreType.DMA((2,)),
        ],
        out_specs=SMEM,
    )(lengths, block_table)

    packed, my_queries = call(
        pack_body, (shape((ring, 2 * GROUP, HD), BF16), shape((2 * GROUP, HD), BF16)), [VMEM]
    )(queries)
    all_queries = exchange(packed, RING)
    all_queries = lax.all_gather(all_queries, "core", axis=0, tiled=False)
    scratch = [pltpu.VMEM((reqs, GROUP, LANES), F32)] * 3
    scratch += [pltpu.VMEM(key_cache.shape, BF16)] * 2 + [pltpu.SemaphoreType.DMA((2, CHUNKS))]
    parts = call(attend_body, shape((ctx, 3 * GROUP, HD), BF16), [SMEM, VMEM, HBM, HBM], scratch)(
        meta, all_queries, key_cache, value_cache
    )
    parts = exchange(parts, CTX)
    parts, mine = lax.optimization_barrier((parts, mine))
    local = call(combine_body, shape((ring, 2 * GROUP, HD), BF16), [VMEM] * 4)(
        parts, my_queries, fresh_keys, fresh_values
    )
    attended = exchange(local, RING)
    attended, met_core = lax.optimization_barrier((attended, met_core))
    projected = call(
        project_body,
        shape((grp, 2, reqs // 2, width), BF16),
        [VMEM] * 3,
        [pltpu.VMEM((ring * 2 * GROUP, HD), F32)],
    )(attended, out_weight, met_out)
    projected = exchange(projected.reshape(grp, reqs, width), GRP)
    pay = call(gather_body, shape((reqs, width), BF16), [VMEM])(projected)
    pay = lax.all_gather(pay, TEAM, axis=0, tiled=False)
    units = blocks * 8
    wide, hidden = call(
        widen_body,
        (shape((rest, 2 * units + 8, LANES), BF16), shape((reqs, width), BF16)),
        [VMEM] * 7,
    )(pay.reshape(team // 2, 2, 2, reqs // 2, width), mine, gate_weight, up_weight, met_core, *met)
    wide = exchange(wide, REST)
    active = call(
        functools.partial(activate_body, width * ctx), shape((ring, units, LANES), BF16), [VMEM]
    )(wide)
    active = exchange(active, RING)
    line = lax.axis_size("zl")
    rows, kept = call(
        functools.partial(down_body, ring),
        (shape((2, reqs, width), BF16), shape((reqs, width), BF16)),
        [VMEM] * 4 + [HBM],
        [pltpu.VMEM((1, reqs), jnp.int32), pltpu.SemaphoreType.DMA(())],
    )(
        active.reshape(ring // (2 * line), 2, line, units, LANES),
        down_weight,
        met_core,
        hidden,
        row_order.reshape(1, reqs),
    )
    rows = exchange(rows.reshape(2 * grp, share, width), LAST)
    return call(finish_body, shape((share, width), BF16), [VMEM] * 2)(
        rows, kept.reshape(grp, share, width)
    )


def solution(mesh, sizes=(4, 2, 4, 2, 2, 4)):
    inner = Mesh(mesh.devices.reshape(sizes), ("yh", "yl", "zl", "core", "zh", "x"))
    in_specs = (
        P(CTX, GRP),
        P(CTX, GRP),
        P(CTX, GRP),
        P(CTX, None, GRP),
        P(CTX, None, GRP),
        P(),
        P(),
        P(None, CTX),
        P(GRP, CTX),
        P(CTX),
        P(CTX, GRP),
        P(CTX, GRP),
        P(GRP, CTX),
        P(),
    )
    out_specs = P(GRP, CTX)
    return jax.shard_map(shards, mesh=inner, in_specs=in_specs, out_specs=out_specs, check_vma=False)
```

```python
import functools

import jax
import jax.numpy as jnp
from jax import lax
from jax.experimental import pallas as pl
from jax.experimental.pallas import tpu as pltpu
from jax.sharding import Mesh
from jax.sharding import PartitionSpec as P

HD = 128
GROUP = 8
LANES = 128
EPS = 1e-05
CHUNKS = 6
NEG = -1e30
VMEM_LIMIT = 16 * 2**20
CTX = ("yh", "yl", "zl", "core")
RING = ("yh", "yl", "zl")
REST = ("yh", "zl")
TEAM = ("yl", "core")
GRP = ("zh", "x")
LAST = ("core",) + GRP
F32 = jnp.float32
BF16 = jnp.bfloat16
VMEM = pl.BlockSpec(memory_space=pltpu.VMEM)
SMEM = pl.BlockSpec(memory_space=pltpu.SMEM)
HBM = pl.BlockSpec(memory_space=pltpu.HBM)


def exchange(x, axes):
    return lax.all_to_all(x, axes, 0, 0, tiled=True)


def lane_ids(shape):
    return lax.broadcasted_iota(jnp.int32, shape, len(shape) - 1)


def call(body, out_shape, in_specs, scratch=(), out_specs=None):
    kernel = pl.pallas_call(
        body,
        out_shape=out_shape,
        in_specs=in_specs,
        out_specs=jax.tree.map(lambda _: VMEM, out_shape) if out_specs is None else out_specs,
        scratch_shapes=list(scratch),
        compiler_params=pltpu.CompilerParams(vmem_limit_bytes=VMEM_LIMIT),
    )

    def run(*operands):
        placed = [
            pltpu.with_memory_space_constraint(x, pltpu.HBM) if spec is HBM else x
            for x, spec in zip(operands, in_specs, strict=True)
        ]
        return kernel(*placed)

    return run


def request_of(place, ring):
    core, at = place >> ring.bit_length(), place & (2 * ring - 1)
    return (at >> 1) * 4 + core * 2 + (at & 1)


def pack_body(q_hbm, out_ref, mine_ref, q_ref, sem):
    fetch = pltpu.make_async_copy(q_hbm, q_ref, sem)
    fetch.start()
    fetch.wait()
    wide = q_ref[...].astype(F32)
    rows = [
        wide[r : r + 1, h * HD : (h + 1) * HD] for r in range(wide.shape[0]) for h in range(GROUP)
    ]
    rows = jnp.concatenate(rows, axis=0).astype(BF16)
    mine_ref[...] = rows
    for d in range(out_ref.shape[0]):
        out_ref[d] = rows


def prepare_body(len_hbm, table_hbm, meta_ref, len_ref, table_ref, sems):
    pairs = ((table_hbm, table_ref), (len_hbm, len_ref))
    copies = [pltpu.make_async_copy(a, b, sems.at[i]) for i, (a, b) in enumerate(pairs)]
    for copy in copies:
        copy.start()
    for copy in copies:
        copy.wait()
    slots = meta_ref.shape[0] // 2
    first = lax.axis_index(CTX) * slots
    table = table_ref[...] - first
    rows, cols = table.shape
    code = lax.broadcasted_iota(jnp.int32, (rows, cols), 0) * cols + lane_ids((rows, cols))
    for s in range(slots):
        found = jnp.min(jnp.where(table == s, code, rows * cols - 1))
        owner = found // cols
        meta_ref[s] = owner
        meta_ref[slots + s] = len_ref[owner] - (found % cols) * LANES


def cut_body(
    ring, gate_ref, up_ref, down_ref, resid_ref, gain_ref, mine, core_ref, met2_ref, met3_ref
):
    me = lax.axis_index(TEAM)
    reqs = resid_ref.shape[0]
    place = lax.broadcasted_iota(jnp.int32, (reqs, reqs), 0)
    turn = (request_of(place, ring) == lane_ids((reqs, reqs))).astype(F32).astype(BF16)
    resid = jnp.dot(turn, resid_ref[...], preferred_element_type=F32).astype(BF16)
    gain = jnp.broadcast_to(gain_ref[...].astype(F32), (LANES, LANES)).astype(BF16)
    mine[0, :reqs] = resid
    mine[1] = gain
    blocks = (met2_ref.shape[0] - 2) // 2
    other = 1 - lax.axis_index("core")
    for z in range(2):
        start = pl.multiple_of((2 * z + other) * blocks * LANES, LANES)
        rows = down_ref[pl.ds(start, blocks * LANES), :]
        core_ref[z * blocks : (z + 1) * blocks] = rows.reshape(blocks, LANES, LANES)
    for flip, out_ref, base in ((1, core_ref, 2 * blocks), (2, met2_ref, 0), (3, met3_ref, 0)):
        start = (me ^ flip) * blocks * LANES
        for b in range(blocks):
            cols = pl.ds(pl.multiple_of(start + b * LANES, LANES), LANES)
            out_ref[base + b] = gate_ref[:, cols]
            out_ref[base + blocks + b] = up_ref[:, cols]
        out_ref[base + 2 * blocks, :reqs] = resid
        out_ref[base + 2 * blocks + 1] = gain


def attend_body(
    meta_ref,
    q_ref,
    k_hbm,
    v_hbm,
    fk_hbm,
    fv_hbm,
    out_ref,
    fresh_ref,
    top_ref,
    sum_ref,
    acc_ref,
    k_ref,
    v_ref,
    fk_ref,
    fv_ref,
    sems,
    fresh_sems,
):
    slots, page = k_ref.shape[0], k_ref.shape[1]
    part = slots // CHUNKS
    fetches = []
    for w, (a, b) in enumerate(((k_hbm, k_ref), (v_hbm, v_ref))):
        for i in range(CHUNKS):
            span = pl.ds(i * part, part)
            fetches.append(pltpu.make_async_copy(a.at[span], b.at[span], sems.at[w, i]))
    fetches.append(pltpu.make_async_copy(fk_hbm, fk_ref, fresh_sems.at[0]))
    fetches.append(pltpu.make_async_copy(fv_hbm, fv_ref, fresh_sems.at[1]))
    for fetch in fetches:
        fetch.start()
    top_ref[...] = jnp.full(top_ref.shape, NEG, F32)
    sum_ref[...] = jnp.zeros(sum_ref.shape, F32)
    acc_ref[...] = jnp.zeros(acc_ref.shape, F32)
    for fetch in fetches:
        fetch.wait()
    fresh_ref[0] = fk_ref[...].astype(F32)
    fresh_ref[1] = fv_ref[...].astype(F32)
    lane = lane_ids((GROUP, page))
    owners, scores = [], []
    for s in range(slots):
        owner, live = meta_ref[s], meta_ref[slots + s]
        home = owner // 2
        pair = q_ref[home % 2, home // 2].astype(F32)
        q = jnp.where(owner % 2 == 1, pair[GROUP:], pair[:GROUP]).astype(BF16)
        score = lax.dot_general(q, k_ref[s], (((1,), (1,)), ((), ())), preferred_element_type=F32)
        score = jnp.where(lane < live, score * HD ** (-0.5), NEG)
        best = jnp.max(score, axis=1, keepdims=True)
        top_ref[owner] = jnp.maximum(top_ref[owner], jnp.broadcast_to(best, (GROUP, LANES)))
        owners.append(owner)
        scores.append(score)
    for s in range(slots):
        owner = owners[s]
        shift = top_ref[owner].astype(BF16).astype(F32)
        weight = jnp.exp(scores[s] - shift)
        total = jnp.sum(weight, axis=1, keepdims=True)
        sum_ref[owner] = sum_ref[owner] + jnp.broadcast_to(total, (GROUP, LANES))
        acc_ref[owner] = acc_ref[owner] + jnp.dot(
            weight.astype(BF16), v_ref[s], preferred_element_type=F32
        )
    lane = lane_ids((GROUP, LANES))
    for d in range(out_ref.shape[0]):
        stats = jnp.zeros((GROUP, LANES), F32)
        for par in range(2):
            total = sum_ref[2 * d + par]
            high = total.astype(BF16).astype(F32)
            base = par * 64
            stats = jnp.where(lane == base, top_ref[2 * d + par], stats)
            stats = jnp.where(lane == base + 1, high, stats)
            stats = jnp.where(lane == base + 2, total - high, stats)
        block = jnp.concatenate([acc_ref[2 * d], acc_ref[2 * d + 1], stats], axis=0)
        out_ref[d] = block.astype(BF16)


def combine_body(part_ref, q_ref, fresh_ref, out_ref):
    count = part_ref.shape[0]
    best = jnp.full((GROUP, LANES), NEG, F32)
    for d in range(count):
        best = jnp.maximum(best, part_ref[d].astype(F32)[2 * GROUP :])
    fk, fv = fresh_ref[0], fresh_ref[1]
    q = q_ref[...].astype(F32)
    tops, totals, accs = [], [], []
    for par in range(2):
        mine = slice(par * GROUP, (par + 1) * GROUP)
        own = jnp.sum(q[mine] * fk[par : par + 1], axis=1, keepdims=True) * HD ** (-0.5)
        top = jnp.maximum(best[:, par * 64 : par * 64 + 1], own)
        own_weight = jnp.exp(own - top)
        tops.append(top)
        totals.append(own_weight)
        accs.append(own_weight.astype(BF16).astype(F32) * fv[par : par + 1])
    for d in range(count):
        block = part_ref[d].astype(F32)
        stats = block[2 * GROUP :]
        for par in range(2):
            base = par * 64
            factor = jnp.exp(stats[:, base : base + 1] - tops[par])
            total = stats[:, base + 1 : base + 2] + stats[:, base + 2 : base + 3]
            totals[par] = totals[par] + factor * total
            accs[par] = accs[par] + factor * block[par * GROUP : (par + 1) * GROUP]
    rows = jnp.concatenate([accs[par] / totals[par] for par in range(2)], axis=0).astype(BF16)
    for d in range(out_ref.shape[0]):
        out_ref[d] = rows


def project_body(att_ref, w_ref, met_ref, out_ref, rows_ref):
    core = lax.axis_index("core")
    count, per, _ = att_ref.shape
    rows_ref[...] = att_ref[...].astype(F32).reshape(count * per, HD)
    reqs = count * per // GROUP
    heads = [rows_ref[pl.ds(h, reqs, stride=GROUP), :].astype(BF16) for h in range(GROUP)]
    heads = jnp.concatenate(heads, axis=1)
    for at, ref in ((core, w_ref), (1 - core, met_ref)):
        total = jnp.dot(heads, ref[...], preferred_element_type=F32).astype(BF16)
        for g in range(out_ref.shape[0]):
            out_ref[g, at] = total


def gather_body(part_ref, out_ref):
    total = part_ref[0].astype(F32)
    for g in range(1, part_ref.shape[0]):
        total = total + part_ref[g].astype(F32)
    out_ref[...] = total.astype(BF16)


def widen_body(
    pay_ref, mine_ref, gate_ref, up_ref, met1_ref, met2_ref, met3_ref, out_ref, hidden_ref
):
    me = lax.axis_index(TEAM)
    team = 2 * pay_ref.shape[0]
    reqs = 2 * pay_ref.shape[3]
    mets = (met1_ref, met2_ref, met3_ref)
    blocks = (met2_ref.shape[0] - 2) // 2
    bases = (met1_ref.shape[0] - met2_ref.shape[0], 0, 0)
    square = jnp.zeros((reqs, 1), F32)
    gained = []
    for flip in range(team):
        ref, at = (mine_ref, 0) if flip == 0 else (mets[flip - 1], bases[flip - 1] + 2 * blocks)
        owner = me ^ flip
        chip, core = owner // 2, owner % 2
        projected = jnp.concatenate([pay_ref[chip, c, core].astype(F32) for c in range(2)], axis=0)
        hidden = (ref[at, :reqs].astype(F32) + projected).astype(BF16)
        if flip == 0:
            hidden_ref[...] = hidden
        wide = hidden.astype(F32)
        square = square + jnp.sum(wide * wide, axis=1, keepdims=True)
        gained.append((wide * ref[at + 1, :reqs].astype(F32)).astype(BF16))
    gained = jnp.concatenate(gained, axis=1)
    tiles = []
    for b in range(2 * blocks):
        ref, at = (gate_ref, b) if b < blocks else (up_ref, b - blocks)
        cols = pl.ds(pl.multiple_of((me * blocks + at) * LANES, LANES), LANES)
        w = jnp.concatenate([ref[:, cols]] + [met_ref[base + b] for met_ref, base in zip(mets, bases)], axis=0)
        x = jnp.dot(gained, w, preferred_element_type=F32)
        tiles.append(x.reshape(reqs // 8, 8, LANES))
    for i in range(blocks):
        out_ref[:, i * 16 : (i + 1) * 16, :] = jnp.concatenate(
            [tiles[2 * i], tiles[2 * i + 1]], axis=1
        ).astype(BF16)
    square = jnp.broadcast_to(square, (reqs, LANES))
    high = square.astype(BF16).astype(F32)
    lane = lane_ids(square.shape)
    square = jnp.where(lane == 0, high, jnp.where(lane == 1, square - high, 0.0))
    out_ref[:, blocks * 16 :, :] = square.reshape(reqs // 8, 8, LANES).astype(BF16)


def activate_body(width, part_ref, out_ref):
    total = part_ref[0].astype(F32)
    for d in range(1, part_ref.shape[0]):
        total = total + part_ref[d].astype(F32)
    units = (total.shape[0] - 8) // 2
    square = total[2 * units :]
    square = square[:, 0:1] + square[:, 1:2]
    inv_rms = lax.rsqrt(jnp.broadcast_to(square, (8, LANES)) / width + EPS)[None]
    gate = total[:units].reshape(units // 8, 8, LANES) * inv_rms
    up = total[units : 2 * units].reshape(units // 8, 8, LANES) * inv_rms
    active = (gate / (1.0 + jnp.exp(-gate)) * up).reshape(units, LANES).astype(BF16)
    for d in range(out_ref.shape[0]):
        out_ref[d] = active


def down_body(
    ring, act_ref, w_ref, met_ref, hidden_ref, order_hbm, out_ref, kept_ref, order_ref, sem
):
    fetch = pltpu.make_async_copy(order_hbm, order_ref, sem)
    fetch.start()
    core = lax.axis_index("core")
    reqs = act_ref.shape[0] * act_ref.shape[2] * 8
    blocks = act_ref.shape[3] // 8
    height = blocks * LANES
    acts, own = [], []
    for z in range(2):
        act = act_ref[:, z].astype(F32).reshape(reqs // 8, blocks * 8, LANES)
        for b in range(blocks):
            acts.append(act[:, b * 8 : b * 8 + 8].reshape(reqs, LANES).astype(BF16))
        own.append(w_ref[pl.ds(pl.multiple_of((2 * z + core) * height, LANES), height), :])
    acts = jnp.concatenate(acts, axis=1)
    met = met_ref[: 2 * blocks].reshape(2 * height, LANES)
    totals = [
        jnp.dot(acts, w, preferred_element_type=F32).astype(BF16)
        for w in (jnp.concatenate(own, axis=0), met)
    ]
    fetch.wait()
    place = lax.broadcasted_iota(jnp.int32, (reqs, reqs), 0)
    pick = (request_of(place, ring) == order_ref[...]).astype(F32).astype(BF16)
    dims = (((0,), (0,)), ((), ()))
    for at, total in ((core, totals[0]), (1 - core, totals[1])):
        total = lax.dot_general(pick, total, dims, preferred_element_type=F32)
        out_ref[at] = total.astype(BF16)
    kept = lax.dot_general(pick, hidden_ref[...], dims, preferred_element_type=F32)
    kept_ref[...] = kept.astype(BF16)


def finish_body(part_ref, kept_ref, out_ref):
    total = kept_ref[lax.axis_index(GRP)].astype(F32)
    for d in range(part_ref.shape[0]):
        total = total + part_ref[d].astype(F32)
    out_ref[...] = total.astype(BF16)


def shards(
    queries,
    fresh_keys,
    fresh_values,
    key_cache,
    value_cache,
    lengths,
    block_table,
    resid,
    out_weight,
    norm_gain,
    gate_weight,
    up_weight,
    down_weight,
    row_order,
):
    ctx, ring, rest, grp = (lax.axis_size(axes) for axes in (CTX, RING, REST, GRP))
    team = lax.axis_size(TEAM)
    reqs, width = resid.shape
    slots = key_cache.shape[0]
    share = reqs // grp
    shape = jax.ShapeDtypeStruct
    blocks = gate_weight.shape[1] // (team * LANES)

    def passed(blocks_out):
        return [
            lax.ppermute(block, TEAM, [(i, i ^ flip) for i in range(team)])
            for flip, block in enumerate(blocks_out, 1)
        ]

    bundle = shape((2 * blocks + 2, LANES, LANES), BF16)
    core_bundle = shape((4 * blocks + 2, LANES, LANES), BF16)
    mine, given_core, *given = call(
        functools.partial(cut_body, ring),
        (shape((2, LANES, LANES), BF16), core_bundle, bundle, bundle),
        [VMEM] * 5,
    )(gate_weight, up_weight, down_weight, resid, norm_gain.reshape(1, width))
    met = [
        lax.ppermute(block, TEAM, [(i, i ^ flip) for i in range(team)])
        for flip, block in enumerate(given, 2)
    ]
    met_core = lax.ppermute(given_core, "core", [(0, 1), (1, 0)])
    met_out = lax.ppermute(out_weight, "core", [(0, 1), (1, 0)])
    meta = call(
        prepare_body,
        shape((2 * slots,), jnp.int32),
        [HBM] * 2,
        [
            pltpu.SMEM(lengths.shape, jnp.int32),
            pltpu.VMEM(block_table.shape, jnp.int32),
            pltpu.SemaphoreType.DMA((2,)),
        ],
        out_specs=SMEM,
    )(lengths, block_table)

    packed, my_queries = call(
        pack_body,
        (shape((ring, 2 * GROUP, HD), BF16), shape((2 * GROUP, HD), BF16)),
        [HBM],
        [pltpu.VMEM(queries.shape, BF16), pltpu.SemaphoreType.DMA(())],
    )(queries)
    all_queries = exchange(packed, RING)
    all_queries = lax.all_gather(all_queries, "core", axis=0, tiled=False)
    scratch = [pltpu.VMEM((reqs, GROUP, LANES), F32)] * 3
    scratch += [pltpu.VMEM(key_cache.shape, BF16)] * 2 + [pltpu.VMEM(fresh_keys.shape, BF16)] * 2
    scratch += [pltpu.SemaphoreType.DMA((2, CHUNKS)), pltpu.SemaphoreType.DMA((2,))]
    parts, fresh = call(
        attend_body,
        (pltpu.HBM((ctx, 3 * GROUP, HD), BF16), shape((2,) + fresh_keys.shape, F32)),
        [SMEM, VMEM] + [HBM] * 4,
        scratch,
    )(meta, all_queries, key_cache, value_cache, fresh_keys, fresh_values)
    parts = exchange(parts, CTX)
    parts, mine = lax.optimization_barrier((parts, mine))
    local = call(combine_body, shape((ring, 2 * GROUP, HD), BF16), [VMEM] * 3)(
        parts, my_queries, fresh
    )
    attended = exchange(local, RING)
    attended, met_core = lax.optimization_barrier((attended, met_core))
    projected = call(
        project_body,
        shape((grp, 2, reqs // 2, width), BF16),
        [VMEM] * 3,
        [pltpu.VMEM((ring * 2 * GROUP, HD), F32)],
    )(attended, out_weight, met_out)
    projected = exchange(projected.reshape(grp, reqs, width), GRP)
    pay = call(gather_body, shape((reqs, width), BF16), [VMEM])(projected)
    pay = lax.all_gather(pay, TEAM, axis=0, tiled=False)
    units = blocks * 8
    wide, hidden = call(
        widen_body,
        (shape((rest, 2 * units + 8, LANES), BF16), shape((reqs, width), BF16)),
        [VMEM] * 7,
    )(pay.reshape(team // 2, 2, 2, reqs // 2, width), mine, gate_weight, up_weight, met_core, *met)
    wide = exchange(wide, REST)
    active = call(
        functools.partial(activate_body, width * ctx), shape((ring, units, LANES), BF16), [VMEM]
    )(wide)
    active = exchange(active, RING)
    line = lax.axis_size("zl")
    rows, kept = call(
        functools.partial(down_body, ring),
        (shape((2, reqs, width), BF16), shape((reqs, width), BF16)),
        [VMEM] * 4 + [HBM],
        [pltpu.VMEM((1, reqs), jnp.int32), pltpu.SemaphoreType.DMA(())],
    )(
        active.reshape(ring // (2 * line), 2, line, units, LANES),
        down_weight,
        met_core,
        hidden,
        row_order.reshape(1, reqs),
    )
    rows = exchange(rows.reshape(2 * grp, share, width), LAST)
    return call(finish_body, shape((share, width), BF16), [VMEM] * 2)(
        rows, kept.reshape(grp, share, width)
    )


def solution(mesh, sizes=(4, 2, 4, 2, 2, 4)):
    inner = Mesh(mesh.devices.reshape(sizes), ("yh", "yl", "zl", "core", "zh", "x"))
    in_specs = (
        P(CTX, GRP),
        P(CTX, GRP),
        P(CTX, GRP),
        P(CTX, None, GRP),
        P(CTX, None, GRP),
        P(),
        P(),
        P(None, CTX),
        P(GRP, CTX),
        P(CTX),
        P(CTX, GRP),
        P(CTX, GRP),
        P(GRP, CTX),
        P(),
    )
    out_specs = P(GRP, CTX)
    return jax.shard_map(shards, mesh=inner, in_specs=in_specs, out_specs=out_specs, check_vma=False)
```

```python
import functools

import jax
import jax.numpy as jnp
from jax import lax
from jax.experimental import pallas as pl
from jax.experimental.pallas import tpu as pltpu
from jax.sharding import Mesh
from jax.sharding import PartitionSpec as P

HD = 128
GROUP = 8
LANES = 128
EPS = 1e-05
CHUNKS = 6
NEG = -1e30
VMEM_LIMIT = 16 * 2**20
CTX = ("yh", "yl", "zl", "core")
RING = ("yh", "yl", "zl")
REST = ("yh", "zl")
TEAM = ("yl", "core")
GRP = ("zh", "x")
LAST = ("core",) + GRP
F32 = jnp.float32
BF16 = jnp.bfloat16
VMEM = pl.BlockSpec(memory_space=pltpu.VMEM)
SMEM = pl.BlockSpec(memory_space=pltpu.SMEM)
HBM = pl.BlockSpec(memory_space=pltpu.HBM)


def exchange(x, axes):
    return lax.all_to_all(x, axes, 0, 0, tiled=True)


def lane_ids(shape):
    return lax.broadcasted_iota(jnp.int32, shape, len(shape) - 1)


def call(body, out_shape, in_specs, scratch=(), out_specs=None):
    kernel = pl.pallas_call(
        body,
        out_shape=out_shape,
        in_specs=in_specs,
        out_specs=jax.tree.map(lambda _: VMEM, out_shape) if out_specs is None else out_specs,
        scratch_shapes=list(scratch),
        compiler_params=pltpu.CompilerParams(vmem_limit_bytes=VMEM_LIMIT),
    )

    def run(*operands):
        placed = [
            pltpu.with_memory_space_constraint(x, pltpu.HBM) if spec is HBM else x
            for x, spec in zip(operands, in_specs, strict=True)
        ]
        return kernel(*placed)

    return run


def request_of(place, ring):
    core, at = place >> ring.bit_length(), place & (2 * ring - 1)
    return (at >> 1) * 4 + core * 2 + (at & 1)


def pack_body(q_hbm, out_ref, mine_ref, q_ref, sem):
    fetch = pltpu.make_async_copy(q_hbm, q_ref, sem)
    fetch.start()
    fetch.wait()
    wide = q_ref[...].astype(F32)
    rows = [
        wide[r : r + 1, h * HD : (h + 1) * HD] for r in range(wide.shape[0]) for h in range(GROUP)
    ]
    rows = jnp.concatenate(rows, axis=0).astype(BF16)
    mine_ref[...] = rows
    for d in range(out_ref.shape[0]):
        out_ref[d] = rows


def prepare_body(len_hbm, table_hbm, meta_ref, len_ref, table_ref, sems):
    pairs = ((table_hbm, table_ref), (len_hbm, len_ref))
    copies = [pltpu.make_async_copy(a, b, sems.at[i]) for i, (a, b) in enumerate(pairs)]
    for copy in copies:
        copy.start()
    for copy in copies:
        copy.wait()
    slots = meta_ref.shape[0] // 2
    first = lax.axis_index(CTX) * slots
    table = table_ref[...] - first
    rows, cols = table.shape
    code = lax.broadcasted_iota(jnp.int32, (rows, cols), 0) * cols + lane_ids((rows, cols))
    for s in range(slots):
        found = jnp.min(jnp.where(table == s, code, rows * cols - 1))
        owner = found // cols
        meta_ref[s] = owner
        meta_ref[slots + s] = len_ref[owner] - (found % cols) * LANES


def cut_body(
    ring, gate_ref, up_ref, down_ref, resid_ref, gain_ref, mine, core_ref, met2_ref, met3_ref
):
    me = lax.axis_index(TEAM)
    reqs = resid_ref.shape[0]
    place = lax.broadcasted_iota(jnp.int32, (reqs, reqs), 0)
    turn = (request_of(place, ring) == lane_ids((reqs, reqs))).astype(F32).astype(BF16)
    resid = jnp.dot(turn, resid_ref[...], preferred_element_type=F32).astype(BF16)
    gain = jnp.broadcast_to(gain_ref[...].astype(F32), (LANES, LANES)).astype(BF16)
    mine[0, :reqs] = resid
    mine[1] = gain
    blocks = (met2_ref.shape[0] - 2) // 2
    other = 1 - lax.axis_index("core")
    for z in range(2):
        start = pl.multiple_of((2 * z + other) * blocks * LANES, LANES)
        rows = down_ref[pl.ds(start, blocks * LANES), :]
        core_ref[z * blocks : (z + 1) * blocks] = rows.reshape(blocks, LANES, LANES)
    for flip, out_ref, base in ((1, core_ref, 2 * blocks), (2, met2_ref, 0), (3, met3_ref, 0)):
        start = (me ^ flip) * blocks * LANES
        for b in range(blocks):
            cols = pl.ds(pl.multiple_of(start + b * LANES, LANES), LANES)
            out_ref[base + b] = gate_ref[:, cols]
            out_ref[base + blocks + b] = up_ref[:, cols]
        out_ref[base + 2 * blocks, :reqs] = resid
        out_ref[base + 2 * blocks + 1] = gain


def attend_body(
    meta_ref,
    q_ref,
    k_hbm,
    v_hbm,
    fk_hbm,
    fv_hbm,
    out_ref,
    fresh_ref,
    top_ref,
    sum_ref,
    acc_ref,
    k_ref,
    v_ref,
    fk_ref,
    fv_ref,
    sems,
    fresh_sems,
):
    slots, page = k_ref.shape[0], k_ref.shape[1]
    part = slots // CHUNKS
    fetches = []
    for w, (a, b) in enumerate(((k_hbm, k_ref), (v_hbm, v_ref))):
        for i in range(CHUNKS):
            span = pl.ds(i * part, part)
            fetches.append(pltpu.make_async_copy(a.at[span], b.at[span], sems.at[w, i]))
    fetches.append(pltpu.make_async_copy(fk_hbm, fk_ref, fresh_sems.at[0]))
    fetches.append(pltpu.make_async_copy(fv_hbm, fv_ref, fresh_sems.at[1]))
    for fetch in fetches:
        fetch.start()
    top_ref[...] = jnp.full(top_ref.shape, NEG, F32)
    sum_ref[...] = jnp.zeros(sum_ref.shape, F32)
    acc_ref[...] = jnp.zeros(acc_ref.shape, F32)
    for fetch in fetches:
        fetch.wait()
    fresh_ref[0] = fk_ref[...].astype(F32)
    fresh_ref[1] = fv_ref[...].astype(F32)
    lane = lane_ids((GROUP, page))
    owners, scores = [], []
    for s in range(slots):
        owner, live = meta_ref[s], meta_ref[slots + s]
        home = owner // 2
        pair = q_ref[home % 2, home // 2].astype(F32)
        q = jnp.where(owner % 2 == 1, pair[GROUP:], pair[:GROUP]).astype(BF16)
        score = lax.dot_general(q, k_ref[s], (((1,), (1,)), ((), ())), preferred_element_type=F32)
        score = jnp.where(lane < live, score * HD ** (-0.5), NEG)
        best = jnp.max(score, axis=1, keepdims=True)
        top_ref[owner] = jnp.maximum(top_ref[owner], jnp.broadcast_to(best, (GROUP, LANES)))
        owners.append(owner)
        scores.append(score)
    for s in range(slots):
        owner = owners[s]
        shift = top_ref[owner].astype(BF16).astype(F32)
        weight = jnp.exp(scores[s] - shift)
        total = jnp.sum(weight, axis=1, keepdims=True)
        sum_ref[owner] = sum_ref[owner] + jnp.broadcast_to(total, (GROUP, LANES))
        acc_ref[owner] = acc_ref[owner] + jnp.dot(
            weight.astype(BF16), v_ref[s], preferred_element_type=F32
        )
    lane = lane_ids((GROUP, LANES))
    for d in range(out_ref.shape[0]):
        stats = jnp.zeros((GROUP, LANES), F32)
        for par in range(2):
            total = sum_ref[2 * d + par]
            high = total.astype(BF16).astype(F32)
            base = par * 64
            stats = jnp.where(lane == base, top_ref[2 * d + par], stats)
            stats = jnp.where(lane == base + 1, high, stats)
            stats = jnp.where(lane == base + 2, total - high, stats)
        block = jnp.concatenate([acc_ref[2 * d], acc_ref[2 * d + 1], stats], axis=0)
        out_ref[d] = block.astype(BF16)


def combine_body(part_ref, q_ref, fresh_ref, out_ref):
    count = part_ref.shape[0]
    best = jnp.full((GROUP, LANES), NEG, F32)
    for d in range(count):
        best = jnp.maximum(best, part_ref[d].astype(F32)[2 * GROUP :])
    fk, fv = fresh_ref[0], fresh_ref[1]
    q = q_ref[...].astype(F32)
    tops, totals, accs = [], [], []
    for par in range(2):
        mine = slice(par * GROUP, (par + 1) * GROUP)
        own = jnp.sum(q[mine] * fk[par : par + 1], axis=1, keepdims=True) * HD ** (-0.5)
        top = jnp.maximum(best[:, par * 64 : par * 64 + 1], own)
        own_weight = jnp.exp(own - top)
        tops.append(top)
        totals.append(own_weight)
        accs.append(own_weight.astype(BF16).astype(F32) * fv[par : par + 1])
    for d in range(count):
        block = part_ref[d].astype(F32)
        stats = block[2 * GROUP :]
        for par in range(2):
            base = par * 64
            factor = jnp.exp(stats[:, base : base + 1] - tops[par])
            total = stats[:, base + 1 : base + 2] + stats[:, base + 2 : base + 3]
            totals[par] = totals[par] + factor * total
            accs[par] = accs[par] + factor * block[par * GROUP : (par + 1) * GROUP]
    rows = jnp.concatenate([accs[par] / totals[par] for par in range(2)], axis=0).astype(BF16)
    for d in range(out_ref.shape[0]):
        out_ref[d] = rows


def project_body(att_ref, w_ref, met_ref, out_ref, rows_ref):
    core = lax.axis_index("core")
    count, per, _ = att_ref.shape
    rows_ref[...] = att_ref[...].astype(F32).reshape(count * per, HD)
    reqs = count * per // GROUP
    heads = [rows_ref[pl.ds(h, reqs, stride=GROUP), :].astype(BF16) for h in range(GROUP)]
    heads = jnp.concatenate(heads, axis=1)
    for at, ref in ((core, w_ref), (1 - core, met_ref)):
        total = jnp.dot(heads, ref[...], preferred_element_type=F32).astype(BF16)
        for g in range(out_ref.shape[0]):
            out_ref[g, at] = total


def gather_body(part_ref, out_ref):
    total = part_ref[0].astype(F32)
    for g in range(1, part_ref.shape[0]):
        total = total + part_ref[g].astype(F32)
    out_ref[...] = total.astype(BF16)


def widen_body(
    pay_ref, mine_ref, gate_ref, up_ref, met1_ref, met2_ref, met3_ref, out_ref, hidden_ref
):
    me = lax.axis_index(TEAM)
    team = 2 * pay_ref.shape[0]
    reqs = 2 * pay_ref.shape[3]
    mets = (met1_ref, met2_ref, met3_ref)
    blocks = (met2_ref.shape[0] - 2) // 2
    bases = (met1_ref.shape[0] - met2_ref.shape[0], 0, 0)
    square = jnp.zeros((reqs, 1), F32)
    gained = []
    for flip in range(team):
        ref, at = (mine_ref, 0) if flip == 0 else (mets[flip - 1], bases[flip - 1] + 2 * blocks)
        owner = me ^ flip
        chip, core = owner // 2, owner % 2
        projected = jnp.concatenate([pay_ref[chip, c, core].astype(F32) for c in range(2)], axis=0)
        hidden = (ref[at, :reqs].astype(F32) + projected).astype(BF16)
        if flip == 0:
            hidden_ref[...] = hidden
        wide = hidden.astype(F32)
        square = square + jnp.sum(wide * wide, axis=1, keepdims=True)
        gained.append((wide * ref[at + 1, :reqs].astype(F32)).astype(BF16))
    gained = jnp.concatenate(gained, axis=1)
    tiles = []
    for b in range(2 * blocks):
        ref, at = (gate_ref, b) if b < blocks else (up_ref, b - blocks)
        cols = pl.ds(pl.multiple_of((me * blocks + at) * LANES, LANES), LANES)
        w = jnp.concatenate([ref[:, cols]] + [met_ref[base + b] for met_ref, base in zip(mets, bases)], axis=0)
        x = jnp.dot(gained, w, preferred_element_type=F32)
        tiles.append(x.reshape(reqs // 8, 8, LANES))
    for i in range(blocks):
        out_ref[:, i * 16 : (i + 1) * 16, :] = jnp.concatenate(
            [tiles[2 * i], tiles[2 * i + 1]], axis=1
        ).astype(BF16)
    square = jnp.broadcast_to(square, (reqs, LANES))
    high = square.astype(BF16).astype(F32)
    lane = lane_ids(square.shape)
    square = jnp.where(lane == 0, high, jnp.where(lane == 1, square - high, 0.0))
    out_ref[:, blocks * 16 :, :] = square.reshape(reqs // 8, 8, LANES).astype(BF16)


def activate_body(width, part_ref, out_ref):
    total = part_ref[0].astype(F32)
    for d in range(1, part_ref.shape[0]):
        total = total + part_ref[d].astype(F32)
    units = (total.shape[0] - 8) // 2
    square = total[2 * units :]
    square = square[:, 0:1] + square[:, 1:2]
    inv_rms = lax.rsqrt(jnp.broadcast_to(square, (8, LANES)) / width + EPS)[None]
    gate = total[:units].reshape(units // 8, 8, LANES) * inv_rms
    up = total[units : 2 * units].reshape(units // 8, 8, LANES) * inv_rms
    active = (gate / (1.0 + jnp.exp(-gate)) * up).reshape(units, LANES).astype(BF16)
    for d in range(out_ref.shape[0]):
        out_ref[d] = active


def down_body(
    ring, act_ref, w_ref, met_ref, hidden_ref, order_hbm, out_ref, kept_ref, order_ref, sem
):
    fetch = pltpu.make_async_copy(order_hbm, order_ref, sem)
    fetch.start()
    core = lax.axis_index("core")
    reqs = act_ref.shape[0] * act_ref.shape[2] * 8
    blocks = act_ref.shape[3] // 8
    height = blocks * LANES
    acts, own = [], []
    for z in range(2):
        act = act_ref[:, z].astype(F32).reshape(reqs // 8, blocks * 8, LANES)
        for b in range(blocks):
            acts.append(act[:, b * 8 : b * 8 + 8].reshape(reqs, LANES).astype(BF16))
        own.append(w_ref[pl.ds(pl.multiple_of((2 * z + core) * height, LANES), height), :])
    acts = jnp.concatenate(acts, axis=1)
    met = met_ref[: 2 * blocks].reshape(2 * height, LANES)
    totals = [
        jnp.dot(acts, w, preferred_element_type=F32).astype(BF16)
        for w in (jnp.concatenate(own, axis=0), met)
    ]
    fetch.wait()
    place = lax.broadcasted_iota(jnp.int32, (reqs, reqs), 0)
    pick = (request_of(place, ring) == order_ref[...]).astype(F32).astype(BF16)
    dims = (((0,), (0,)), ((), ()))
    for at, total in ((core, totals[0]), (1 - core, totals[1])):
        total = lax.dot_general(pick, total, dims, preferred_element_type=F32)
        out_ref[at] = total.astype(BF16)
    kept = lax.dot_general(pick, hidden_ref[...], dims, preferred_element_type=F32)
    kept_ref[...] = kept.astype(BF16)


def finish_body(part_ref, kept_ref, out_ref):
    total = kept_ref[lax.axis_index(GRP)].astype(F32)
    for d in range(part_ref.shape[0]):
        total = total + part_ref[d].astype(F32)
    out_ref[...] = total.astype(BF16)


def shards(
    queries,
    fresh_keys,
    fresh_values,
    key_cache,
    value_cache,
    lengths,
    block_table,
    resid,
    out_weight,
    norm_gain,
    gate_weight,
    up_weight,
    down_weight,
    row_order,
):
    ctx, ring, rest, grp = (lax.axis_size(axes) for axes in (CTX, RING, REST, GRP))
    team = lax.axis_size(TEAM)
    reqs, width = resid.shape
    slots = key_cache.shape[0]
    share = reqs // grp
    shape = jax.ShapeDtypeStruct
    blocks = gate_weight.shape[1] // (team * LANES)

    def passed(blocks_out):
        return [
            lax.ppermute(block, TEAM, [(i, i ^ flip) for i in range(team)])
            for flip, block in enumerate(blocks_out, 1)
        ]

    bundle = pltpu.HBM((2 * blocks + 2, LANES, LANES), BF16)
    core_bundle = pltpu.HBM((4 * blocks + 2, LANES, LANES), BF16)
    mine, given_core, *given = call(
        functools.partial(cut_body, ring),
        (shape((2, LANES, LANES), BF16), core_bundle, bundle, bundle),
        [VMEM] * 5,
    )(gate_weight, up_weight, down_weight, resid, norm_gain.reshape(1, width))
    met = [
        lax.ppermute(block, TEAM, [(i, i ^ flip) for i in range(team)])
        for flip, block in enumerate(given, 2)
    ]
    met_core = lax.ppermute(given_core, "core", [(0, 1), (1, 0)])
    met_out = lax.ppermute(out_weight, "core", [(0, 1), (1, 0)])
    meta = call(
        prepare_body,
        shape((2 * slots,), jnp.int32),
        [HBM] * 2,
        [
            pltpu.SMEM(lengths.shape, jnp.int32),
            pltpu.VMEM(block_table.shape, jnp.int32),
            pltpu.SemaphoreType.DMA((2,)),
        ],
        out_specs=SMEM,
    )(lengths, block_table)

    packed, my_queries = call(
        pack_body,
        (shape((ring, 2 * GROUP, HD), BF16), shape((2 * GROUP, HD), BF16)),
        [HBM],
        [pltpu.VMEM(queries.shape, BF16), pltpu.SemaphoreType.DMA(())],
    )(queries)
    all_queries = exchange(packed, RING)
    all_queries = lax.all_gather(all_queries, "core", axis=0, tiled=False)
    scratch = [pltpu.VMEM((reqs, GROUP, LANES), F32)] * 3
    scratch += [pltpu.VMEM(key_cache.shape, BF16)] * 2 + [pltpu.VMEM(fresh_keys.shape, BF16)] * 2
    scratch += [pltpu.SemaphoreType.DMA((2, CHUNKS)), pltpu.SemaphoreType.DMA((2,))]
    parts, fresh = call(
        attend_body,
        (pltpu.HBM((ctx, 3 * GROUP, HD), BF16), shape((2,) + fresh_keys.shape, F32)),
        [SMEM, VMEM] + [HBM] * 4,
        scratch,
    )(meta, all_queries, key_cache, value_cache, fresh_keys, fresh_values)
    parts = exchange(parts, CTX)
    parts, mine = lax.optimization_barrier((parts, mine))
    local = call(combine_body, shape((ring, 2 * GROUP, HD), BF16), [VMEM] * 3)(
        parts, my_queries, fresh
    )
    attended = exchange(local, RING)
    attended, met_core, met[0] = lax.optimization_barrier((attended, met_core, met[0]))
    projected = call(
        project_body,
        shape((grp, 2, reqs // 2, width), BF16),
        [VMEM] * 3,
        [pltpu.VMEM((ring * 2 * GROUP, HD), F32)],
    )(attended, out_weight, met_out)
    projected = exchange(projected.reshape(grp, reqs, width), GRP)
    pay = call(gather_body, shape((reqs, width), BF16), [VMEM])(projected)
    pay = lax.all_gather(pay, TEAM, axis=0, tiled=False)
    units = blocks * 8
    wide, hidden = call(
        widen_body,
        (shape((rest, 2 * units + 8, LANES), BF16), shape((reqs, width), BF16)),
        [VMEM] * 7,
    )(pay.reshape(team // 2, 2, 2, reqs // 2, width), mine, gate_weight, up_weight, met_core, *met)
    wide = exchange(wide, REST)
    active = call(
        functools.partial(activate_body, width * ctx), shape((ring, units, LANES), BF16), [VMEM]
    )(wide)
    active = exchange(active, RING)
    line = lax.axis_size("zl")
    rows, kept = call(
        functools.partial(down_body, ring),
        (shape((2, reqs, width), BF16), shape((reqs, width), BF16)),
        [VMEM] * 4 + [HBM],
        [pltpu.VMEM((1, reqs), jnp.int32), pltpu.SemaphoreType.DMA(())],
    )(
        active.reshape(ring // (2 * line), 2, line, units, LANES),
        down_weight,
        met_core,
        hidden,
        row_order.reshape(1, reqs),
    )
    rows = exchange(rows.reshape(2 * grp, share, width), LAST)
    return call(finish_body, shape((share, width), BF16), [VMEM] * 2)(
        rows, kept.reshape(grp, share, width)
    )


def solution(mesh, sizes=(4, 2, 4, 2, 2, 4)):
    inner = Mesh(mesh.devices.reshape(sizes), ("yh", "yl", "zl", "core", "zh", "x"))
    in_specs = (
        P(CTX, GRP),
        P(CTX, GRP),
        P(CTX, GRP),
        P(CTX, None, GRP),
        P(CTX, None, GRP),
        P(),
        P(),
        P(None, CTX),
        P(GRP, CTX),
        P(CTX),
        P(CTX, GRP),
        P(CTX, GRP),
        P(GRP, CTX),
        P(),
    )
    out_specs = P(GRP, CTX)
    return jax.shard_map(shards, mesh=inner, in_specs=in_specs, out_specs=out_specs, check_vma=False)
```

```python
import functools

import jax
import jax.numpy as jnp
from jax import lax
from jax.experimental import pallas as pl
from jax.experimental.pallas import tpu as pltpu
from jax.sharding import Mesh
from jax.sharding import PartitionSpec as P

HD = 128
GROUP = 8
LANES = 128
EPS = 1e-05
CHUNKS = 6
NEG = -1e30
VMEM_LIMIT = 16 * 2**20
CTX = ("yh", "yl", "zl", "core")
RING = ("yh", "yl", "zl")
REST = ("yh", "zl")
TEAM = ("yl", "core")
GRP = ("zh", "x")
LAST = ("core",) + GRP
F32 = jnp.float32
BF16 = jnp.bfloat16
VMEM = pl.BlockSpec(memory_space=pltpu.VMEM)
SMEM = pl.BlockSpec(memory_space=pltpu.SMEM)
HBM = pl.BlockSpec(memory_space=pltpu.HBM)


def exchange(x, axes):
    return lax.all_to_all(x, axes, 0, 0, tiled=True)


def lane_ids(shape):
    return lax.broadcasted_iota(jnp.int32, shape, len(shape) - 1)


def call(body, out_shape, in_specs, scratch=(), out_specs=None):
    kernel = pl.pallas_call(
        body,
        out_shape=out_shape,
        in_specs=in_specs,
        out_specs=jax.tree.map(lambda _: VMEM, out_shape) if out_specs is None else out_specs,
        scratch_shapes=list(scratch),
        compiler_params=pltpu.CompilerParams(vmem_limit_bytes=VMEM_LIMIT),
    )

    def run(*operands):
        placed = [
            pltpu.with_memory_space_constraint(x, pltpu.HBM) if spec is HBM else x
            for x, spec in zip(operands, in_specs, strict=True)
        ]
        return kernel(*placed)

    return run


def request_of(place, ring):
    core, at = place >> ring.bit_length(), place & (2 * ring - 1)
    return (at >> 1) * 4 + core * 2 + (at & 1)


def pack_body(q_hbm, out_ref, mine_ref, q_ref, sem):
    fetch = pltpu.make_async_copy(q_hbm, q_ref, sem)
    fetch.start()
    fetch.wait()
    wide = q_ref[...].astype(F32)
    rows = [
        wide[r : r + 1, h * HD : (h + 1) * HD] for r in range(wide.shape[0]) for h in range(GROUP)
    ]
    rows = jnp.concatenate(rows, axis=0).astype(BF16)
    mine_ref[...] = rows
    for d in range(out_ref.shape[0]):
        out_ref[d] = rows


def prepare_body(len_hbm, table_hbm, meta_ref, len_ref, table_ref, sems):
    pairs = ((table_hbm, table_ref), (len_hbm, len_ref))
    copies = [pltpu.make_async_copy(a, b, sems.at[i]) for i, (a, b) in enumerate(pairs)]
    for copy in copies:
        copy.start()
    for copy in copies:
        copy.wait()
    slots = meta_ref.shape[0] // 2
    first = lax.axis_index(CTX) * slots
    table = table_ref[...] - first
    rows, cols = table.shape
    code = lax.broadcasted_iota(jnp.int32, (rows, cols), 0) * cols + lane_ids((rows, cols))
    for s in range(slots):
        found = jnp.min(jnp.where(table == s, code, rows * cols - 1))
        owner = found // cols
        meta_ref[s] = owner
        meta_ref[slots + s] = len_ref[owner] - (found % cols) * LANES


def cut_body(
    ring, gate_ref, up_ref, down_ref, resid_ref, gain_ref, mine, core_ref, met2_ref, met3_ref
):
    me = lax.axis_index(TEAM)
    reqs = resid_ref.shape[0]
    place = lax.broadcasted_iota(jnp.int32, (reqs, reqs), 0)
    turn = (request_of(place, ring) == lane_ids((reqs, reqs))).astype(F32).astype(BF16)
    resid = jnp.dot(turn, resid_ref[...], preferred_element_type=F32).astype(BF16)
    gain = jnp.broadcast_to(gain_ref[...].astype(F32), (LANES, LANES)).astype(BF16)
    mine[0, :reqs] = resid
    mine[1] = gain
    blocks = (met2_ref.shape[0] - 2) // 2
    other = 1 - lax.axis_index("core")
    for z in range(2):
        start = pl.multiple_of((2 * z + other) * blocks * LANES, LANES)
        rows = down_ref[pl.ds(start, blocks * LANES), :]
        core_ref[z * blocks : (z + 1) * blocks] = rows.reshape(blocks, LANES, LANES)
    for flip, out_ref, base in ((1, core_ref, 2 * blocks), (2, met2_ref, 0), (3, met3_ref, 0)):
        start = (me ^ flip) * blocks * LANES
        for b in range(blocks):
            cols = pl.ds(pl.multiple_of(start + b * LANES, LANES), LANES)
            out_ref[base + b] = gate_ref[:, cols]
            out_ref[base + blocks + b] = up_ref[:, cols]
        out_ref[base + 2 * blocks, :reqs] = resid
        out_ref[base + 2 * blocks + 1] = gain


def attend_body(
    meta_ref,
    q_ref,
    k_hbm,
    v_hbm,
    fk_hbm,
    fv_hbm,
    out_ref,
    fresh_ref,
    top_ref,
    sum_ref,
    acc_ref,
    k_ref,
    v_ref,
    fk_ref,
    fv_ref,
    sems,
    fresh_sems,
):
    slots, page = k_ref.shape[0], k_ref.shape[1]
    part = slots // CHUNKS
    fetches = []
    for w, (a, b) in enumerate(((k_hbm, k_ref), (v_hbm, v_ref))):
        for i in range(CHUNKS):
            span = pl.ds(i * part, part)
            fetches.append(pltpu.make_async_copy(a.at[span], b.at[span], sems.at[w, i]))
    fetches.append(pltpu.make_async_copy(fk_hbm, fk_ref, fresh_sems.at[0]))
    fetches.append(pltpu.make_async_copy(fv_hbm, fv_ref, fresh_sems.at[1]))
    for fetch in fetches:
        fetch.start()
    top_ref[...] = jnp.full(top_ref.shape, NEG, F32)
    sum_ref[...] = jnp.zeros(sum_ref.shape, F32)
    acc_ref[...] = jnp.zeros(acc_ref.shape, F32)
    for fetch in fetches[:CHUNKS]:
        fetch.wait()
    lane = lane_ids((GROUP, page))
    owners, scores = [], []
    for s in range(slots):
        owner, live = meta_ref[s], meta_ref[slots + s]
        home = owner // 2
        pair = q_ref[home % 2, home // 2].astype(F32)
        q = jnp.where(owner % 2 == 1, pair[GROUP:], pair[:GROUP]).astype(BF16)
        score = lax.dot_general(q, k_ref[s], (((1,), (1,)), ((), ())), preferred_element_type=F32)
        score = jnp.where(lane < live, score * HD ** (-0.5), NEG)
        best = jnp.max(score, axis=1, keepdims=True)
        top_ref[owner] = jnp.maximum(top_ref[owner], jnp.broadcast_to(best, (GROUP, LANES)))
        owners.append(owner)
        scores.append(score)
    for fetch in fetches[CHUNKS:]:
        fetch.wait()
    fresh_ref[0] = fk_ref[...].astype(F32)
    fresh_ref[1] = fv_ref[...].astype(F32)
    for s in range(slots):
        owner = owners[s]
        shift = top_ref[owner].astype(BF16).astype(F32)
        weight = jnp.exp(scores[s] - shift)
        total = jnp.sum(weight, axis=1, keepdims=True)
        sum_ref[owner] = sum_ref[owner] + jnp.broadcast_to(total, (GROUP, LANES))
        acc_ref[owner] = acc_ref[owner] + jnp.dot(
            weight.astype(BF16), v_ref[s], preferred_element_type=F32
        )
    lane = lane_ids((GROUP, LANES))
    for d in range(out_ref.shape[0]):
        stats = jnp.zeros((GROUP, LANES), F32)
        for par in range(2):
            total = sum_ref[2 * d + par]
            high = total.astype(BF16).astype(F32)
            base = par * 64
            stats = jnp.where(lane == base, top_ref[2 * d + par], stats)
            stats = jnp.where(lane == base + 1, high, stats)
            stats = jnp.where(lane == base + 2, total - high, stats)
        block = jnp.concatenate([acc_ref[2 * d], acc_ref[2 * d + 1], stats], axis=0)
        out_ref[d] = block.astype(BF16)


def combine_body(part_ref, q_ref, fresh_ref, out_ref):
    count = part_ref.shape[0]
    best = jnp.full((GROUP, LANES), NEG, F32)
    for d in range(count):
        best = jnp.maximum(best, part_ref[d].astype(F32)[2 * GROUP :])
    fk, fv = fresh_ref[0], fresh_ref[1]
    q = q_ref[...].astype(F32)
    tops, totals, accs = [], [], []
    for par in range(2):
        mine = slice(par * GROUP, (par + 1) * GROUP)
        own = jnp.sum(q[mine] * fk[par : par + 1], axis=1, keepdims=True) * HD ** (-0.5)
        top = jnp.maximum(best[:, par * 64 : par * 64 + 1], own)
        own_weight = jnp.exp(own - top)
        tops.append(top)
        totals.append(own_weight)
        accs.append(own_weight.astype(BF16).astype(F32) * fv[par : par + 1])
    for d in range(count):
        block = part_ref[d].astype(F32)
        stats = block[2 * GROUP :]
        for par in range(2):
            base = par * 64
            factor = jnp.exp(stats[:, base : base + 1] - tops[par])
            total = stats[:, base + 1 : base + 2] + stats[:, base + 2 : base + 3]
            totals[par] = totals[par] + factor * total
            accs[par] = accs[par] + factor * block[par * GROUP : (par + 1) * GROUP]
    rows = jnp.concatenate([accs[par] / totals[par] for par in range(2)], axis=0).astype(BF16)
    for d in range(out_ref.shape[0]):
        out_ref[d] = rows


def project_body(att_ref, w_ref, met_ref, out_ref, rows_ref):
    core = lax.axis_index("core")
    count, per, _ = att_ref.shape
    rows_ref[...] = att_ref[...].astype(F32).reshape(count * per, HD)
    reqs = count * per // GROUP
    heads = [rows_ref[pl.ds(h, reqs, stride=GROUP), :].astype(BF16) for h in range(GROUP)]
    heads = jnp.concatenate(heads, axis=1)
    for at, ref in ((core, w_ref), (1 - core, met_ref)):
        total = jnp.dot(heads, ref[...], preferred_element_type=F32).astype(BF16)
        for g in range(out_ref.shape[0]):
            out_ref[g, at] = total


def gather_body(part_ref, out_ref):
    total = part_ref[0].astype(F32)
    for g in range(1, part_ref.shape[0]):
        total = total + part_ref[g].astype(F32)
    out_ref[...] = total.astype(BF16)


def widen_body(
    pay_ref, mine_ref, gate_ref, up_ref, met1_ref, met2_ref, met3_ref, out_ref, hidden_ref
):
    me = lax.axis_index(TEAM)
    team = 2 * pay_ref.shape[0]
    reqs = 2 * pay_ref.shape[3]
    mets = (met1_ref, met2_ref, met3_ref)
    blocks = (met2_ref.shape[0] - 2) // 2
    bases = (met1_ref.shape[0] - met2_ref.shape[0], 0, 0)
    square = jnp.zeros((reqs, 1), F32)
    gained = []
    for flip in range(team):
        ref, at = (mine_ref, 0) if flip == 0 else (mets[flip - 1], bases[flip - 1] + 2 * blocks)
        owner = me ^ flip
        chip, core = owner // 2, owner % 2
        projected = jnp.concatenate([pay_ref[chip, c, core].astype(F32) for c in range(2)], axis=0)
        hidden = (ref[at, :reqs].astype(F32) + projected).astype(BF16)
        if flip == 0:
            hidden_ref[...] = hidden
        wide = hidden.astype(F32)
        square = square + jnp.sum(wide * wide, axis=1, keepdims=True)
        gained.append((wide * ref[at + 1, :reqs].astype(F32)).astype(BF16))
    gained = jnp.concatenate(gained, axis=1)
    tiles = []
    for b in range(2 * blocks):
        ref, at = (gate_ref, b) if b < blocks else (up_ref, b - blocks)
        cols = pl.ds(pl.multiple_of((me * blocks + at) * LANES, LANES), LANES)
        w = jnp.concatenate([ref[:, cols]] + [met_ref[base + b] for met_ref, base in zip(mets, bases)], axis=0)
        x = jnp.dot(gained, w, preferred_element_type=F32)
        tiles.append(x.reshape(reqs // 8, 8, LANES))
    for i in range(blocks):
        out_ref[:, i * 16 : (i + 1) * 16, :] = jnp.concatenate(
            [tiles[2 * i], tiles[2 * i + 1]], axis=1
        ).astype(BF16)
    square = jnp.broadcast_to(square, (reqs, LANES))
    high = square.astype(BF16).astype(F32)
    lane = lane_ids(square.shape)
    square = jnp.where(lane == 0, high, jnp.where(lane == 1, square - high, 0.0))
    out_ref[:, blocks * 16 :, :] = square.reshape(reqs // 8, 8, LANES).astype(BF16)


def activate_body(width, part_ref, out_ref):
    total = part_ref[0].astype(F32)
    for d in range(1, part_ref.shape[0]):
        total = total + part_ref[d].astype(F32)
    units = (total.shape[0] - 8) // 2
    square = total[2 * units :]
    square = square[:, 0:1] + square[:, 1:2]
    inv_rms = lax.rsqrt(jnp.broadcast_to(square, (8, LANES)) / width + EPS)[None]
    gate = total[:units].reshape(units // 8, 8, LANES) * inv_rms
    up = total[units : 2 * units].reshape(units // 8, 8, LANES) * inv_rms
    active = (gate / (1.0 + jnp.exp(-gate)) * up).reshape(units, LANES).astype(BF16)
    for d in range(out_ref.shape[0]):
        out_ref[d] = active


def down_body(
    ring, act_ref, w_ref, met_ref, hidden_ref, order_hbm, out_ref, kept_ref, order_ref, sem
):
    fetch = pltpu.make_async_copy(order_hbm, order_ref, sem)
    fetch.start()
    core = lax.axis_index("core")
    reqs = act_ref.shape[0] * act_ref.shape[2] * 8
    blocks = act_ref.shape[3] // 8
    height = blocks * LANES
    acts, own = [], []
    for z in range(2):
        act = act_ref[:, z].astype(F32).reshape(reqs // 8, blocks * 8, LANES)
        for b in range(blocks):
            acts.append(act[:, b * 8 : b * 8 + 8].reshape(reqs, LANES).astype(BF16))
        own.append(w_ref[pl.ds(pl.multiple_of((2 * z + core) * height, LANES), height), :])
    acts = jnp.concatenate(acts, axis=1)
    met = met_ref[: 2 * blocks].reshape(2 * height, LANES)
    totals = [
        jnp.dot(acts, w, preferred_element_type=F32).astype(BF16)
        for w in (jnp.concatenate(own, axis=0), met)
    ]
    fetch.wait()
    place = lax.broadcasted_iota(jnp.int32, (reqs, reqs), 0)
    pick = (request_of(place, ring) == order_ref[...]).astype(F32).astype(BF16)
    dims = (((0,), (0,)), ((), ()))
    for at, total in ((core, totals[0]), (1 - core, totals[1])):
        total = lax.dot_general(pick, total, dims, preferred_element_type=F32)
        out_ref[at] = total.astype(BF16)
    kept = lax.dot_general(pick, hidden_ref[...], dims, preferred_element_type=F32)
    kept_ref[...] = kept.astype(BF16)


def finish_body(part_ref, kept_ref, out_ref):
    total = kept_ref[lax.axis_index(GRP)].astype(F32)
    for d in range(part_ref.shape[0]):
        total = total + part_ref[d].astype(F32)
    out_ref[...] = total.astype(BF16)


def shards(
    queries,
    fresh_keys,
    fresh_values,
    key_cache,
    value_cache,
    lengths,
    block_table,
    resid,
    out_weight,
    norm_gain,
    gate_weight,
    up_weight,
    down_weight,
    row_order,
):
    ctx, ring, rest, grp = (lax.axis_size(axes) for axes in (CTX, RING, REST, GRP))
    team = lax.axis_size(TEAM)
    reqs, width = resid.shape
    slots = key_cache.shape[0]
    share = reqs // grp
    shape = jax.ShapeDtypeStruct
    blocks = gate_weight.shape[1] // (team * LANES)

    def passed(blocks_out):
        return [
            lax.ppermute(block, TEAM, [(i, i ^ flip) for i in range(team)])
            for flip, block in enumerate(blocks_out, 1)
        ]

    bundle = pltpu.HBM((2 * blocks + 2, LANES, LANES), BF16)
    core_bundle = pltpu.HBM((4 * blocks + 2, LANES, LANES), BF16)
    mine, given_core, *given = call(
        functools.partial(cut_body, ring),
        (shape((2, LANES, LANES), BF16), core_bundle, bundle, bundle),
        [VMEM] * 5,
    )(gate_weight, up_weight, down_weight, resid, norm_gain.reshape(1, width))
    met = [
        lax.ppermute(block, TEAM, [(i, i ^ flip) for i in range(team)])
        for flip, block in enumerate(given, 2)
    ]
    met_core = lax.ppermute(given_core, "core", [(0, 1), (1, 0)])
    met_out = lax.ppermute(out_weight, "core", [(0, 1), (1, 0)])
    meta = call(
        prepare_body,
        shape((2 * slots,), jnp.int32),
        [HBM] * 2,
        [
            pltpu.SMEM(lengths.shape, jnp.int32),
            pltpu.VMEM(block_table.shape, jnp.int32),
            pltpu.SemaphoreType.DMA((2,)),
        ],
        out_specs=SMEM,
    )(lengths, block_table)

    packed, my_queries = call(
        pack_body,
        (shape((ring, 2 * GROUP, HD), BF16), shape((2 * GROUP, HD), BF16)),
        [HBM],
        [pltpu.VMEM(queries.shape, BF16), pltpu.SemaphoreType.DMA(())],
    )(queries)
    all_queries = exchange(packed, RING)
    all_queries = lax.all_gather(all_queries, "core", axis=0, tiled=False)
    scratch = [pltpu.VMEM((reqs, GROUP, LANES), F32)] * 3
    scratch += [pltpu.VMEM(key_cache.shape, BF16)] * 2 + [pltpu.VMEM(fresh_keys.shape, BF16)] * 2
    scratch += [pltpu.SemaphoreType.DMA((2, CHUNKS)), pltpu.SemaphoreType.DMA((2,))]
    parts, fresh = call(
        attend_body,
        (pltpu.HBM((ctx, 3 * GROUP, HD), BF16), shape((2,) + fresh_keys.shape, F32)),
        [SMEM, VMEM] + [HBM] * 4,
        scratch,
    )(meta, all_queries, key_cache, value_cache, fresh_keys, fresh_values)
    parts = exchange(parts, CTX)
    parts, mine = lax.optimization_barrier((parts, mine))
    local = call(combine_body, shape((ring, 2 * GROUP, HD), BF16), [VMEM] * 3)(
        parts, my_queries, fresh
    )
    attended = exchange(local, RING)
    attended, met_core, met[0] = lax.optimization_barrier((attended, met_core, met[0]))
    projected = call(
        project_body,
        shape((grp, 2, reqs // 2, width), BF16),
        [VMEM] * 3,
        [pltpu.VMEM((ring * 2 * GROUP, HD), F32)],
    )(attended, out_weight, met_out)
    projected = exchange(projected.reshape(grp, reqs, width), GRP)
    pay = call(gather_body, shape((reqs, width), BF16), [VMEM])(projected)
    pay = lax.all_gather(pay, TEAM, axis=0, tiled=False)
    units = blocks * 8
    wide, hidden = call(
        widen_body,
        (shape((rest, 2 * units + 8, LANES), BF16), shape((reqs, width), BF16)),
        [VMEM] * 7,
    )(pay.reshape(team // 2, 2, 2, reqs // 2, width), mine, gate_weight, up_weight, met_core, *met)
    wide = exchange(wide, REST)
    active = call(
        functools.partial(activate_body, width * ctx), shape((ring, units, LANES), BF16), [VMEM]
    )(wide)
    active = exchange(active, RING)
    line = lax.axis_size("zl")
    rows, kept = call(
        functools.partial(down_body, ring),
        (shape((2, reqs, width), BF16), shape((reqs, width), BF16)),
        [VMEM] * 4 + [HBM],
        [pltpu.VMEM((1, reqs), jnp.int32), pltpu.SemaphoreType.DMA(())],
    )(
        active.reshape(ring // (2 * line), 2, line, units, LANES),
        down_weight,
        met_core,
        hidden,
        row_order.reshape(1, reqs),
    )
    rows = exchange(rows.reshape(2 * grp, share, width), LAST)
    return call(finish_body, shape((share, width), BF16), [VMEM] * 2)(
        rows, kept.reshape(grp, share, width)
    )


def solution(mesh, sizes=(4, 2, 4, 2, 2, 4)):
    inner = Mesh(mesh.devices.reshape(sizes), ("yh", "yl", "zl", "core", "zh", "x"))
    in_specs = (
        P(CTX, GRP),
        P(CTX, GRP),
        P(CTX, GRP),
        P(CTX, None, GRP),
        P(CTX, None, GRP),
        P(),
        P(),
        P(None, CTX),
        P(GRP, CTX),
        P(CTX),
        P(CTX, GRP),
        P(CTX, GRP),
        P(GRP, CTX),
        P(),
    )
    out_specs = P(GRP, CTX)
    return jax.shard_map(shards, mesh=inner, in_specs=in_specs, out_specs=out_specs, check_vma=False)
```
